128 devices in a mesh: seq: 8 (over x_hi, z), res: 16 (over x_lo, y, core).
Axes of the slice: x: 4 (x_hi: 2, x_lo: 2; x = x_hi * 2 + x_lo), y: 4, z: 4, core: 2. Of those that a mesh axis runs over, the one named last changes fastest.
Arguments:
- alignment: bfloat16 [32, 768, 768], P('seq', 'res'), may hold values from -6 to 6
- cotangent: bfloat16 [32, 768, 768], P('seq', 'res'), may hold values from -6 to 6
- gain_row: float32 [768], replicated, may hold values from 0.25 to 1.75
- query_row: bfloat16 [768, 768], replicated, may hold values from -0.25 to 0.25
- key_row: bfloat16 [768, 768], replicated, may hold values from -1.2 to 1.2
- value_row: bfloat16 [768, 768], replicated, may hold values from -0.21875 to 0.21875
- out_row: bfloat16 [768, 768], replicated, may hold values from -0.21875 to 0.21875
- gain_col: float32 [768], replicated, may hold values from 0.25 to 1.75
- query_col: bfloat16 [768, 768], replicated, may hold values from -0.25 to 0.25
- key_col: bfloat16 [768, 768], replicated, may hold values from -3.6 to 3.6
- value_col: bfloat16 [768, 768], replicated, may hold values from -0.21875 to 0.21875
- out_col: bfloat16 [768, 768], replicated, may hold values from -0.21875 to 0.21875
Outputs:
- block_out: bfloat16 [32, 768, 768], P('seq', 'res')
- input_grad: bfloat16 [32, 768, 768], P('seq', 'res')
The draws below stay inside these ranges and needn't reach their ends.
All inputs are finite; a program needn't handle non-finite values.
Results may differ from the reference program's by a relative error of at most 0.02.
Values may be sent and summed in bfloat16 or wider, within the bound.
No kernel may reach another device: no remote copies, remote signals or barrier semaphores. Data moves between devices by JAX's collectives and lax.ppermute only.
A program may use at most 192 MiB of HBM per device.

```python
import math
import jax
import jax.numpy as jnp
from jax import lax

D = 768
HEADS = 12
HEAD_DIM = 64
SEQS = 32
RESIDUES = 768


def base_weight(key, salt):
    return jax.random.uniform(jax.random.fold_in(key, salt), (D, D), jnp.float32, -1.0, 1.0) * math.sqrt(3.0 / D)


def draw_query_row(key, part):
    shared = base_weight(key, 101)
    return shared.astype(jnp.bfloat16)


def draw_key_row(key, part):
    key = jax.random.fold_in(key, 2)
    fresh = jax.random.uniform(key, (D, D), jnp.float32, -1.0, 1.0) * math.sqrt(3.0 / D)
    return fresh.astype(jnp.bfloat16)


def draw_query_col(key, part):
    shared = base_weight(key, 202)
    return shared.astype(jnp.bfloat16)


def draw_key_col(key, part):
    key = jax.random.fold_in(key, 4)
    fresh = jax.random.uniform(key, (D, D), jnp.float32, -1.0, 1.0) * math.sqrt(3.0 / D)
    return fresh.astype(jnp.bfloat16)


def shard_levels(key, extent, pieces, low, top_value):
    factor_of, own = 1.0, jax.random.fold_in(key, 6)
    for axis_at, blocks in pieces:
        steps = jnp.exp(jax.random.uniform(jax.random.fold_in(own, axis_at), (blocks,), jnp.float32, low / len(pieces), top_value / len(pieces)))
        factor_of = factor_of * jnp.repeat(steps, extent[axis_at] // blocks).reshape([-1 if axis == axis_at else 1 for axis in range(len(extent))])
    return factor_of


def scatter_about(rng, extent, scale, reach, pieces=(), held_as=jnp.bfloat16):
    entries = jax.random.normal(rng, extent, jnp.float32) * scale
    if len(pieces) > 0:
        entries = shard_levels(rng, extent, pieces, -0.22, 0.18) * entries
    return jnp.clip(entries, min=-reach, max=reach).astype(held_as)


def setup_inputs(seed: int = 0) -> dict:
    arg_keys = jax.random.split(jax.random.key(seed), 13)
    alignment = scatter_about(arg_keys[0], (SEQS, RESIDUES, D), 1.0, 6.0, ((0, 8), (1, 16)))
    cotangent = scatter_about(arg_keys[1], (SEQS, RESIDUES, D), 1.0, 6.0, ((0, 8), (1, 16)))
    gain_row = jnp.clip(1.0 + 0.15 * jax.random.normal(arg_keys[2], (D,), jnp.float32), 0.25, 1.75)
    query_row = draw_query_row(jax.random.fold_in(arg_keys[12], 71), 0)
    key_row = draw_key_row(jax.random.fold_in(arg_keys[12], 71), 0)
    value_row = scatter_about(arg_keys[5], (D, D), D ** -0.5, 0.21875)
    out_row = scatter_about(arg_keys[6], (D, D), D ** -0.5, 0.21875)
    gain_col = jnp.clip(1.0 + 0.15 * jax.random.normal(arg_keys[7], (D,), jnp.float32), 0.25, 1.75)
    query_col = draw_query_col(jax.random.fold_in(arg_keys[12], 71), 0)
    key_col = draw_key_col(jax.random.fold_in(arg_keys[12], 71), 0)
    value_col = scatter_about(arg_keys[10], (D, D), D ** -0.5, 0.21875)
    out_col = scatter_about(arg_keys[11], (D, D), D ** -0.5, 0.21875)
    return dict(alignment=alignment, cotangent=cotangent, gain_row=gain_row, query_row=query_row, key_row=key_row, value_row=value_row, out_row=out_row, gain_col=gain_col, query_col=query_col, key_col=key_col, value_col=value_col, out_col=out_col)


def normalize(values, gain):
    mean = lax.optimization_barrier(jnp.mean(values, axis=-1, keepdims=True))
    centred = values - mean
    spread = lax.optimization_barrier(jnp.mean(centred * centred, axis=-1, keepdims=True))
    return centred * lax.rsqrt(spread + 1e-05) * gain

def project(flat, weight):
    return jnp.dot(flat, weight, preferred_element_type=jnp.float32)

def back_project(flat, weight):
    return jnp.dot(flat, weight.T, preferred_element_type=jnp.float32)

def reference(alignment, cotangent, gain_row, query_row, key_row, value_row, out_row, gain_col, query_col, key_col, value_col, out_col):
    f32 = jnp.float32
    bf16 = jnp.bfloat16
    tokens = SEQS * RESIDUES
    shape_heads = (SEQS, RESIDUES, HEADS, HEAD_DIM)
    row_scale = 1.0 / math.sqrt(HEAD_DIM * SEQS)
    col_scale = 1.0 / math.sqrt(HEAD_DIM)
    flat_input = alignment.astype(f32).reshape(tokens, D)
    normed = normalize(flat_input, gain_row).astype(bf16)
    row_q = project(normed, query_row).astype(bf16).reshape(shape_heads)
    row_k = project(normed, key_row).astype(bf16).reshape(shape_heads)
    row_v = project(normed, value_row).astype(bf16).reshape(shape_heads)
    row_logits = jnp.einsum('sihd,sjhd->hij', row_q.astype(f32), row_k.astype(f32)) * row_scale
    row_probs = jax.nn.softmax(row_logits, axis=-1)
    row_weights = row_probs.astype(bf16)
    row_att = jnp.einsum('hij,sjhd->sihd', row_weights.astype(f32), row_v.astype(f32)).astype(bf16)
    middle = (flat_input + project(row_att.reshape(tokens, D), out_row)).astype(bf16)
    middle_f = middle.astype(f32)
    normed_col = normalize(middle_f, gain_col).astype(bf16)
    col_q = project(normed_col, query_col).astype(bf16).reshape(shape_heads)
    col_k = project(normed_col, key_col).astype(bf16).reshape(shape_heads)
    col_v = project(normed_col, value_col).astype(bf16).reshape(shape_heads)
    col_logits = jnp.einsum('schd,tchd->chst', col_q.astype(f32), col_k.astype(f32)) * col_scale
    col_probs = jax.nn.softmax(col_logits, axis=-1)
    col_weights = col_probs.astype(bf16)
    col_att = jnp.einsum('chst,tchd->schd', col_weights.astype(f32), col_v.astype(f32)).astype(bf16)
    block_out = (middle_f + project(col_att.reshape(tokens, D), out_col)).astype(bf16)
    grad_out = cotangent.reshape(tokens, D)
    grad_col_att = back_project(grad_out, out_col).astype(bf16).reshape(shape_heads)
    col_grad_probs = jnp.einsum('schd,tchd->chst', grad_col_att.astype(f32), col_v.astype(f32))
    col_dlogits = (col_probs * (col_grad_probs - lax.optimization_barrier(jnp.sum(col_probs * col_grad_probs, axis=-1, keepdims=True))) * col_scale).astype(bf16)
    grad_col_q = jnp.einsum('chst,tchd->schd', col_dlogits.astype(f32), col_k.astype(f32)).astype(bf16)
    grad_col_k = jnp.einsum('chst,schd->tchd', col_dlogits.astype(f32), col_q.astype(f32)).astype(bf16)
    grad_col_v = jnp.einsum('chst,schd->tchd', col_weights.astype(f32), grad_col_att.astype(f32)).astype(bf16)
    grad_normed_col = back_project(grad_col_q.reshape(tokens, D), query_col) + back_project(grad_col_k.reshape(tokens, D), key_col) + back_project(grad_col_v.reshape(tokens, D), value_col)
    _, pull_col = jax.vjp(lambda values: normalize(values, gain_col), middle_f)
    grad_middle = (grad_out.astype(f32) + pull_col(grad_normed_col)[0]).astype(bf16)
    grad_row_att = back_project(grad_middle, out_row).astype(bf16).reshape(shape_heads)
    row_grad_probs = jnp.einsum('sihd,sjhd->hij', grad_row_att.astype(f32), row_v.astype(f32))
    row_dlogits = (row_probs * (row_grad_probs - lax.optimization_barrier(jnp.sum(row_probs * row_grad_probs, axis=-1, keepdims=True))) * row_scale).astype(bf16)
    grad_row_q = jnp.einsum('hij,sjhd->sihd', row_dlogits.astype(f32), row_k.astype(f32)).astype(bf16)
    grad_row_k = jnp.einsum('hij,sihd->sjhd', row_dlogits.astype(f32), row_q.astype(f32)).astype(bf16)
    grad_row_v = jnp.einsum('hij,sihd->sjhd', row_weights.astype(f32), grad_row_att.astype(f32)).astype(bf16)
    grad_normed = back_project(grad_row_q.reshape(tokens, D), query_row) + back_project(grad_row_k.reshape(tokens, D), key_row) + back_project(grad_row_v.reshape(tokens, D), value_row)
    _, pull_row = jax.vjp(lambda values: normalize(values, gain_row), flat_input)
    input_grad = (grad_middle.astype(f32) + pull_row(grad_normed)[0]).astype(bf16)
    return (block_out.reshape(SEQS, RESIDUES, D), input_grad.reshape(SEQS, RESIDUES, D))
```

```python
import math

import jax
import jax.numpy as jnp
from jax import lax
from jax.experimental import pallas as pl
from jax.experimental.pallas import tpu as pltpu
from jax.sharding import Mesh
from jax.sharding import PartitionSpec as P

F32 = jnp.float32
BF16 = jnp.bfloat16
D = 768
HEADS = 12
HEAD_DIM = 64
SEQ = ("xh", "z")
GRP = ("xl", "c")
WIDE = ("xh", "z", "xl", "c")
ALLRES = ("y", "xl", "c")
NS, NG, NY = 8, 4, 4
GH = HEADS // NG
S = 4
R = 48
I = R * NG
CR = 6
CP = 8
TOK = NS * S * CP
ROWS = GH * I // NS
WIDTH = GH * S * HEAD_DIM
ROW_SCALE = 1.0 / math.sqrt(HEAD_DIM * 32)
COL_SCALE = 1.0 / math.sqrt(HEAD_DIM)


def dot(a, b):
    return lax.dot_general(a, b, (((1,), (0,)), ((), ())), preferred_element_type=F32)


def dot_nt(a, b):
    return lax.dot_general(a, b, (((1,), (1,)), ((), ())), preferred_element_type=F32)


def dot_tn(a, b):
    return lax.dot_general(a, b, (((0,), (0,)), ((), ())), preferred_element_type=F32)


def call(kernel, outs, *args, mem=32, scratch=()):
    shapes = [jax.ShapeDtypeStruct(s, t) for s, t in outs]
    res = pl.pallas_call(
        kernel,
        out_shape=shapes,
        in_specs=[pl.BlockSpec(memory_space=pltpu.VMEM)] * len(args),
        out_specs=[pl.BlockSpec(memory_space=pltpu.VMEM)] * len(outs),
        scratch_shapes=list(scratch),
        compiler_params=pltpu.CompilerParams(vmem_limit_bytes=mem * 2**20),
    )(*args)
    return res[0] if len(outs) == 1 else res


def halves(a, b, half_a, half_b):
    low = lax.broadcasted_iota(jnp.int32, a.shape, 1) < 64
    a = a if half_a == 0 else pltpu.roll(a, 64, 1)
    b = b if half_b == 1 else pltpu.roll(b, 64, 1)
    return jnp.where(low, a, b)


def blk(v, n):
    return v[:, n * 128 : (n + 1) * 128]


def to_column():
    row = lax.broadcasted_iota(jnp.int32, (TOK, S * R), 0)
    col = lax.broadcasted_iota(jnp.int32, (TOK, S * R), 1)
    r = row % CP
    want = ((row // CP) % S) * R + (row // (CP * S)) * CR + r
    return jnp.where((r < CR) & (col == want), 1.0, 0.0).astype(BF16)


def to_wide():
    row = lax.broadcasted_iota(jnp.int32, (TOK, I), 0)
    col = lax.broadcasted_iota(jnp.int32, (TOK, I), 1)
    r = row % CP
    want = ((row // CP) % NG) * R + (row // (CP * NG)) * CR + r
    return jnp.where((r < CR) & (col == want), 1.0, 0.0).astype(BF16)


def moments(v):
    mean = jnp.mean(v, axis=-1, keepdims=True)
    centred = v - mean
    r = lax.rsqrt(jnp.mean(centred * centred, axis=-1, keepdims=True) + 1e-05)
    return centred * r, r


def norm_grad(grad, gain, hat, r):
    g = grad * gain
    return r * (
        g - jnp.mean(g, axis=-1, keepdims=True) - hat * jnp.mean(g * hat, axis=-1, keepdims=True)
    )


def k_send(x, cot, out):
    perm = to_column()
    a = dot(perm, x[...].astype(F32).reshape(S * R, D).astype(BF16)).astype(BF16)
    b = dot(perm, cot[...].astype(F32).reshape(S * R, D).astype(BF16)).astype(BF16)
    out[:, 0:D] = a
    out[:, D : 2 * D] = b


def k_project(x, gain, wq, wk, wv, keys, qv):
    hat, _ = moments(x[...].astype(F32).reshape(S * R, D))
    normed = (hat * gain[...]).astype(BF16)
    for which, w in enumerate((wk, wq, wv)):
        y = dot(normed, w[...])
        for g in range(NG):
            for h in range(GH):
                n = g * GH + h
                src = blk(y, n // 2)
                for sp in range(2):
                    a = src[2 * sp * R : (2 * sp + 1) * R]
                    b = src[(2 * sp + 1) * R : (2 * sp + 2) * R]
                    piece = halves(a, b, n % 2, n % 2).astype(BF16)
                    at = h * 256 + sp * 128
                    if which == 0:
                        for yy in range(NY):
                            keys[yy * NG + g, :, at : at + 128] = piece
                    else:
                        at = at + (which - 1) * WIDTH
                        qv[g, :, at : at + 128] = piece


def k_logits(qv, keys, out):
    tops = []
    for h in range(GH):
        c = slice(h * 256, (h + 1) * 256)
        tops.append(dot_nt(qv[:, c], keys[:, c]))
    full = jnp.concatenate(tops, axis=0)
    for a in range(NS):
        out[a] = full[a * ROWS : (a + 1) * ROWS].astype(BF16)


def summed(parts):
    total = parts[0].astype(F32)
    for a in range(1, parts.shape[0]):
        total = total + parts[a].astype(F32)
    return total


def k_softmax(parts, probs, weights):
    logits = summed(parts) * ROW_SCALE
    e = jnp.exp(logits - jnp.max(logits, axis=-1, keepdims=True))
    p = e / jnp.sum(e, axis=-1, keepdims=True)
    probs[...] = p
    w = p.astype(BF16)
    for a in range(NS):
        weights[a] = w


def k_attend(weights, values, out):
    perm = to_wide()
    for h in range(GH):
        c = slice(h * 256, (h + 1) * 256)
        att = dot(weights[h * I : (h + 1) * I], values[:, c]).astype(BF16)
        out[:, c] = dot(perm, att).astype(BF16)


def k_column(
    att_in, xc, gain, out_row, wq, wk, wv, out_col, back, grad_out, att_s, gq_s, gk_s, gv_s
):
    raw = att_in[...].astype(F32).reshape(NS, NG, CP, WIDTH)
    groups = [raw[:, g].reshape(NS * CP, WIDTH) for g in range(NG)]
    per_seq = []
    for s in range(S):
        cols = []
        for fb in range(6):
            pair = []
            for n in (2 * fb, 2 * fb + 1):
                pair.append(blk(groups[n // GH], (n % GH) * 2 + s // 2))
            cols.append(halves(pair[0], pair[1], s % 2, s % 2))
        per_seq.append(jnp.concatenate(cols, axis=1).reshape(NS, 1, CP, D))
    att_row = jnp.concatenate(per_seq, axis=1).reshape(TOK, D).astype(BF16)
    middle = (xc[:, 0:D].astype(F32) + dot(att_row, out_row[...])).astype(BF16)
    mid = middle.astype(F32)
    cot = xc[:, D : 2 * D]
    hat, r = moments(mid)
    normed = (hat * gain[...]).astype(BF16)
    q = dot(normed, wq[...]).astype(BF16)
    k = dot(normed, wk[...]).astype(BF16)
    v = dot(normed, wv[...]).astype(BF16)
    ga = dot_nt(cot, out_col[...]).astype(BF16)
    row = lax.broadcasted_iota(jnp.int32, (TOK, TOK), 0)
    col = lax.broadcasted_iota(jnp.int32, (TOK, TOK), 1)
    same = (row % CP) == (col % CP)
    lane = lax.broadcasted_iota(jnp.int32, (1, 128), 1)
    for fb in range(6):
        qb, kb, vb, gb = (blk(t, fb) for t in (q, k, v, ga))
        att = gq = gk = gv = None
        for half in range(2):
            mask = jnp.where((lane < 64) == (half == 0), 1.0, 0.0).astype(BF16)
            km, vm, qm, gm = kb * mask, vb * mask, qb * mask, gb * mask
            logits = jnp.where(same, dot_nt(qb, km) * COL_SCALE, -1e30)
            e = jnp.exp(logits - jnp.max(logits, axis=-1, keepdims=True))
            p = e / jnp.sum(e, axis=-1, keepdims=True)
            w = p.astype(BF16)
            grads = dot_nt(gb, vm)
            dl = p * (grads - jnp.sum(p * grads, axis=-1, keepdims=True)) * COL_SCALE
            dl = dl.astype(BF16)
            parts = (dot(w, vm), dot(dl, km), dot_tn(dl, qm), dot_tn(w, gm))
            if half == 0:
                att, gq, gk, gv = parts
            else:
                att, gq, gk, gv = (t + u for t, u in zip((att, gq, gk, gv), parts))
        at = slice(fb * 128, (fb + 1) * 128)
        att_s[:, at] = att.astype(BF16)
        gq_s[:, at] = gq.astype(BF16)
        gk_s[:, at] = gk.astype(BF16)
        gv_s[:, at] = gv.astype(BF16)
    back[:, 0:D] = (mid + dot(att_s[...], out_col[...])).astype(BF16)
    gn = (
        dot_nt(gq_s[...], wq[...]) + dot_nt(gk_s[...], wk[...]) + dot_nt(gv_s[...], wv[...])
    )
    gmid = (cot.astype(F32) + norm_grad(gn, gain[...], hat, r)).astype(BF16)
    back[:, D : 2 * D] = gmid
    gra = dot_nt(gmid, out_row[...]).reshape(NS, S, CP, D)
    seqs = [gra[:, s].reshape(NS * CP, D) for s in range(S)]
    per_group = []
    for g in range(NG):
        cols = []
        for h in range(GH):
            n = g * GH + h
            for sp in range(2):
                cols.append(
                    halves(blk(seqs[2 * sp], n // 2), blk(seqs[2 * sp + 1], n // 2), n % 2, n % 2)
                )
        per_group.append(jnp.concatenate(cols, axis=1).reshape(NS, 1, CP, WIDTH))
    grad_out[...] = jnp.concatenate(per_group, axis=1).reshape(TOK, WIDTH).astype(BF16)


def k_grad_probs(grads, values, gra, out):
    perm = to_wide()
    tops = []
    for h in range(GH):
        c = slice(h * 256, (h + 1) * 256)
        g = dot_tn(perm, grads[:, c]).astype(BF16)
        gra[:, c] = g
        tops.append(dot_nt(g, values[:, c]))
    full = jnp.concatenate(tops, axis=0)
    for a in range(NS):
        out[a] = full[a * ROWS : (a + 1) * ROWS].astype(BF16)


def k_grad_values(weights, gra, out):
    for h in range(GH):
        c = slice(h * 256, (h + 1) * 256)
        out[:, c] = dot_tn(weights[h * I : (h + 1) * I], gra[:, c]).astype(BF16)


def k_softmax_grad(parts, probs, out):
    grads = summed(parts)
    p = probs[...]
    dl = p * (grads - jnp.sum(p * grads, axis=-1, keepdims=True)) * ROW_SCALE
    dl = dl.astype(BF16)
    for a in range(NS):
        out[a] = dl


def k_grad_qk(dl, keys, qv, gq, gk):
    for h in range(GH):
        c = slice(h * 256, (h + 1) * 256)
        d = dl[h * I : (h + 1) * I]
        gk[:, c] = dot_tn(d, qv[:, c]).astype(BF16)
        gq[:, c] = dot(d, keys[:, c]).astype(BF16)


def k_finish(gq, gk, gv, x, back, gain, wq, wk, wv, block_out, input_grad):
    total = None
    for kind, w in ((0, wq), (1, wk), (2, wv)):
        groups = []
        for g in range(NG):
            if kind == 0:
                t = gq[g].astype(F32)
            elif kind == 2:
                t = gv[g].astype(F32)
            else:
                t = gk[g].astype(F32)
                for yy in range(1, NY):
                    t = t + gk[yy * NG + g].astype(F32)
            groups.append(t)
        rows = []
        for s in range(S):
            cols = []
            for fb in range(6):
                pair = []
                for n in (2 * fb, 2 * fb + 1):
                    pair.append(blk(groups[n // GH], (n % GH) * 2 + s // 2))
                cols.append(halves(pair[0], pair[1], s % 2, s % 2))
            rows.append(jnp.concatenate(cols, axis=1))
        t = dot_nt(jnp.concatenate(rows, axis=0).astype(BF16), w[...])
        total = t if total is None else total + t
    perm = to_column()
    bo = dot_tn(perm, back[:, 0:D])
    gmid = dot_tn(perm, back[:, D : 2 * D])
    hat, r = moments(x[...].astype(F32).reshape(S * R, D))
    block_out[...] = bo.reshape(S, R, D).astype(BF16)
    grad = gmid + norm_grad(total, gain[...], hat, r)
    input_grad[...] = grad.reshape(S, R, D).astype(BF16)


def swap(x, axes):
    return lax.all_to_all(x, axes, split_axis=0, concat_axis=0, tiled=True)


def local(
    x,
    cot,
    gain_row,
    query_row,
    key_row,
    value_row,
    out_row,
    gain_col,
    query_col,
    key_col,
    value_col,
    out_col,
):
    gain_row = gain_row.reshape(1, D)
    gain_col = gain_col.reshape(1, D)
    keys, qv = call(
        k_project,
        [((NY * NG, R, WIDTH), BF16), ((NG, R, 2 * WIDTH), BF16)],
        x, gain_row, query_row, key_row, value_row,
    )
    keys = swap(keys, ALLRES).reshape(NY * I, WIDTH)
    qv = swap(qv, GRP).reshape(I, 2 * WIDTH)
    values = lax.all_gather(qv[:, WIDTH:], "y", axis=0, tiled=True)
    sent = call(k_send, [((TOK, 2 * D), BF16)], x, cot)
    xc = swap(sent, SEQ)
    parts = swap(call(k_logits, [((NS, ROWS, NY * I), BF16)], qv, keys), SEQ)
    probs, weights = call(
        k_softmax, [((ROWS, NY * I), F32), ((NS, ROWS, NY * I), BF16)], parts
    )
    weights = swap(weights, SEQ).reshape(GH * I, NY * I)
    att = swap(call(k_attend, [((TOK, WIDTH), BF16)], weights, values), WIDE)
    back, grads = call(
        k_column,
        [((TOK, 2 * D), BF16), ((TOK, WIDTH), BF16)],
        att, xc, gain_col, out_row, query_col, key_col, value_col, out_col,
        mem=48,
        scratch=[pltpu.VMEM((TOK, D), BF16)] * 4,
    )
    grads = swap(grads, WIDE)
    gra, gparts = call(
        k_grad_probs, [((I, WIDTH), BF16), ((NS, ROWS, NY * I), BF16)], grads, values
    )
    gparts = swap(gparts, SEQ)
    gv = call(k_grad_values, [((NY * I, WIDTH), BF16)], weights, gra)
    gv = lax.psum_scatter(gv, "y", scatter_dimension=0, tiled=True)
    dl = call(k_softmax_grad, [((NS, ROWS, NY * I), BF16)], gparts, probs)
    dl = swap(dl, SEQ).reshape(GH * I, NY * I)
    back = swap(back, SEQ)
    gq, gk = call(
        k_grad_qk, [((I, WIDTH), BF16), ((NY * I, WIDTH), BF16)], dl, keys, qv
    )
    gk = swap(gk, ALLRES).reshape(NY * NG, R, WIDTH)
    gq = swap(gq, GRP).reshape(NG, R, WIDTH)
    gv = swap(gv, GRP).reshape(NG, R, WIDTH)
    return call(
        k_finish,
        [((S, R, D), BF16), ((S, R, D), BF16)],
        gq, gk, gv, x, back, gain_row, query_row, key_row, value_row,
    )


def solution(mesh):
    fine = Mesh(mesh.devices.reshape(2, 4, 2, 4, 2), ("xh", "z", "xl", "y", "c"))
    spec = P(("xh", "z"), ("xl", "y", "c"), None)
    return jax.shard_map(
        local,
        mesh=fine,
        in_specs=(spec, spec) + (P(),) * 10,
        out_specs=(spec, spec),
        check_vma=False,
    )
```

```python
import math

import jax
import jax.numpy as jnp
from jax import lax
from jax.experimental import pallas as pl
from jax.experimental.pallas import tpu as pltpu
from jax.sharding import Mesh
from jax.sharding import PartitionSpec as P

F32 = jnp.float32
BF16 = jnp.bfloat16
D = 768
HEADS = 12
HEAD_DIM = 64
SEQ = ("xh", "z")
GRP = ("xl", "c")
WIDE = ("xh", "z", "xl", "c")
ALLRES = ("y", "xl", "c")
NS, NG, NY = 8, 4, 4
GH = HEADS // NG
S = 4
R = 48
I = R * NG
CR = 6
CP = 8
TOK = NS * S * CP
ROWS = GH * I // NS
SENT = S * CR
BLOCK = ROWS + 2 * SENT
WIDTH = GH * S * HEAD_DIM
ROW_SCALE = 1.0 / math.sqrt(HEAD_DIM * 32)
COL_SCALE = 1.0 / math.sqrt(HEAD_DIM)


def dot(a, b):
    return lax.dot_general(a, b, (((1,), (0,)), ((), ())), preferred_element_type=F32)


def dot_nt(a, b):
    return lax.dot_general(a, b, (((1,), (1,)), ((), ())), preferred_element_type=F32)


def dot_tn(a, b):
    return lax.dot_general(a, b, (((0,), (0,)), ((), ())), preferred_element_type=F32)


def call(kernel, outs, *args, mem=16, scratch=()):
    shapes = [jax.ShapeDtypeStruct(s, t) for s, t in outs]
    res = pl.pallas_call(
        kernel,
        out_shape=shapes,
        in_specs=[pl.BlockSpec(memory_space=pltpu.VMEM)] * len(args),
        out_specs=[pl.BlockSpec(memory_space=pltpu.VMEM)] * len(outs),
        scratch_shapes=list(scratch),
        compiler_params=pltpu.CompilerParams(vmem_limit_bytes=mem * 2**20),
    )(*args)
    return res[0] if len(outs) == 1 else res


def halves(a, b, half_a, half_b):
    low = lax.broadcasted_iota(jnp.int32, a.shape, 1) < 64
    a = a if half_a == 0 else pltpu.roll(a, 64, 1)
    b = b if half_b == 1 else pltpu.roll(b, 64, 1)
    return jnp.where(low, a, b)


def blk(v, n):
    return v[:, n * 128 : (n + 1) * 128]


def to_column():
    row = lax.broadcasted_iota(jnp.int32, (S * R, S * R), 0)
    col = lax.broadcasted_iota(jnp.int32, (S * R, S * R), 1)
    want = ((row // CR) % S) * R + (row // (CR * S)) * CR + row % CR
    return jnp.where(col == want, 1.0, 0.0).astype(BF16)


def to_padded():
    row = lax.broadcasted_iota(jnp.int32, (TOK, S * R), 0)
    col = lax.broadcasted_iota(jnp.int32, (TOK, S * R), 1)
    r = row % CP
    return jnp.where((r < CR) & (col == (row // CP) * CR + r), 1.0, 0.0).astype(BF16)


def to_wide():
    row = lax.broadcasted_iota(jnp.int32, (TOK, I), 0)
    col = lax.broadcasted_iota(jnp.int32, (TOK, I), 1)
    r = row % CP
    want = ((row // CP) % NG) * R + (row // (CP * NG)) * CR + r
    return jnp.where((r < CR) & (col == want), 1.0, 0.0).astype(BF16)


def moments(v):
    mean = jnp.mean(v, axis=-1, keepdims=True)
    centred = v - mean
    r = lax.rsqrt(jnp.mean(centred * centred, axis=-1, keepdims=True) + 1e-05)
    return centred * r, r


def norm_grad(grad, gain, hat, r):
    g = grad * gain
    return r * (
        g - jnp.mean(g, axis=-1, keepdims=True) - hat * jnp.mean(g * hat, axis=-1, keepdims=True)
    )


def k_project(x, gain, wq, wk, wv, keys, qv):
    hat, _ = moments(x[...].astype(F32).reshape(S * R, D))
    normed = (hat * gain[...]).astype(BF16)
    for which, w in enumerate((wk, wq, wv)):
        y = dot(normed, w[...])
        for g in range(NG):
            for h in range(GH):
                n = g * GH + h
                src = blk(y, n // 2)
                for sp in range(2):
                    a = src[2 * sp * R : (2 * sp + 1) * R]
                    b = src[(2 * sp + 1) * R : (2 * sp + 2) * R]
                    piece = halves(a, b, n % 2, n % 2).astype(BF16)
                    at = h * 256 + sp * 128
                    if which == 0:
                        for yy in range(NY):
                            keys[yy * NG + g, :, at : at + 128] = piece
                    else:
                        at = at + (which - 1) * WIDTH
                        qv[g, :, at : at + 128] = piece


def rows_out(out, tops, first, second):
    full = jnp.concatenate(tops, axis=0)
    for a in range(NS):
        t = slice(a * SENT, (a + 1) * SENT)
        rows = (full[a * ROWS : (a + 1) * ROWS], first[t], second[t])
        out[a] = jnp.concatenate(rows, axis=0).astype(BF16)


def rows_in(parts):
    got = [parts[a].astype(F32) for a in range(NS)]
    first = jnp.concatenate([t[ROWS : ROWS + SENT] for t in got], axis=0)
    second = jnp.concatenate([t[ROWS + SENT :] for t in got], axis=0)
    return first, second


def k_logits(qv, keys, x, cot, out):
    tops = []
    for h in range(GH):
        c = slice(h * 256, (h + 1) * 256)
        tops.append(dot_nt(qv[:, c], keys[:, c]))
    perm = to_column()
    first = dot(perm, x[...].astype(F32).reshape(S * R, D).astype(BF16))
    second = dot(perm, cot[...].astype(F32).reshape(S * R, D).astype(BF16))
    rows_out(out, tops, first, second)


def summed(parts):
    total = parts[0].astype(F32)
    for a in range(1, NS):
        total = total + parts[a].astype(F32)
    return total[:ROWS]


def k_softmax(parts, probs, weights):
    logits = summed(parts) * ROW_SCALE
    e = jnp.exp(logits - jnp.max(logits, axis=-1, keepdims=True))
    p = e / jnp.sum(e, axis=-1, keepdims=True)
    probs[...] = p
    w = p.astype(BF16)
    for a in range(NS):
        weights[a] = w


def k_attend(weights, values, out):
    perm = to_wide()
    for h in range(GH):
        c = slice(h * 256, (h + 1) * 256)
        att = dot(weights[h * I : (h + 1) * I], values[:, c]).astype(BF16)
        out[:, c] = dot(perm, att).astype(BF16)


def k_column(
    att_in, sent, gain, out_row, wq, wk, wv, out_col, back, grad_out, att_s, gq_s, gk_s, gv_s
):
    raw = att_in[...].astype(F32).reshape(NS, NG, CP, WIDTH)
    groups = [raw[:, g].reshape(NS * CP, WIDTH) for g in range(NG)]
    per_seq = []
    for s in range(S):
        cols = []
        for fb in range(6):
            pair = []
            for n in (2 * fb, 2 * fb + 1):
                pair.append(blk(groups[n // GH], (n % GH) * 2 + s // 2))
            cols.append(halves(pair[0], pair[1], s % 2, s % 2))
        per_seq.append(jnp.concatenate(cols, axis=1).reshape(NS, 1, CP, D))
    att_row = jnp.concatenate(per_seq, axis=1).reshape(TOK, D).astype(BF16)
    first, second = rows_in(sent)
    pad = to_padded()
    xc = dot(pad, first.astype(BF16))
    cot = dot(pad, second.astype(BF16)).astype(BF16)
    middle = (xc + dot(att_row, out_row[...])).astype(BF16)
    mid = middle.astype(F32)
    hat, r = moments(mid)
    normed = (hat * gain[...]).astype(BF16)
    q = dot(normed, wq[...]).astype(BF16)
    k = dot(normed, wk[...]).astype(BF16)
    v = dot(normed, wv[...]).astype(BF16)
    ga = dot_nt(cot, out_col[...]).astype(BF16)
    row = lax.broadcasted_iota(jnp.int32, (TOK, TOK), 0)
    col = lax.broadcasted_iota(jnp.int32, (TOK, TOK), 1)
    same = (row % CP) == (col % CP)
    lane = lax.broadcasted_iota(jnp.int32, (1, 128), 1)
    for fb in range(6):
        qb, kb, vb, gb = (blk(t, fb) for t in (q, k, v, ga))
        att = gq = gk = gv = None
        for half in range(2):
            mask = jnp.where((lane < 64) == (half == 0), 1.0, 0.0).astype(BF16)
            km, vm, qm, gm = kb * mask, vb * mask, qb * mask, gb * mask
            logits = jnp.where(same, dot_nt(qb, km) * COL_SCALE, -1e30)
            e = jnp.exp(logits - jnp.max(logits, axis=-1, keepdims=True))
            p = e / jnp.sum(e, axis=-1, keepdims=True)
            w = p.astype(BF16)
            grads = dot_nt(gb, vm)
            dl = p * (grads - jnp.sum(p * grads, axis=-1, keepdims=True)) * COL_SCALE
            dl = dl.astype(BF16)
            parts = (dot(w, vm), dot(dl, km), dot_tn(dl, qm), dot_tn(w, gm))
            if half == 0:
                att, gq, gk, gv = parts
            else:
                att, gq, gk, gv = (t + u for t, u in zip((att, gq, gk, gv), parts))
        at = slice(fb * 128, (fb + 1) * 128)
        att_s[:, at] = att.astype(BF16)
        gq_s[:, at] = gq.astype(BF16)
        gk_s[:, at] = gk.astype(BF16)
        gv_s[:, at] = gv.astype(BF16)
    back[:, 0:D] = (mid + dot(att_s[...], out_col[...])).astype(BF16)
    gn = (
        dot_nt(gq_s[...], wq[...]) + dot_nt(gk_s[...], wk[...]) + dot_nt(gv_s[...], wv[...])
    )
    gmid = (cot.astype(F32) + norm_grad(gn, gain[...], hat, r)).astype(BF16)
    back[:, D : 2 * D] = gmid
    gra = dot_nt(gmid, out_row[...]).reshape(NS, S, CP, D)
    seqs = [gra[:, s].reshape(NS * CP, D) for s in range(S)]
    per_group = []
    for g in range(NG):
        cols = []
        for h in range(GH):
            n = g * GH + h
            for sp in range(2):
                cols.append(
                    halves(blk(seqs[2 * sp], n // 2), blk(seqs[2 * sp + 1], n // 2), n % 2, n % 2)
                )
        per_group.append(jnp.concatenate(cols, axis=1).reshape(NS, 1, CP, WIDTH))
    grad_out[...] = jnp.concatenate(per_group, axis=1).reshape(TOK, WIDTH).astype(BF16)


def k_grad_probs(grads, values, back, gra, out):
    perm = to_wide()
    tops = []
    for h in range(GH):
        c = slice(h * 256, (h + 1) * 256)
        g = dot_tn(perm, grads[:, c]).astype(BF16)
        gra[:, c] = g
        tops.append(dot_nt(g, values[:, c]))
    pad = to_padded()
    rows_out(out, tops, dot_tn(pad, back[:, 0:D]), dot_tn(pad, back[:, D : 2 * D]))


def k_grad_values(weights, gra, out):
    for h in range(GH):
        c = slice(h * 256, (h + 1) * 256)
        out[:, c] = dot_tn(weights[h * I : (h + 1) * I], gra[:, c]).astype(BF16)


def k_softmax_grad(parts, probs, out):
    grads = summed(parts)
    p = probs[...]
    dl = p * (grads - jnp.sum(p * grads, axis=-1, keepdims=True)) * ROW_SCALE
    dl = dl.astype(BF16)
    for a in range(NS):
        out[a] = dl


def k_grad_qk(dl, keys, qv, gv, gqv, gk):
    for h in range(GH):
        c = slice(h * 256, (h + 1) * 256)
        d = dl[h * I : (h + 1) * I]
        gk[:, c] = dot_tn(d, qv[:, c]).astype(BF16)
        gqv[:, c] = dot(d, keys[:, c]).astype(BF16)
    gqv[:, WIDTH : 2 * WIDTH] = gv[...]


def k_finish(gqv, gk, x, sent, gain, wq, wk, wv, block_out, input_grad):
    total = None
    for kind, w in ((0, wq), (1, wk), (2, wv)):
        groups = []
        for g in range(NG):
            if kind == 0:
                t = gqv[g, :, 0:WIDTH].astype(F32)
            elif kind == 2:
                t = gqv[g, :, WIDTH : 2 * WIDTH].astype(F32)
            else:
                t = gk[g].astype(F32)
                for yy in range(1, NY):
                    t = t + gk[yy * NG + g].astype(F32)
            groups.append(t)
        rows = []
        for s in range(S):
            cols = []
            for fb in range(6):
                pair = []
                for n in (2 * fb, 2 * fb + 1):
                    pair.append(blk(groups[n // GH], (n % GH) * 2 + s // 2))
                cols.append(halves(pair[0], pair[1], s % 2, s % 2))
            rows.append(jnp.concatenate(cols, axis=1))
        t = dot_nt(jnp.concatenate(rows, axis=0).astype(BF16), w[...])
        total = t if total is None else total + t
    perm = to_column()
    first, second = rows_in(sent)
    bo = dot_tn(perm, first.astype(BF16))
    gmid = dot_tn(perm, second.astype(BF16))
    hat, r = moments(x[...].astype(F32).reshape(S * R, D))
    block_out[...] = bo.reshape(S, R, D).astype(BF16)
    grad = gmid + norm_grad(total, gain[...], hat, r)
    input_grad[...] = grad.reshape(S, R, D).astype(BF16)


def swap(x, axes):
    return lax.all_to_all(x, axes, split_axis=0, concat_axis=0, tiled=True)


def local(
    x,
    cot,
    gain_row,
    query_row,
    key_row,
    value_row,
    out_row,
    gain_col,
    query_col,
    key_col,
    value_col,
    out_col,
):
    gain_row = gain_row.reshape(1, D)
    gain_col = gain_col.reshape(1, D)
    keys, qv = call(
        k_project,
        [((NY * NG, R, WIDTH), BF16), ((NG, R, 2 * WIDTH), BF16)],
        x, gain_row, query_row, key_row, value_row,
    )
    keys = swap(keys, ALLRES).reshape(NY * I, WIDTH)
    qv = swap(qv, GRP).reshape(I, 2 * WIDTH)
    values = lax.all_gather(qv[:, WIDTH:], "y", axis=0, tiled=True)
    parts = swap(call(k_logits, [((NS, BLOCK, D), BF16)], qv, keys, x, cot), SEQ)
    probs, weights = call(
        k_softmax, [((ROWS, NY * I), F32), ((NS, ROWS, NY * I), BF16)], parts
    )
    weights = swap(weights, SEQ).reshape(GH * I, NY * I)
    att = swap(call(k_attend, [((TOK, WIDTH), BF16)], weights, values), WIDE)
    back, grads = call(
        k_column,
        [((TOK, 2 * D), BF16), ((TOK, WIDTH), BF16)],
        att, parts, gain_col, out_row, query_col, key_col, value_col, out_col,
        mem=32,
        scratch=[pltpu.VMEM((TOK, D), BF16)] * 4,
    )
    grads = swap(grads, WIDE)
    gra, gparts = call(
        k_grad_probs, [((I, WIDTH), BF16), ((NS, BLOCK, D), BF16)], grads, values, back
    )
    gparts = swap(gparts, SEQ)
    gv = call(k_grad_values, [((NY * I, WIDTH), BF16)], weights, gra)
    gv = lax.psum_scatter(gv, "y", scatter_dimension=0, tiled=True)
    dl = call(k_softmax_grad, [((NS, ROWS, NY * I), BF16)], gparts, probs)
    dl = swap(dl, SEQ).reshape(GH * I, NY * I)
    gqv, gk = call(
        k_grad_qk, [((I, 2 * WIDTH), BF16), ((NY * I, WIDTH), BF16)], dl, keys, qv, gv
    )
    gk = swap(gk, ALLRES).reshape(NY * NG, R, WIDTH)
    gqv = swap(gqv, GRP).reshape(NG, R, 2 * WIDTH)
    return call(
        k_finish,
        [((S, R, D), BF16), ((S, R, D), BF16)],
        gqv, gk, x, gparts, gain_row, query_row, key_row, value_row,
    )


def solution(mesh):
    fine = Mesh(mesh.devices.reshape(2, 4, 2, 4, 2), ("xh", "z", "xl", "y", "c"))
    spec = P(("xh", "z"), ("xl", "y", "c"), None)
    return jax.shard_map(
        local,
        mesh=fine,
        in_specs=(spec, spec) + (P(),) * 10,
        out_specs=(spec, spec),
        check_vma=False,
    )
```

```python
import math

import jax
import jax.numpy as jnp
from jax import lax
from jax.experimental import pallas as pl
from jax.experimental.pallas import tpu as pltpu
from jax.sharding import Mesh
from jax.sharding import PartitionSpec as P

F32 = jnp.float32
BF16 = jnp.bfloat16
D = 768
HEADS = 12
HEAD_DIM = 64
SEQ = ("xh", "z")
GRP = ("xl", "c")
WIDE = ("xh", "z", "xl", "c")
ALLRES = ("y", "xl", "c")
NS, NG, NY = 8, 4, 4
GH = HEADS // NG
S = 4
R = 48
I = R * NG
CR = 6
CP = 8
TOK = NS * S * CP
ROWS = GH * I // NS
SENT = S * CR
BLOCK = ROWS + 2 * SENT
WIDTH = GH * S * HEAD_DIM
ROW_SCALE = 1.0 / math.sqrt(HEAD_DIM * 32)
COL_SCALE = 1.0 / math.sqrt(HEAD_DIM)


def dot(a, b):
    return lax.dot_general(a, b, (((1,), (0,)), ((), ())), preferred_element_type=F32)


def dot_nt(a, b):
    return lax.dot_general(a, b, (((1,), (1,)), ((), ())), preferred_element_type=F32)


def dot_tn(a, b):
    return lax.dot_general(a, b, (((0,), (0,)), ((), ())), preferred_element_type=F32)


def call(kernel, outs, *args, mem=16, scratch=(), far=(), sems=0):
    scratch = list(scratch)
    if sems:
        scratch.append(pltpu.SemaphoreType.DMA((sems,)))
    args = [
        pltpu.with_memory_space_constraint(a, pltpu.HBM) if i in far else a
        for i, a in enumerate(args)
    ]
    shapes = [jax.ShapeDtypeStruct(*o) if isinstance(o, tuple) else o for o in outs]
    spaces = [pltpu.VMEM if isinstance(o, tuple) else o.memory_space for o in outs]
    res = pl.pallas_call(
        kernel,
        out_shape=shapes,
        in_specs=[
            pl.BlockSpec(memory_space=pltpu.HBM if i in far else pltpu.VMEM)
            for i in range(len(args))
        ],
        out_specs=[pl.BlockSpec(memory_space=m) for m in spaces],
        scratch_shapes=scratch,
        compiler_params=pltpu.CompilerParams(vmem_limit_bytes=mem * 2**20),
    )(*args)
    return res[0] if len(outs) == 1 else res


def fetch(sources, targets, sems, wait_only=False):
    copies = [
        pltpu.make_async_copy(src, dst, sems.at[i])
        for i, (src, dst) in enumerate(zip(sources, targets))
    ]
    for c in copies:
        c.start()

    def reader(c, dst):
        done = []

        def read():
            if not done:
                c.wait()
                done.append(1)
            return None if wait_only else dst[...]

        return read

    return [reader(c, dst) for c, dst in zip(copies, targets)]


class Pushes:
    def __init__(self, sems, first=0):
        self.sems, self.first, self.begun = sems, first, []

    def start(self, src, dst):
        c = pltpu.make_async_copy(src, dst, self.sems.at[self.first + len(self.begun)])
        c.start()
        self.begun.append(c)

    def finish(self):
        for c in self.begun:
            c.wait()


def my_group():
    return lax.axis_index("xl") * 2 + lax.axis_index("c")


def halves(a, b, half_a, half_b):
    low = lax.broadcasted_iota(jnp.int32, a.shape, 1) < 64
    a = a if half_a == 0 else pltpu.roll(a, 64, 1)
    b = b if half_b == 1 else pltpu.roll(b, 64, 1)
    return jnp.where(low, a, b)


def blk(v, n):
    return v[:, n * 128 : (n + 1) * 128]


def to_column():
    row = lax.broadcasted_iota(jnp.int32, (S * R, S * R), 0)
    col = lax.broadcasted_iota(jnp.int32, (S * R, S * R), 1)
    want = ((row // CR) % S) * R + (row // (CR * S)) * CR + row % CR
    return jnp.where(col == want, 1.0, 0.0).astype(BF16)


def to_padded():
    row = lax.broadcasted_iota(jnp.int32, (TOK, S * R), 0)
    col = lax.broadcasted_iota(jnp.int32, (TOK, S * R), 1)
    r = row % CP
    return jnp.where((r < CR) & (col == (row // CP) * CR + r), 1.0, 0.0).astype(BF16)


def to_wide():
    row = lax.broadcasted_iota(jnp.int32, (TOK, I), 0)
    col = lax.broadcasted_iota(jnp.int32, (TOK, I), 1)
    r = row % CP
    want = ((row // CP) % NG) * R + (row // (CP * NG)) * CR + r
    return jnp.where((r < CR) & (col == want), 1.0, 0.0).astype(BF16)


def moments(v):
    mean = jnp.mean(v, axis=-1, keepdims=True)
    centred = v - mean
    r = lax.rsqrt(jnp.mean(centred * centred, axis=-1, keepdims=True) + 1e-05)
    return centred * r, r


def norm_grad(grad, gain, hat, r):
    g = grad * gain
    return r * (
        g - jnp.mean(g, axis=-1, keepdims=True) - hat * jnp.mean(g * hat, axis=-1, keepdims=True)
    )


def k_project(
    x, gain, wk, wq, wv, keys, qv0, qv1, qv2, qv3, x_s, g_s, wk_s, wq_s, wv_s, keys_s, qv, sems
):
    x, gain, wk, wq, wv = fetch((x, gain, wk, wq, wv), (x_s, g_s, wk_s, wq_s, wv_s), sems)
    push = Pushes(sems, 5)
    hat, _ = moments(x().astype(F32).reshape(S * R, D))
    normed = (hat * gain().reshape(1, D)).astype(BF16)
    for which, w in enumerate((wk, wq, wv)):
        y = dot(normed, w())
        for g in range(NG):
            for h in range(GH):
                n = g * GH + h
                src = blk(y, n // 2)
                for sp in range(2):
                    a = src[2 * sp * R : (2 * sp + 1) * R]
                    b = src[(2 * sp + 1) * R : (2 * sp + 2) * R]
                    piece = halves(a, b, n % 2, n % 2).astype(BF16)
                    at = h * 256 + sp * 128
                    if which == 0:
                        keys_s[g, :, at : at + 128] = piece
                    else:
                        at = at + (which - 1) * WIDTH
                        qv[g, :, at : at + 128] = piece
        if which == 0:
            for yy in range(NY):
                push.start(keys_s, keys.at[yy * NG : (yy + 1) * NG])
    me = my_group()
    for k, out in enumerate((qv0, qv1, qv2, qv3)):
        out[...] = qv[me ^ k]
    push.finish()


def rows_out(out, out_s, products, first, second, push):
    done = []
    for a in range(NS):
        while len(done) * I < (a + 1) * ROWS:
            done.append(products(len(done)))
        head = a * ROWS // I
        rows = jnp.concatenate(done[head:], axis=0)
        lo = a * ROWS - head * I
        t = slice(a * SENT, (a + 1) * SENT)
        rows = jnp.concatenate((rows[lo : lo + ROWS], first[t], second[t]), axis=0)
        out_s[a] = rows.astype(BF16)
        push.start(out_s.at[a], out.at[a])


def rows_in(parts):
    got = [parts[a].astype(F32) for a in range(NS)]
    first = jnp.concatenate([t[ROWS : ROWS + SENT] for t in got], axis=0)
    second = jnp.concatenate([t[ROWS + SENT :] for t in got], axis=0)
    return first, second


def k_logits(
    qv0, qv1, qv2, qv3, keys, x, cot, out, queries, values, out_s, q_s, v_s, sems
):
    push = Pushes(sems)
    me = my_group()
    for k, qv in enumerate((qv0, qv1, qv2, qv3)):
        q_s[me ^ k] = qv[:, 0:WIDTH]
        v_s[me ^ k] = qv[:, WIDTH : 2 * WIDTH]
    push.start(q_s, queries)
    push.start(v_s, values)
    perm = to_column()
    first = dot(perm, x[...].astype(F32).reshape(S * R, D).astype(BF16))
    second = dot(perm, cot[...].astype(F32).reshape(S * R, D).astype(BF16))

    def products(h):
        c = slice(h * 256, (h + 1) * 256)
        return dot_nt(q_s[:, :, c].reshape(I, 256), keys[:, c])

    rows_out(out, out_s, products, first, second, push)
    push.finish()


def summed(parts):
    total = parts[0].astype(F32)
    for a in range(1, NS):
        total = total + parts[a].astype(F32)
    return total[:ROWS]


def k_softmax(parts, probs, weights, p_s, w_s, sems):
    push = Pushes(sems)
    logits = summed(parts) * ROW_SCALE
    e = jnp.exp(logits - jnp.max(logits, axis=-1, keepdims=True))
    p = e / jnp.sum(e, axis=-1, keepdims=True)
    w_s[...] = p.astype(BF16)
    for a in range(NS):
        push.start(w_s, weights.at[a])
    p_s[...] = p
    push.start(p_s, probs)
    push.finish()


def gather_values(parts, values, sems):
    me = lax.axis_index("y")
    reads = fetch(parts, [values.at[me ^ k] for k in range(NY)], sems, wait_only=True)
    for read in reads:
        read()


def k_attend(weights, v0, v1, v2, v3, out, values, sems):
    gather_values((v0, v1, v2, v3), values, sems)
    perm = to_wide()
    for h in range(GH):
        c = slice(h * 256, (h + 1) * 256)
        v = values[:, :, c].reshape(NY * I, 256)
        att = dot(weights[h * I : (h + 1) * I], v).astype(BF16)
        out[:, c] = dot(perm, att).astype(BF16)


def k_column(
    att_in, sent, gain, out_row, wq, wk, wv, out_col, back, grad_out,
    wk_s, wv_s, oc_s, att_s, gq_s, gk_s, gv_s, sems,
):
    wk, wv, out_col = fetch((wk, wv, out_col), (wk_s, wv_s, oc_s), sems)
    raw = att_in[...].astype(F32).reshape(NS, NG, CP, WIDTH)
    groups = [raw[:, g].reshape(NS * CP, WIDTH) for g in range(NG)]
    per_seq = []
    for s in range(S):
        cols = []
        for fb in range(6):
            pair = []
            for n in (2 * fb, 2 * fb + 1):
                pair.append(blk(groups[n // GH], (n % GH) * 2 + s // 2))
            cols.append(halves(pair[0], pair[1], s % 2, s % 2))
        per_seq.append(jnp.concatenate(cols, axis=1).reshape(NS, 1, CP, D))
    att_row = jnp.concatenate(per_seq, axis=1).reshape(TOK, D).astype(BF16)
    first, second = rows_in(sent)
    pad = to_padded()
    xc = dot(pad, first.astype(BF16))
    cot = dot(pad, second.astype(BF16)).astype(BF16)
    middle = (xc + dot(att_row, out_row[...])).astype(BF16)
    mid = middle.astype(F32)
    hat, r = moments(mid)
    normed = (hat * gain[...].reshape(1, D)).astype(BF16)
    q = dot(normed, wq[...]).astype(BF16)
    k = dot(normed, wk()).astype(BF16)
    v = dot(normed, wv()).astype(BF16)
    ga = dot_nt(cot, out_col()).astype(BF16)
    row = lax.broadcasted_iota(jnp.int32, (TOK, TOK), 0)
    col = lax.broadcasted_iota(jnp.int32, (TOK, TOK), 1)
    same = (row % CP) == (col % CP)
    lane = lax.broadcasted_iota(jnp.int32, (1, 128), 1)
    for fb in range(6):
        qb, kb, vb, gb = (blk(t, fb) for t in (q, k, v, ga))
        att = gq = gk = gv = None
        for half in range(2):
            mask = jnp.where((lane < 64) == (half == 0), 1.0, 0.0).astype(BF16)
            km, vm, qm, gm = kb * mask, vb * mask, qb * mask, gb * mask
            logits = jnp.where(same, dot_nt(qb, km) * COL_SCALE, -1e30)
            e = jnp.exp(logits - jnp.max(logits, axis=-1, keepdims=True))
            p = e / jnp.sum(e, axis=-1, keepdims=True)
            w = p.astype(BF16)
            grads = dot_nt(gb, vm)
            dl = p * (grads - jnp.sum(p * grads, axis=-1, keepdims=True)) * COL_SCALE
            dl = dl.astype(BF16)
            parts = (dot(w, vm), dot(dl, km), dot_tn(dl, qm), dot_tn(w, gm))
            if half == 0:
                att, gq, gk, gv = parts
            else:
                att, gq, gk, gv = (t + u for t, u in zip((att, gq, gk, gv), parts))
        at = slice(fb * 128, (fb + 1) * 128)
        att_s[:, at] = att.astype(BF16)
        gq_s[:, at] = gq.astype(BF16)
        gk_s[:, at] = gk.astype(BF16)
        gv_s[:, at] = gv.astype(BF16)
    back[:, 0:D] = (mid + dot(att_s[...], out_col())).astype(BF16)
    gn = (
        dot_nt(gq_s[...], wq[...]) + dot_nt(gk_s[...], wk()) + dot_nt(gv_s[...], wv())
    )
    gmid = (cot.astype(F32) + norm_grad(gn, gain[...].reshape(1, D), hat, r)).astype(BF16)
    back[:, D : 2 * D] = gmid
    gra = dot_nt(gmid, out_row[...]).reshape(NS, S, CP, D)
    seqs = [gra[:, s].reshape(NS * CP, D) for s in range(S)]
    per_group = []
    for g in range(NG):
        cols = []
        for h in range(GH):
            n = g * GH + h
            for sp in range(2):
                cols.append(
                    halves(blk(seqs[2 * sp], n // 2), blk(seqs[2 * sp + 1], n // 2), n % 2, n % 2)
                )
        per_group.append(jnp.concatenate(cols, axis=1).reshape(NS, 1, CP, WIDTH))
    grad_out[...] = jnp.concatenate(per_group, axis=1).reshape(TOK, WIDTH).astype(BF16)


def k_grad_probs(grads, v0, v1, v2, v3, back, gra, out, values, out_s, sems):
    me = lax.axis_index("y")
    reads = fetch(
        (v0, v1, v2, v3), [values.at[me ^ k] for k in range(NY)], sems, wait_only=True
    )
    push = Pushes(sems, NY)
    perm = to_wide()
    for h in range(GH):
        c = slice(h * 256, (h + 1) * 256)
        gra[:, c] = dot_tn(perm, grads[:, c]).astype(BF16)
    pad = to_padded()
    first, second = dot_tn(pad, back[:, 0:D]), dot_tn(pad, back[:, D : 2 * D])
    for read in reads:
        read()

    def products(h):
        c = slice(h * 256, (h + 1) * 256)
        return dot_nt(gra[:, c], values[:, :, c].reshape(NY * I, 256))

    rows_out(out, out_s, products, first, second, push)
    push.finish()


def k_grad_values(weights, gra, gv0, gv1, gv2, gv3, gv, sems):
    for h in range(GH):
        c = slice(h * 256, (h + 1) * 256)
        t = dot_tn(weights[h * I : (h + 1) * I], gra[:, c]).astype(BF16)
        gv[:, :, c] = t.reshape(NY, I, 256)
    me = lax.axis_index("y")
    push = Pushes(sems)
    push.start(gv.at[me], gv0)
    for k, out in enumerate((gv1, gv2, gv3)):
        out[...] = gv[me ^ (k + 1)]
    push.finish()


def k_softmax_grad(parts, probs, *refs):
    out = refs[-1]
    grads = summed(parts)
    p = probs[...]
    dl = p * (grads - jnp.sum(p * grads, axis=-1, keepdims=True)) * ROW_SCALE
    dl = dl.astype(BF16)
    for a in range(NS):
        out[a] = dl


def k_grad_qk(
    dl, keys, queries, gv0, gv1, gv2, gv3, gk, gqv0, gqv1, gqv2, gqv3,
    dl_s, q_s, got_s, gv_s, gq_s, gk_s, own_s, sems,
):
    heads = [slice(h * I, (h + 1) * I) for h in range(GH)]
    *dl, queries, gv0, gv1, gv2, gv3 = fetch(
        [dl.at[c] for c in heads] + [queries, gv0, gv1, gv2, gv3],
        [dl_s.at[c] for c in heads] + [q_s] + [got_s.at[k] for k in range(NY)],
        sems,
    )
    push = Pushes(sems, GH + 1 + NY)
    dl = [d() for d in dl]
    queries = queries()
    for n in range(3):
        r = slice(n * 256, (n + 1) * 256)
        for h in range(GH):
            c = slice(h * 256, (h + 1) * 256)
            gk_s[r, c] = dot_tn(dl[h][:, r], queries[:, c]).astype(BF16)
        push.start(gk_s.at[r], gk.at[r])
    for h in range(GH):
        c = slice(h * 256, (h + 1) * 256)
        gq_s[:, :, c] = dot(dl[h], keys[:, c]).astype(BF16).reshape(NG, R, 256)
    total = gv0().astype(F32)
    for t in (gv1, gv2, gv3):
        total = total + t().astype(F32)
    gv_s[...] = total.astype(BF16).reshape(NG, R, WIDTH)
    me = my_group()
    for k, out in enumerate((own_s, gqv1, gqv2, gqv3)):
        out[:, 0:WIDTH] = gq_s[me ^ k]
        out[:, WIDTH : 2 * WIDTH] = gv_s[me ^ k]
    push.start(own_s, gqv0)
    push.finish()


def k_finish(
    gqv0, gqv1, gqv2, gqv3, gk, x, sent, gain, wq, wk, wv, block_out, input_grad,
    gqv, wq_s, wk_s, wv_s, sems,
):
    wq, wk, wv = fetch((wq, wk, wv), (wq_s, wk_s, wv_s), sems)
    me = my_group()
    for k, got in enumerate((gqv0, gqv1, gqv2, gqv3)):
        gqv[me ^ k] = got[...]
    total = None
    for kind, w in ((0, wq), (1, wk), (2, wv)):
        groups = []
        for g in range(NG):
            if kind == 0:
                t = gqv[g, :, 0:WIDTH].astype(F32)
            elif kind == 2:
                t = gqv[g, :, WIDTH : 2 * WIDTH].astype(F32)
            else:
                t = gk[g].astype(F32)
                for yy in range(1, NY):
                    t = t + gk[yy * NG + g].astype(F32)
            groups.append(t)
        rows = []
        for s in range(S):
            cols = []
            for fb in range(6):
                pair = []
                for n in (2 * fb, 2 * fb + 1):
                    pair.append(blk(groups[n // GH], (n % GH) * 2 + s // 2))
                cols.append(halves(pair[0], pair[1], s % 2, s % 2))
            rows.append(jnp.concatenate(cols, axis=1))
        t = dot_nt(jnp.concatenate(rows, axis=0).astype(BF16), w())
        total = t if total is None else total + t
    perm = to_column()
    first, second = rows_in(sent)
    bo = dot_tn(perm, first.astype(BF16))
    gmid = dot_tn(perm, second.astype(BF16))
    hat, r = moments(x[...].astype(F32).reshape(S * R, D))
    block_out[...] = bo.reshape(S, R, D).astype(BF16)
    grad = gmid + norm_grad(total, gain[...].reshape(1, D), hat, r)
    input_grad[...] = grad.reshape(S, R, D).astype(BF16)


def swap(x, axes):
    return lax.all_to_all(x, axes, split_axis=0, concat_axis=0, tiled=True)


def spread(parts, axes):
    n = len(parts)
    pairs = [[(i, i ^ k) for i in range(n)] for k in range(n)]
    return [parts[0]] + [lax.ppermute(parts[k], axes, pairs[k]) for k in range(1, n)]


def local(
    x,
    cot,
    gain_row,
    query_row,
    key_row,
    value_row,
    out_row,
    gain_col,
    query_col,
    key_col,
    value_col,
    out_col,
):
    piece = ((R, 2 * WIDTH), BF16)
    block = ((NS, BLOCK, NY * I), BF16)
    part = ((NG, R, WIDTH), BF16)
    weight = pltpu.VMEM((D, D), BF16)
    keys, *qv = call(
        k_project,
        [pltpu.HBM((NY * NG, R, WIDTH), BF16)] + [piece] * NG,
        x, gain_row, key_row, query_row, value_row,
        far=(0, 1, 2, 3, 4),
        sems=5 + NY,
        scratch=[pltpu.VMEM((S, R, D), BF16), pltpu.VMEM((D,), F32)]
        + [weight] * 3
        + [pltpu.VMEM(*part), pltpu.VMEM((NG, R, 2 * WIDTH), BF16)],
    )
    qv = spread(qv, GRP)
    keys = swap(keys, ALLRES).reshape(NY * I, WIDTH)
    parts, queries, values = call(
        k_logits,
        [pltpu.HBM(*block), pltpu.HBM(*part), pltpu.HBM(*part)],
        *qv, keys, x, cot,
        sems=2 + NS,
        scratch=[pltpu.VMEM(*block), pltpu.VMEM(*part), pltpu.VMEM(*part)],
    )
    queries = queries.reshape(I, WIDTH)
    parts = swap(parts, SEQ)
    values = spread([values.reshape(I, WIDTH)] * NY, "y")
    probs, weights = call(
        k_softmax,
        [pltpu.HBM((ROWS, NY * I), F32), pltpu.HBM((NS, ROWS, NY * I), BF16)],
        parts,
        sems=1 + NS,
        scratch=[pltpu.VMEM((ROWS, NY * I), F32), pltpu.VMEM((ROWS, NY * I), BF16)],
    )
    weights = swap(weights, SEQ).reshape(GH * I, NY * I)
    gathered = pltpu.VMEM((NY, I, WIDTH), BF16)
    att = call(
        k_attend,
        [((TOK, WIDTH), BF16)],
        weights, *values,
        far=(1, 2, 3, 4),
        sems=NY,
        scratch=[gathered],
    )
    att = swap(att, WIDE)
    back, grads = call(
        k_column,
        [((TOK, 2 * D), BF16), ((TOK, WIDTH), BF16)],
        att, parts, gain_col, out_row, query_col, key_col, value_col, out_col,
        mem=32,
        far=(5, 6, 7),
        sems=3,
        scratch=[weight] * 3 + [pltpu.VMEM((TOK, D), BF16)] * 4,
    )
    grads = swap(grads, WIDE)
    gra, gparts = call(
        k_grad_probs,
        [((I, WIDTH), BF16), pltpu.HBM(*block)],
        grads, *values, back,
        far=(1, 2, 3, 4),
        sems=NY + NS,
        scratch=[gathered, pltpu.VMEM(*block)],
    )
    gparts = swap(gparts, SEQ)
    gv = call(
        k_grad_values,
        [pltpu.HBM((I, WIDTH), BF16)] + [((I, WIDTH), BF16)] * (NY - 1),
        weights, gra,
        sems=1,
        scratch=[gathered],
    )
    gv = spread(gv, "y")
    dl = call(
        k_softmax_grad,
        [((NS, ROWS, NY * I), BF16)],
        gparts, probs, *gv,
        far=(2, 3, 4, 5),
    )
    dl = swap(dl, SEQ).reshape(GH * I, NY * I)
    gk, *gqv = call(
        k_grad_qk,
        [pltpu.HBM((D, D), BF16), pltpu.HBM(*piece)] + [piece] * (NG - 1),
        dl, keys, queries, *gv,
        far=(0, 2, 3, 4, 5, 6),
        sems=GH + 1 + NY + 4,
        scratch=[
            pltpu.VMEM((GH * I, NY * I), BF16),
            pltpu.VMEM((I, WIDTH), BF16),
            gathered,
            pltpu.VMEM(*part),
            pltpu.VMEM(*part),
            weight,
            pltpu.VMEM(*piece),
        ],
    )
    gqv = spread(gqv, GRP)
    gk = swap(gk, ALLRES).reshape(NY * NG, R, WIDTH)
    return call(
        k_finish,
        [((S, R, D), BF16), ((S, R, D), BF16)],
        *gqv, gk, x, gparts, gain_row, query_row, key_row, value_row,
        far=(8, 9, 10),
        sems=3,
        scratch=[pltpu.VMEM((NG, R, 2 * WIDTH), BF16)] + [weight] * 3,
    )


def solution(mesh):
    fine = Mesh(mesh.devices.reshape(2, 4, 2, 4, 2), ("xh", "z", "xl", "y", "c"))
    spec = P(("xh", "z"), ("xl", "y", "c"), None)
    return jax.shard_map(
        local,
        mesh=fine,
        in_specs=(spec, spec) + (P(),) * 10,
        out_specs=(spec, spec),
        check_vma=False,
    )
```

```python
import math

import jax
import jax.numpy as jnp
from jax import lax
from jax.experimental import pallas as pl
from jax.experimental.pallas import tpu as pltpu
from jax.sharding import Mesh
from jax.sharding import PartitionSpec as P

F32 = jnp.float32
BF16 = jnp.bfloat16
D = 768
HEADS = 12
HEAD_DIM = 64
SEQ = ("xh", "z")
GRP = ("xl", "c")
WIDE = ("xh", "z", "xl", "c")
ALLRES = ("y", "xl", "c")
NS, NG, NY = 8, 4, 4
GH = HEADS // NG
S = 4
R = 48
I = R * NG
CR = 6
CP = 8
TOK = NS * S * CP
ROWS = GH * I // NS
SENT = S * CR
BLOCK = ROWS + 2 * SENT
WIDTH = GH * S * HEAD_DIM
ROW_SCALE = 1.0 / math.sqrt(HEAD_DIM * 32)
COL_SCALE = 1.0 / math.sqrt(HEAD_DIM)


def dot(a, b):
    return lax.dot_general(a, b, (((1,), (0,)), ((), ())), preferred_element_type=F32)


def dot_nt(a, b):
    return lax.dot_general(a, b, (((1,), (1,)), ((), ())), preferred_element_type=F32)


def dot_tn(a, b):
    return lax.dot_general(a, b, (((0,), (0,)), ((), ())), preferred_element_type=F32)


def call(kernel, outs, *args, mem=16, scratch=(), far=(), sems=0):
    scratch = list(scratch)
    if sems:
        scratch.append(pltpu.SemaphoreType.DMA((sems,)))
    args = [
        pltpu.with_memory_space_constraint(a, pltpu.HBM) if i in far else a
        for i, a in enumerate(args)
    ]
    shapes = [jax.ShapeDtypeStruct(*o) if isinstance(o, tuple) else o for o in outs]
    spaces = [pltpu.VMEM if isinstance(o, tuple) else o.memory_space for o in outs]
    res = pl.pallas_call(
        kernel,
        out_shape=shapes,
        in_specs=[
            pl.BlockSpec(memory_space=pltpu.HBM if i in far else pltpu.VMEM)
            for i in range(len(args))
        ],
        out_specs=[pl.BlockSpec(memory_space=m) for m in spaces],
        scratch_shapes=scratch,
        compiler_params=pltpu.CompilerParams(vmem_limit_bytes=mem * 2**20),
    )(*args)
    return res[0] if len(outs) == 1 else res


def fetch(sources, targets, sems, wait_only=False, cuts=1):
    reads, at = [], 0
    for src, dst in zip(sources, targets):
        copies = []
        parts = cuts if src.shape[0] == D and len(src.shape) == 2 else 1
        for n in range(parts):
            rows = slice(n * D // parts, (n + 1) * D // parts)
            a, b = (src.at[rows], dst.at[rows]) if parts > 1 else (src, dst)
            copies.append(pltpu.make_async_copy(a, b, sems.at[at]))
            at += 1
        for c in copies:
            c.start()

        def read(copies=copies, dst=dst):
            for c in copies:
                c.wait()
            copies.clear()
            return None if wait_only else dst[...]

        reads.append(read)
    return reads


class Pushes:
    def __init__(self, sems, first=0):
        self.sems, self.first, self.begun = sems, first, []

    def start(self, src, dst):
        c = pltpu.make_async_copy(src, dst, self.sems.at[self.first + len(self.begun)])
        c.start()
        self.begun.append(c)

    def finish(self):
        for c in self.begun:
            c.wait()


def my_group():
    return lax.axis_index("xl") * 2 + lax.axis_index("c")


def halves(a, b, half_a, half_b):
    low = lax.broadcasted_iota(jnp.int32, a.shape, 1) < 64
    a = a if half_a == 0 else pltpu.roll(a, 64, 1)
    b = b if half_b == 1 else pltpu.roll(b, 64, 1)
    return jnp.where(low, a, b)


def blk(v, n):
    return v[:, n * 128 : (n + 1) * 128]


def to_column():
    row = lax.broadcasted_iota(jnp.int32, (S * R, S * R), 0)
    col = lax.broadcasted_iota(jnp.int32, (S * R, S * R), 1)
    want = ((row // CR) % S) * R + (row // (CR * S)) * CR + row % CR
    return jnp.where(col == want, 1.0, 0.0).astype(BF16)


def to_padded():
    row = lax.broadcasted_iota(jnp.int32, (TOK, S * R), 0)
    col = lax.broadcasted_iota(jnp.int32, (TOK, S * R), 1)
    r = row % CP
    return jnp.where((r < CR) & (col == (row // CP) * CR + r), 1.0, 0.0).astype(BF16)


def to_wide():
    row = lax.broadcasted_iota(jnp.int32, (TOK, I), 0)
    col = lax.broadcasted_iota(jnp.int32, (TOK, I), 1)
    r = row % CP
    want = ((row // CP) % NG) * R + (row // (CP * NG)) * CR + r
    return jnp.where((r < CR) & (col == want), 1.0, 0.0).astype(BF16)


def moments(v):
    mean = jnp.mean(v, axis=-1, keepdims=True)
    centred = v - mean
    r = lax.rsqrt(jnp.mean(centred * centred, axis=-1, keepdims=True) + 1e-05)
    return centred * r, r


def norm_grad(grad, gain, hat, r):
    g = grad * gain
    return r * (
        g - jnp.mean(g, axis=-1, keepdims=True) - hat * jnp.mean(g * hat, axis=-1, keepdims=True)
    )


def pieces(y, put, after=None):
    for g in range(NG):
        for h in range(GH):
            n = g * GH + h
            src = blk(y, n // 2)
            for sp in range(2):
                a = src[2 * sp * R : (2 * sp + 1) * R]
                b = src[(2 * sp + 1) * R : (2 * sp + 2) * R]
                put(g, h * 256 + sp * 128, halves(a, b, n % 2, n % 2).astype(BF16))
        if after is not None:
            after(g)


def normed_input(x, gain):
    hat, _ = moments(x.astype(F32).reshape(S * R, D))
    return (hat * gain.reshape(1, D)).astype(BF16)


def k_keys(x, gain, w, keys, x_s, g_s, w_s, keys_s, sems):
    x, gain, w = fetch((x, gain, w), (x_s, g_s, w_s), sems, cuts=4)
    push = Pushes(sems, 6)
    normed = normed_input(x(), gain())

    def put(g, at, piece):
        keys_s[g, :, at : at + 128] = piece

    def after(g):
        for yy in range(NY):
            push.start(keys_s.at[g], keys.at[yy * NG + g])

    pieces(dot(normed, w()), put, after)
    push.finish()


def k_queries_values(x, gain, wq, wv, qv0, qv1, qv2, qv3, x_s, g_s, wq_s, wv_s, qv, sems):
    x, gain, wq, wv = fetch((x, gain, wq, wv), (x_s, g_s, wq_s, wv_s), sems)
    normed = normed_input(x(), gain())
    for first, w in ((0, wq), (WIDTH, wv)):

        def put(g, at, piece, first=first):
            qv[g, :, first + at : first + at + 128] = piece

        pieces(dot(normed, w()), put)
    me = my_group()
    for k, out in enumerate((qv0, qv1, qv2, qv3)):
        out[...] = qv[me ^ k]


def rows_out(out, out_s, products, first, second, push):
    done = []
    for a in range(NS):
        while len(done) * I < (a + 1) * ROWS:
            done.append(products(len(done)))
        head = a * ROWS // I
        rows = jnp.concatenate(done[head:], axis=0)
        lo = a * ROWS - head * I
        t = slice(a * SENT, (a + 1) * SENT)
        rows = jnp.concatenate((rows[lo : lo + ROWS], first[t], second[t]), axis=0)
        out_s[a] = rows.astype(BF16)
        push.start(out_s.at[a], out.at[a])


def rows_in(parts):
    got = [parts[a].astype(F32) for a in range(NS)]
    first = jnp.concatenate([t[ROWS : ROWS + SENT] for t in got], axis=0)
    second = jnp.concatenate([t[ROWS + SENT :] for t in got], axis=0)
    return first, second


def k_logits(
    qv0, qv1, qv2, qv3, keys, x, cot, out, queries, values, out_s, q_s, v_s, sems
):
    push = Pushes(sems)
    me = my_group()
    for k, qv in enumerate((qv0, qv1, qv2, qv3)):
        q_s[me ^ k] = qv[:, 0:WIDTH]
        v_s[me ^ k] = qv[:, WIDTH : 2 * WIDTH]
    push.start(q_s, queries)
    push.start(v_s, values)
    perm = to_column()
    first = dot(perm, x[...].astype(F32).reshape(S * R, D).astype(BF16))
    second = dot(perm, cot[...].astype(F32).reshape(S * R, D).astype(BF16))

    def products(h):
        c = slice(h * 256, (h + 1) * 256)
        return dot_nt(q_s[:, :, c].reshape(I, 256), keys[:, c])

    rows_out(out, out_s, products, first, second, push)
    push.finish()


def summed(parts):
    total = parts[0].astype(F32)
    for a in range(1, NS):
        total = total + parts[a].astype(F32)
    return total[:ROWS]


def k_softmax(parts, values, probs, weights, p_s, w_s, sems):
    push = Pushes(sems)
    logits = summed(parts) * ROW_SCALE
    e = jnp.exp(logits - jnp.max(logits, axis=-1, keepdims=True))
    p = e / jnp.sum(e, axis=-1, keepdims=True)
    w_s[...] = p.astype(BF16)
    for a in range(NS):
        push.start(w_s, weights.at[a])
    p_s[...] = p
    push.start(p_s, probs)
    push.finish()


def k_gather(v0, v1, v2, v3, out, values, sems):
    me = lax.axis_index("y")
    (own,) = fetch((v0,), (values.at[me],), sems, wait_only=True)
    push = Pushes(sems, 1)
    for k, v in enumerate((v1, v2, v3)):
        values[me ^ (k + 1)] = v[...]
    own()
    push.start(values, out)
    push.finish()


def k_attend(weights, values, out):
    perm = to_wide()
    for h in range(GH):
        c = slice(h * 256, (h + 1) * 256)
        v = values[:, :, c].reshape(NY * I, 256)
        att = dot(weights[h * I : (h + 1) * I], v).astype(BF16)
        out[:, c] = dot(perm, att).astype(BF16)


def k_column(
    att_in, sent, gain, out_row, wq, wk, wv, out_col, back, grad_out,
    wk_s, wv_s, oc_s, att_s, gq_s, gk_s, gv_s, sems,
):
    wk, wv, out_col = fetch((wk, wv, out_col), (wk_s, wv_s, oc_s), sems, cuts=2)
    raw = att_in[...].astype(F32).reshape(NS, NG, CP, WIDTH)
    groups = [raw[:, g].reshape(NS * CP, WIDTH) for g in range(NG)]
    per_seq = []
    for s in range(S):
        cols = []
        for fb in range(6):
            pair = []
            for n in (2 * fb, 2 * fb + 1):
                pair.append(blk(groups[n // GH], (n % GH) * 2 + s // 2))
            cols.append(halves(pair[0], pair[1], s % 2, s % 2))
        per_seq.append(jnp.concatenate(cols, axis=1).reshape(NS, 1, CP, D))
    att_row = jnp.concatenate(per_seq, axis=1).reshape(TOK, D).astype(BF16)
    pad = to_padded()
    att_row = dot_tn(pad, att_row).astype(BF16)
    xc, cot = rows_in(sent)
    cot = cot.astype(BF16)
    middle = (xc + dot(att_row, out_row[...])).astype(BF16)
    mid = middle.astype(F32)
    hat, r = moments(mid)
    normed = (hat * gain[...].reshape(1, D)).astype(BF16)
    q = dot(normed, wq[...]).astype(BF16)
    k = dot(normed, wk()).astype(BF16)
    v = dot(normed, wv()).astype(BF16)
    ga = dot_nt(cot, out_col()).astype(BF16)
    row = lax.broadcasted_iota(jnp.int32, (S * R, 1), 0)
    col = lax.broadcasted_iota(jnp.int32, (1, S * R), 1)
    same = (row % CR) == (col % CR)
    lane = lax.broadcasted_iota(jnp.int32, (1, 128), 1)
    for fb in range(6):
        qb, kb, vb, gb = (blk(t, fb) for t in (q, k, v, ga))
        att = gq = gk = gv = None
        for half in range(2):
            mask = jnp.where((lane < 64) == (half == 0), 1.0, 0.0).astype(BF16)
            km, vm, qm, gm = kb * mask, vb * mask, qb * mask, gb * mask
            logits = jnp.where(same, dot_nt(qb, km) * COL_SCALE, -1e30)
            e = jnp.exp(logits - jnp.max(logits, axis=-1, keepdims=True))
            p = e / jnp.sum(e, axis=-1, keepdims=True)
            w = p.astype(BF16)
            grads = dot_nt(gb, vm)
            dl = p * (grads - jnp.sum(p * grads, axis=-1, keepdims=True)) * COL_SCALE
            dl = dl.astype(BF16)
            parts = (dot(w, vm), dot(dl, km), dot_tn(dl, qm), dot_tn(w, gm))
            if half == 0:
                att, gq, gk, gv = parts
            else:
                att, gq, gk, gv = (t + u for t, u in zip((att, gq, gk, gv), parts))
        at = slice(fb * 128, (fb + 1) * 128)
        att_s[:, at] = att.astype(BF16)
        gq_s[:, at] = gq.astype(BF16)
        gk_s[:, at] = gk.astype(BF16)
        gv_s[:, at] = gv.astype(BF16)
    back[:, 0:D] = (mid + dot(att_s[...], out_col())).astype(BF16)
    gn = (
        dot_nt(gq_s[...], wq[...]) + dot_nt(gk_s[...], wk()) + dot_nt(gv_s[...], wv())
    )
    gmid = (cot.astype(F32) + norm_grad(gn, gain[...].reshape(1, D), hat, r)).astype(BF16)
    back[:, D : 2 * D] = gmid
    gra = dot_nt(gmid, out_row[...]).astype(BF16)
    gra = dot(pad, gra).reshape(NS, S, CP, D)
    seqs = [gra[:, s].reshape(NS * CP, D) for s in range(S)]
    per_group = []
    for g in range(NG):
        cols = []
        for h in range(GH):
            n = g * GH + h
            for sp in range(2):
                cols.append(
                    halves(blk(seqs[2 * sp], n // 2), blk(seqs[2 * sp + 1], n // 2), n % 2, n % 2)
                )
        per_group.append(jnp.concatenate(cols, axis=1).reshape(NS, 1, CP, WIDTH))
    grad_out[...] = jnp.concatenate(per_group, axis=1).reshape(TOK, WIDTH).astype(BF16)


def k_grad_probs(grads, values, back, gra, out, gra_s, out_s, sems):
    push = Pushes(sems)
    perm = to_wide()
    for h in range(GH):
        c = slice(h * 256, (h + 1) * 256)
        gra_s[:, c] = dot_tn(perm, grads[:, c]).astype(BF16)
    push.start(gra_s, gra)
    first, second = back[:, 0:D].astype(F32), back[:, D : 2 * D].astype(F32)

    def products(h):
        c = slice(h * 256, (h + 1) * 256)
        return dot_nt(gra_s[:, c], values[:, :, c].reshape(NY * I, 256))

    rows_out(out, out_s, products, first, second, push)
    push.finish()


def k_grad_values(weights, gra, gv0, gv1, gv2, gv3, gv, sems):
    for h in range(GH):
        c = slice(h * 256, (h + 1) * 256)
        t = dot_tn(weights[h * I : (h + 1) * I], gra[:, c]).astype(BF16)
        gv[:, :, c] = t.reshape(NY, I, 256)
    me = lax.axis_index("y")
    push = Pushes(sems)
    push.start(gv.at[me], gv0)
    for k, out in enumerate((gv1, gv2, gv3)):
        out[...] = gv[me ^ (k + 1)]
    push.finish()


def k_sum_values(gv0, gv1, gv2, gv3, gv, g_s, gv_s, sems):
    (gv0,) = fetch((gv0,), (g_s,), sems)
    push = Pushes(sems, 1)
    total = gv1[...].astype(F32) + gv2[...].astype(F32) + gv3[...].astype(F32)
    gv_s[...] = (total + gv0().astype(F32)).astype(BF16)
    push.start(gv_s, gv)
    push.finish()


def k_softmax_grad(parts, probs, gv, out, p_s, sems):
    (probs,) = fetch((probs,), (p_s,), sems)
    grads = summed(parts)
    p = probs()
    dl = p * (grads - jnp.sum(p * grads, axis=-1, keepdims=True)) * ROW_SCALE
    dl = dl.astype(BF16)
    for a in range(NS):
        out[a] = dl


def k_grad_keys(dl, queries, gk, dl_s, q_s, gk_s, sems):
    heads = [slice(h * I, (h + 1) * I) for h in range(GH)]
    *dl, queries = fetch(
        [dl.at[c] for c in heads] + [queries], [dl_s.at[c] for c in heads] + [q_s], sems
    )
    push = Pushes(sems, GH + 1)
    queries = queries()
    for h in range(GH):
        c = slice(h * 256, (h + 1) * 256)
        gk_s[:, c] = dot_tn(dl[h](), queries[:, c]).astype(BF16)
        push.start(gk_s.at[:, c], gk.at[:, c])
    push.finish()


def k_grad_queries(
    dl, keys, gv, gqv0, gqv1, gqv2, gqv3, dl_s, gv_s, gq_s, o0, o1, o2, o3, sems
):
    heads = [slice(h * I, (h + 1) * I) for h in range(GH)]
    *dl, gv = fetch(
        [dl.at[c] for c in heads] + [gv], [dl_s.at[c] for c in heads] + [gv_s], sems
    )
    push = Pushes(sems, GH + 1)
    for h in range(GH):
        c = slice(h * 256, (h + 1) * 256)
        gq_s[:, :, c] = dot(dl[h](), keys[:, c]).astype(BF16).reshape(NG, R, 256)
    gv()
    me = my_group()
    for k, (held, out) in enumerate(zip((o0, o1, o2, o3), (gqv0, gqv1, gqv2, gqv3))):
        held[:, 0:WIDTH] = gq_s[me ^ k]
        held[:, WIDTH : 2 * WIDTH] = gv_s[me ^ k]
        push.start(held, out)
    push.finish()


def k_block_out(sent, out):
    first, _ = rows_in(sent)
    out[...] = dot_tn(to_column(), first.astype(BF16)).reshape(S, R, D).astype(BF16)


def k_finish(
    gqv0, gqv1, gqv2, gqv3, gk, x, sent, gain, wq, wk, wv, input_grad,
    gqv, own_s, gk_s, wq_s, wk_s, wv_s, sems,
):
    gqv0, gk, wq, wk, wv = fetch(
        (gqv0, gk, wq, wk, wv), (own_s, gk_s, wq_s, wk_s, wv_s), sems, cuts=2
    )
    me = my_group()
    for k, got in enumerate((gqv1, gqv2, gqv3)):
        gqv[me ^ (k + 1)] = got[...]
    perm = to_column()
    _, second = rows_in(sent)
    gmid = dot_tn(perm, second.astype(BF16))
    hat, r = moments(x[...].astype(F32).reshape(S * R, D))
    gqv[me] = gqv0()
    gk()
    total = None
    for kind, w in ((0, wq), (1, wk), (2, wv)):
        groups = []
        for g in range(NG):
            if kind == 0:
                t = gqv[g, :, 0:WIDTH].astype(F32)
            elif kind == 2:
                t = gqv[g, :, WIDTH : 2 * WIDTH].astype(F32)
            else:
                t = gk_s[g].astype(F32)
                for yy in range(1, NY):
                    t = t + gk_s[yy * NG + g].astype(F32)
            groups.append(t)
        rows = []
        for s in range(S):
            cols = []
            for fb in range(6):
                pair = []
                for n in (2 * fb, 2 * fb + 1):
                    pair.append(blk(groups[n // GH], (n % GH) * 2 + s // 2))
                cols.append(halves(pair[0], pair[1], s % 2, s % 2))
            rows.append(jnp.concatenate(cols, axis=1))
        t = dot_nt(jnp.concatenate(rows, axis=0).astype(BF16), w())
        total = t if total is None else total + t
    grad = gmid + norm_grad(total, gain[...].reshape(1, D), hat, r)
    input_grad[...] = grad.reshape(S, R, D).astype(BF16)


def swap(x, axes):
    return lax.all_to_all(x, axes, split_axis=0, concat_axis=0, tiled=True)


def spread(parts, axes):
    n = len(parts)
    pairs = [[(i, i ^ k) for i in range(n)] for k in range(n)]
    return [parts[0]] + [lax.ppermute(parts[k], axes, pairs[k]) for k in range(1, n)]


def local(
    x,
    cot,
    gain_row,
    query_row,
    key_row,
    value_row,
    out_row,
    gain_col,
    query_col,
    key_col,
    value_col,
    out_col,
):
    piece = ((R, 2 * WIDTH), BF16)
    block = ((NS, BLOCK, NY * I), BF16)
    part = ((NG, R, WIDTH), BF16)
    weight = pltpu.VMEM((D, D), BF16)
    row = pltpu.VMEM((S, R, D), BF16)
    gain = pltpu.VMEM((D,), F32)
    keys = call(
        k_keys,
        [pltpu.HBM((NY * NG, R, WIDTH), BF16)],
        x, gain_row, key_row,
        far=(0, 1, 2),
        sems=6 + NY * NG,
        scratch=[row, gain, weight, pltpu.VMEM(*part)],
    )
    qv = call(
        k_queries_values,
        [piece] * NG,
        x, gain_row, query_row, value_row,
        far=(0, 1, 2, 3),
        sems=4,
        scratch=[row, gain, weight, weight, pltpu.VMEM((NG, R, 2 * WIDTH), BF16)],
    )
    qv = spread(qv, GRP)
    keys = swap(keys, ALLRES).reshape(NY * I, WIDTH)
    parts, queries, values = call(
        k_logits,
        [pltpu.HBM(*block), pltpu.HBM(*part), pltpu.HBM(*part)],
        *qv, keys, x, cot,
        sems=2 + NS,
        scratch=[pltpu.VMEM(*block), pltpu.VMEM(*part), pltpu.VMEM(*part)],
    )
    queries = queries.reshape(I, WIDTH)
    parts = swap(parts, SEQ)
    values = spread([values.reshape(I, WIDTH)] * NY, "y")
    gathered = pltpu.VMEM((NY, I, WIDTH), BF16)
    values = call(
        k_gather,
        [pltpu.HBM((NY, I, WIDTH), BF16)],
        *values,
        far=(0,),
        sems=2,
        scratch=[gathered],
    )
    probs, weights = call(
        k_softmax,
        [pltpu.HBM((ROWS, NY * I), F32), pltpu.HBM((NS, ROWS, NY * I), BF16)],
        parts, values,
        far=(1,),
        sems=1 + NS,
        scratch=[pltpu.VMEM((ROWS, NY * I), F32), pltpu.VMEM((ROWS, NY * I), BF16)],
    )
    weights = swap(weights, SEQ).reshape(GH * I, NY * I)
    att = call(k_attend, [((TOK, WIDTH), BF16)], weights, values)
    att = swap(att, WIDE)
    back, grads = call(
        k_column,
        [((S * R, 2 * D), BF16), ((TOK, WIDTH), BF16)],
        att, parts, gain_col, out_row, query_col, key_col, value_col, out_col,
        mem=32,
        far=(5, 6, 7),
        sems=6,
        scratch=[weight] * 3 + [pltpu.VMEM((S * R, D), BF16)] * 4,
    )
    grads = swap(grads, WIDE)
    gra, gparts = call(
        k_grad_probs,
        [pltpu.HBM((I, WIDTH), BF16), pltpu.HBM(*block)],
        grads, values, back,
        sems=1 + NS,
        scratch=[pltpu.VMEM((I, WIDTH), BF16), pltpu.VMEM(*block)],
    )
    gparts = swap(gparts, SEQ)
    gv = call(
        k_grad_values,
        [pltpu.HBM((I, WIDTH), BF16)] + [((I, WIDTH), BF16)] * (NY - 1),
        weights, gra,
        sems=1,
        scratch=[gathered],
    )
    gv = spread(gv, "y")
    summand = pltpu.VMEM((I, WIDTH), BF16)
    gv = call(
        k_sum_values,
        [pltpu.HBM((I, WIDTH), BF16)],
        *gv,
        far=(0,),
        sems=2,
        scratch=[summand, summand],
    )
    dl = call(
        k_softmax_grad,
        [((NS, ROWS, NY * I), BF16)],
        gparts, probs, gv,
        far=(1, 2),
        sems=1,
        scratch=[pltpu.VMEM((ROWS, NY * I), F32)],
    )
    dl = swap(dl, SEQ).reshape(GH * I, NY * I)
    dl_s = pltpu.VMEM((GH * I, NY * I), BF16)
    gk = call(
        k_grad_keys,
        [pltpu.HBM((D, D), BF16)],
        dl, queries,
        far=(0, 1),
        sems=2 * GH + 1,
        scratch=[dl_s, summand, weight],
    )
    gqv = call(
        k_grad_queries,
        [pltpu.HBM(*piece)] * NG,
        dl, keys, gv.reshape(*part[0]),
        far=(0, 2),
        sems=GH + 1 + NG,
        scratch=[dl_s, pltpu.VMEM(*part), pltpu.VMEM(*part)] + [pltpu.VMEM(*piece)] * NG,
    )
    gqv = spread(gqv, GRP)
    gk = swap(gk, ALLRES).reshape(NY * NG, R, WIDTH)
    block_out = call(k_block_out, [((S, R, D), BF16)], gparts)
    input_grad = call(
        k_finish,
        [((S, R, D), BF16)],
        *gqv, gk, x, gparts, gain_row, query_row, key_row, value_row,
        far=(0, 4, 8, 9, 10),
        sems=8,
        scratch=[
            pltpu.VMEM((NG, R, 2 * WIDTH), BF16),
            pltpu.VMEM(*piece),
            pltpu.VMEM((NY * NG, R, WIDTH), BF16),
            weight,
            weight,
            weight,
        ],
    )
    return block_out, input_grad


def solution(mesh):
    fine = Mesh(mesh.devices.reshape(2, 4, 2, 4, 2), ("xh", "z", "xl", "y", "c"))
    spec = P(("xh", "z"), ("xl", "y", "c"), None)
    return jax.shard_map(
        local,
        mesh=fine,
        in_specs=(spec, spec) + (P(),) * 10,
        out_specs=(spec, spec),
        check_vma=False,
    )
```

```python
import math

import jax
import jax.numpy as jnp
from jax import lax
from jax.experimental import pallas as pl
from jax.experimental.pallas import tpu as pltpu
from jax.sharding import Mesh
from jax.sharding import PartitionSpec as P

F32 = jnp.float32
BF16 = jnp.bfloat16
D = 768
HEADS = 12
HEAD_DIM = 64
SEQ = ("xh", "z")
GRP = ("xl", "c")
WIDE = ("xh", "z", "xl", "c")
ALLRES = ("y", "xl", "c")
NS, NG, NY = 8, 4, 4
GH = HEADS // NG
S = 4
R = 48
I = R * NG
CR = 6
CP = 8
TOK = NS * S * CP
ROWS = GH * I // NS
SENT = S * CR
BLOCK = ROWS + 2 * SENT
WIDTH = GH * S * HEAD_DIM
ROW_SCALE = 1.0 / math.sqrt(HEAD_DIM * 32)
COL_SCALE = 1.0 / math.sqrt(HEAD_DIM)


def dot(a, b):
    return lax.dot_general(a, b, (((1,), (0,)), ((), ())), preferred_element_type=F32)


def dot_nt(a, b):
    return lax.dot_general(a, b, (((1,), (1,)), ((), ())), preferred_element_type=F32)


def dot_tn(a, b):
    return lax.dot_general(a, b, (((0,), (0,)), ((), ())), preferred_element_type=F32)


def call(kernel, outs, *args, mem=16, scratch=(), far=(), sems=0):
    scratch = list(scratch)
    if sems:
        scratch.append(pltpu.SemaphoreType.DMA((sems,)))
    args = [
        pltpu.with_memory_space_constraint(a, pltpu.HBM) if i in far else a
        for i, a in enumerate(args)
    ]
    shapes = [jax.ShapeDtypeStruct(*o) if isinstance(o, tuple) else o for o in outs]
    spaces = [pltpu.VMEM if isinstance(o, tuple) else o.memory_space for o in outs]
    res = pl.pallas_call(
        kernel,
        out_shape=shapes,
        in_specs=[
            pl.BlockSpec(memory_space=pltpu.HBM if i in far else pltpu.VMEM)
            for i in range(len(args))
        ],
        out_specs=[pl.BlockSpec(memory_space=m) for m in spaces],
        scratch_shapes=scratch,
        compiler_params=pltpu.CompilerParams(vmem_limit_bytes=mem * 2**20),
    )(*args)
    return res[0] if len(outs) == 1 else res


def fetch(sources, targets, sems, wait_only=False, cuts=1):
    reads, at = [], 0
    for src, dst in zip(sources, targets):
        copies = []
        parts = cuts if src.shape[0] == D and len(src.shape) == 2 else 1
        for n in range(parts):
            rows = slice(n * D // parts, (n + 1) * D // parts)
            a, b = (src.at[rows], dst.at[rows]) if parts > 1 else (src, dst)
            copies.append(pltpu.make_async_copy(a, b, sems.at[at]))
            at += 1
        for c in copies:
            c.start()

        def read(copies=copies, dst=dst):
            for c in copies:
                c.wait()
            copies.clear()
            return None if wait_only else dst[...]

        reads.append(read)
    return reads


class Pushes:
    def __init__(self, sems, first=0):
        self.sems, self.first, self.begun = sems, first, []

    def start(self, src, dst):
        c = pltpu.make_async_copy(src, dst, self.sems.at[self.first + len(self.begun)])
        c.start()
        self.begun.append(c)

    def finish(self):
        for c in self.begun:
            c.wait()


def my_group():
    return lax.axis_index("xl") * 2 + lax.axis_index("c")


def halves(a, b, half_a, half_b):
    low = lax.broadcasted_iota(jnp.int32, a.shape, 1) < 64
    a = a if half_a == 0 else pltpu.roll(a, 64, 1)
    b = b if half_b == 1 else pltpu.roll(b, 64, 1)
    return jnp.where(low, a, b)


def blk(v, n):
    return v[:, n * 128 : (n + 1) * 128]


def to_column():
    row = lax.broadcasted_iota(jnp.int32, (S * R, S * R), 0)
    col = lax.broadcasted_iota(jnp.int32, (S * R, S * R), 1)
    want = ((row // CR) % S) * R + (row // (CR * S)) * CR + row % CR
    return jnp.where(col == want, 1.0, 0.0).astype(BF16)


def to_padded():
    row = lax.broadcasted_iota(jnp.int32, (TOK, S * R), 0)
    col = lax.broadcasted_iota(jnp.int32, (TOK, S * R), 1)
    r = row % CP
    return jnp.where((r < CR) & (col == (row // CP) * CR + r), 1.0, 0.0).astype(BF16)


def to_wide():
    row = lax.broadcasted_iota(jnp.int32, (TOK, I), 0)
    col = lax.broadcasted_iota(jnp.int32, (TOK, I), 1)
    r = row % CP
    want = ((row // CP) % NG) * R + (row // (CP * NG)) * CR + r
    return jnp.where((r < CR) & (col == want), 1.0, 0.0).astype(BF16)


def moments(v):
    mean = jnp.mean(v, axis=-1, keepdims=True)
    centred = v - mean
    r = lax.rsqrt(jnp.mean(centred * centred, axis=-1, keepdims=True) + 1e-05)
    return centred * r, r


def norm_grad(grad, gain, hat, r):
    g = grad * gain
    return r * (
        g - jnp.mean(g, axis=-1, keepdims=True) - hat * jnp.mean(g * hat, axis=-1, keepdims=True)
    )


def pieces(y, put, after=None):
    for g in range(NG):
        for h in range(GH):
            n = g * GH + h
            src = blk(y, n // 2)
            for sp in range(2):
                a = src[2 * sp * R : (2 * sp + 1) * R]
                b = src[(2 * sp + 1) * R : (2 * sp + 2) * R]
                put(g, h * 256 + sp * 128, halves(a, b, n % 2, n % 2).astype(BF16))
        if after is not None:
            after(g)


def normed_input(x, gain):
    hat, _ = moments(x.astype(F32).reshape(S * R, D))
    return (hat * gain.reshape(1, D)).astype(BF16)


def k_keys(x, gain, w, keys, x_s, g_s, w_s, keys_s, sems):
    x, gain, w = fetch((x, gain, w), (x_s, g_s, w_s), sems, cuts=4)
    push = Pushes(sems, 6)
    normed = normed_input(x(), gain())

    def put(g, at, piece):
        keys_s[g, :, at : at + 128] = piece

    def after(g):
        for yy in range(NY):
            push.start(keys_s.at[g], keys.at[yy * NG + g])

    pieces(dot(normed, w()), put, after)
    push.finish()


def k_queries_values(x, gain, wq, wv, qv0, qv1, qv2, qv3, x_s, g_s, wq_s, wv_s, qv, sems):
    x, gain, wq, wv = fetch((x, gain, wq, wv), (x_s, g_s, wq_s, wv_s), sems)
    normed = normed_input(x(), gain())
    for first, w in ((0, wq), (WIDTH, wv)):

        def put(g, at, piece, first=first):
            qv[g, :, first + at : first + at + 128] = piece

        pieces(dot(normed, w()), put)
    me = my_group()
    for k, out in enumerate((qv0, qv1, qv2, qv3)):
        out[...] = qv[me ^ k]


def rows_out(out, out_s, products, first, second, push):
    done = []
    for a in range(NS):
        while len(done) * I < (a + 1) * ROWS:
            done.append(products(len(done)))
        head = a * ROWS // I
        rows = jnp.concatenate(done[head:], axis=0)
        lo = a * ROWS - head * I
        t = slice(a * SENT, (a + 1) * SENT)
        rows = jnp.concatenate((rows[lo : lo + ROWS], first[t], second[t]), axis=0)
        out_s[a] = rows.astype(BF16)
        push.start(out_s.at[a], out.at[a])


def rows_in(parts):
    got = [parts[a].astype(F32) for a in range(NS)]
    first = jnp.concatenate([t[ROWS : ROWS + SENT] for t in got], axis=0)
    second = jnp.concatenate([t[ROWS + SENT :] for t in got], axis=0)
    return first, second


def k_logits(
    qv0, qv1, qv2, qv3, keys, x, cot, out, queries, values, out_s, q_s, v_s, sems
):
    push = Pushes(sems)
    me = my_group()
    for k, qv in enumerate((qv0, qv1, qv2, qv3)):
        q_s[me ^ k] = qv[:, 0:WIDTH]
        v_s[me ^ k] = qv[:, WIDTH : 2 * WIDTH]
    push.start(q_s, queries)
    push.start(v_s, values)
    perm = to_column()
    first = dot(perm, x[...].astype(F32).reshape(S * R, D).astype(BF16))
    second = dot(perm, cot[...].astype(F32).reshape(S * R, D).astype(BF16))

    def products(h):
        c = slice(h * 256, (h + 1) * 256)
        return dot_nt(q_s[:, :, c].reshape(I, 256), keys[:, c])

    rows_out(out, out_s, products, first, second, push)
    push.finish()


def summed(parts):
    total = parts[0].astype(F32)
    for a in range(1, NS):
        total = total + parts[a].astype(F32)
    return total[:ROWS]


def k_softmax(parts, values, probs, weights, p_s, sems):
    push = Pushes(sems)
    logits = summed(parts) * ROW_SCALE
    e = jnp.exp(logits - jnp.max(logits, axis=-1, keepdims=True))
    p = e * (1.0 / jnp.sum(e, axis=-1, keepdims=True))
    p_s[...] = p
    push.start(p_s, probs)
    w = p.astype(BF16)
    for a in range(NS):
        weights[a] = w
    push.finish()


def k_gather(v0, v1, v2, v3, out, values, sems):
    me = lax.axis_index("y")
    (own,) = fetch((v0,), (values.at[me],), sems, wait_only=True)
    push = Pushes(sems, 1)
    for k, v in enumerate((v1, v2, v3)):
        values[me ^ (k + 1)] = v[...]
    own()
    push.start(values, out)
    push.finish()


def k_attend(weights, values, out):
    perm = to_wide()
    for h in range(GH):
        c = slice(h * 256, (h + 1) * 256)
        v = values[:, :, c].reshape(NY * I, 256)
        att = dot(weights[h * I : (h + 1) * I], v).astype(BF16)
        out[:, c] = dot(perm, att).astype(BF16)


def k_column(
    att_in, sent, gain, out_row, wq, wk, wv, out_col, back, grad_out,
    wk_s, wv_s, oc_s, att_s, gq_s, gk_s, gv_s, sems,
):
    wk, wv, out_col = fetch((wk, wv, out_col), (wk_s, wv_s, oc_s), sems, cuts=2)
    raw = att_in[...].astype(F32).reshape(NS, NG, CP, WIDTH)
    groups = [raw[:, g].reshape(NS * CP, WIDTH) for g in range(NG)]
    per_seq = []
    for s in range(S):
        cols = []
        for fb in range(6):
            pair = []
            for n in (2 * fb, 2 * fb + 1):
                pair.append(blk(groups[n // GH], (n % GH) * 2 + s // 2))
            cols.append(halves(pair[0], pair[1], s % 2, s % 2))
        per_seq.append(jnp.concatenate(cols, axis=1).reshape(NS, 1, CP, D))
    att_row = jnp.concatenate(per_seq, axis=1).reshape(TOK, D).astype(BF16)
    pad = to_padded()
    att_row = dot_tn(pad, att_row).astype(BF16)
    xc, cot = rows_in(sent)
    cot = cot.astype(BF16)
    middle = (xc + dot(att_row, out_row[...])).astype(BF16)
    mid = middle.astype(F32)
    hat, r = moments(mid)
    normed = (hat * gain[...].reshape(1, D)).astype(BF16)
    q = dot(normed, wq[...]).astype(BF16) * jnp.asarray(COL_SCALE, BF16)
    k = dot(normed, wk()).astype(BF16)
    v = dot(normed, wv()).astype(BF16)
    ga = dot_nt(cot, out_col()).astype(BF16)
    row = lax.broadcasted_iota(jnp.int32, (2 * S * R, 1), 0)
    col = lax.broadcasted_iota(jnp.int32, (1, S * R), 1)
    same = (row % CR) == (col % CR)
    low = lax.broadcasted_iota(jnp.int32, (1, 128), 1) < 64
    masks = [jnp.where(low == first, 1.0, 0.0).astype(BF16) for first in (True, False)]

    def stack(t):
        return jnp.concatenate([t * masks[0], t * masks[1]], axis=0)

    def unstack(t):
        return jnp.where(low, t[: S * R], t[S * R :])

    for fb in range(6):
        at = slice(fb * 128, (fb + 1) * 128)
        kb, vb = blk(k, fb), blk(v, fb)
        qs, gs = stack(blk(q, fb)), stack(blk(ga, fb))
        logits = jnp.where(same, dot_nt(qs, kb), -1e30)
        e = jnp.exp(logits - jnp.max(logits, axis=-1, keepdims=True))
        p = e * (1.0 / jnp.sum(e, axis=-1, keepdims=True))
        w = p.astype(BF16)
        grads = dot_nt(gs, vb)
        dl = (p * (grads - jnp.sum(p * grads, axis=-1, keepdims=True))).astype(BF16)
        att_s[:, at] = unstack(dot(w, vb)).astype(BF16)
        gq_s[:, at] = (unstack(dot(dl, kb)) * COL_SCALE).astype(BF16)
        gk_s[:, at] = dot_tn(dl, qs).astype(BF16)
        gv_s[:, at] = dot_tn(w, gs).astype(BF16)
    back[:, 0:D] = (mid + dot(att_s[...], out_col())).astype(BF16)
    gn = (
        dot_nt(gq_s[...], wq[...]) + dot_nt(gk_s[...], wk()) + dot_nt(gv_s[...], wv())
    )
    gmid = (cot.astype(F32) + norm_grad(gn, gain[...].reshape(1, D), hat, r)).astype(BF16)
    back[:, D : 2 * D] = gmid
    gra = dot_nt(gmid, out_row[...]).astype(BF16)
    gra = dot(pad, gra).reshape(NS, S, CP, D)
    seqs = [gra[:, s].reshape(NS * CP, D) for s in range(S)]
    per_group = []
    for g in range(NG):
        cols = []
        for h in range(GH):
            n = g * GH + h
            for sp in range(2):
                cols.append(
                    halves(blk(seqs[2 * sp], n // 2), blk(seqs[2 * sp + 1], n // 2), n % 2, n % 2)
                )
        per_group.append(jnp.concatenate(cols, axis=1).reshape(NS, 1, CP, WIDTH))
    grad_out[...] = jnp.concatenate(per_group, axis=1).reshape(TOK, WIDTH).astype(BF16)


def k_grad_probs(grads, values, back, gra, out, gra_s, out_s, sems):
    push = Pushes(sems)
    perm = to_wide()
    for h in range(GH):
        c = slice(h * 256, (h + 1) * 256)
        gra_s[:, c] = dot_tn(perm, grads[:, c]).astype(BF16)
    push.start(gra_s, gra)
    first, second = back[:, 0:D].astype(F32), back[:, D : 2 * D].astype(F32)

    def products(h):
        c = slice(h * 256, (h + 1) * 256)
        return dot_nt(gra_s[:, c], values[:, :, c].reshape(NY * I, 256))

    rows_out(out, out_s, products, first, second, push)
    push.finish()


def k_grad_values(weights, gra, gv0, gv1, gv2, gv3, gv, sems):
    for h in range(GH):
        c = slice(h * 256, (h + 1) * 256)
        t = dot_tn(weights[h * I : (h + 1) * I], gra[:, c]).astype(BF16)
        gv[:, :, c] = t.reshape(NY, I, 256)
    me = lax.axis_index("y")
    push = Pushes(sems)
    push.start(gv.at[me], gv0)
    for k, out in enumerate((gv1, gv2, gv3)):
        out[...] = gv[me ^ (k + 1)]
    push.finish()


def k_sum_values(gv0, gv1, gv3, gv, g_s, gv_s, sems):
    (gv0,) = fetch((gv0,), (g_s,), sems)
    push = Pushes(sems, 1)
    total = gv1[...].astype(F32) + gv3[...].astype(F32)
    gv_s[...] = total + gv0().astype(F32)
    push.start(gv_s, gv)
    push.finish()


def k_softmax_grad(parts, probs, gv, out, p_s, out_s, sems):
    (probs,) = fetch((probs,), (p_s,), sems)
    push = Pushes(sems, 1)
    grads = summed(parts)
    p = probs()
    dl = p * (grads - jnp.sum(p * grads, axis=-1, keepdims=True)) * ROW_SCALE
    out_s[...] = dl.astype(BF16)
    for a in range(NS):
        push.start(out_s, out.at[a])
    push.finish()


def k_grad_keys(dl, queries, before, gk, dl_s, q_s, gk_s, sems):
    heads = [slice(h * I, (h + 1) * I) for h in range(GH)]
    queries, *dl = fetch(
        [queries] + [dl.at[c] for c in heads], [q_s] + [dl_s.at[c] for c in heads], sems
    )
    push = Pushes(sems, GH + 1)
    queries = queries()
    for h in range(GH):
        c = slice(h * 256, (h + 1) * 256)
        gk_s[:, c] = dot_tn(dl[h](), queries[:, c]).astype(BF16)
        push.start(gk_s.at[:, c], gk.at[:, c])
    push.finish()


def k_grad_queries(
    dl, keys, gv, gv2, gqv0, gqv1, gqv2, gqv3,
    dl_s, sum_s, two_s, gv_s, gq_s, o0, o1, o2, o3, sems,
):
    heads = [slice(h * I, (h + 1) * I) for h in range(GH)]
    *dl, gv, gv2 = fetch(
        [dl.at[c] for c in heads] + [gv, gv2],
        [dl_s.at[c] for c in heads] + [sum_s, two_s],
        sems,
    )
    push = Pushes(sems, GH + 2)
    for h in range(GH):
        c = slice(h * 256, (h + 1) * 256)
        gq_s[:, :, c] = dot(dl[h](), keys[:, c]).astype(BF16).reshape(NG, R, 256)
    gv_s[...] = (gv() + gv2().astype(F32)).astype(BF16).reshape(NG, R, WIDTH)
    me = my_group()
    for k, (held, out) in enumerate(zip((o0, o1, o2, o3), (gqv0, gqv1, gqv2, gqv3))):
        held[:, 0:WIDTH] = gq_s[me ^ k]
        held[:, WIDTH : 2 * WIDTH] = gv_s[me ^ k]
        push.start(held, out)
    push.finish()


def k_block_out(sent, out):
    first, _ = rows_in(sent)
    out[...] = dot_tn(to_column(), first.astype(BF16)).reshape(S, R, D).astype(BF16)


def k_finish(
    gqv0, gqv1, gqv2, gqv3, gk, x, sent, gain, wq, wk, wv, input_grad,
    gqv, own_s, gk_s, wq_s, wk_s, wv_s, sems,
):
    gqv0, wq, gk, wk, wv = fetch(
        (gqv0, wq, gk, wk, wv), (own_s, wq_s, gk_s, wk_s, wv_s), sems, cuts=2
    )
    me = my_group()
    for k, got in enumerate((gqv1, gqv2, gqv3)):
        gqv[me ^ (k + 1)] = got[...]
    perm = to_column()
    _, second = rows_in(sent)
    gmid = dot_tn(perm, second.astype(BF16))
    hat, r = moments(x[...].astype(F32).reshape(S * R, D))
    gqv[me] = gqv0()
    total = None
    for kind, w in ((0, wq), (1, wk), (2, wv)):
        groups = []
        if kind == 1:
            gk()
        for g in range(NG):
            if kind == 0:
                t = gqv[g, :, 0:WIDTH].astype(F32)
            elif kind == 2:
                t = gqv[g, :, WIDTH : 2 * WIDTH].astype(F32)
            else:
                t = gk_s[g].astype(F32)
                for yy in range(1, NY):
                    t = t + gk_s[yy * NG + g].astype(F32)
            groups.append(t)
        rows = []
        for s in range(S):
            cols = []
            for fb in range(6):
                pair = []
                for n in (2 * fb, 2 * fb + 1):
                    pair.append(blk(groups[n // GH], (n % GH) * 2 + s // 2))
                cols.append(halves(pair[0], pair[1], s % 2, s % 2))
            rows.append(jnp.concatenate(cols, axis=1))
        t = dot_nt(jnp.concatenate(rows, axis=0).astype(BF16), w())
        total = t if total is None else total + t
    grad = gmid + norm_grad(total, gain[...].reshape(1, D), hat, r)
    input_grad[...] = grad.reshape(S, R, D).astype(BF16)


def swap(x, axes):
    return lax.all_to_all(x, axes, split_axis=0, concat_axis=0, tiled=True)


def spread(parts, axes):
    n = len(parts)
    pairs = [[(i, i ^ k) for i in range(n)] for k in range(n)]
    return [parts[0]] + [lax.ppermute(parts[k], axes, pairs[k]) for k in range(1, n)]


def local(
    x,
    cot,
    gain_row,
    query_row,
    key_row,
    value_row,
    out_row,
    gain_col,
    query_col,
    key_col,
    value_col,
    out_col,
):
    piece = ((R, 2 * WIDTH), BF16)
    block = ((NS, BLOCK, NY * I), BF16)
    part = ((NG, R, WIDTH), BF16)
    weight = pltpu.VMEM((D, D), BF16)
    row = pltpu.VMEM((S, R, D), BF16)
    gain = pltpu.VMEM((D,), F32)
    keys = call(
        k_keys,
        [pltpu.HBM((NY * NG, R, WIDTH), BF16)],
        x, gain_row, key_row,
        far=(0, 1, 2),
        sems=6 + NY * NG,
        scratch=[row, gain, weight, pltpu.VMEM(*part)],
    )
    qv = call(
        k_queries_values,
        [piece] * NG,
        x, gain_row, query_row, value_row,
        far=(0, 1, 2, 3),
        sems=4,
        scratch=[row, gain, weight, weight, pltpu.VMEM((NG, R, 2 * WIDTH), BF16)],
    )
    qv = spread(qv, GRP)
    keys = swap(keys, ALLRES).reshape(NY * I, WIDTH)
    parts, queries, values = call(
        k_logits,
        [pltpu.HBM(*block), pltpu.HBM(*part), pltpu.HBM(*part)],
        *qv, keys, x, cot,
        sems=2 + NS,
        scratch=[pltpu.VMEM(*block), pltpu.VMEM(*part), pltpu.VMEM(*part)],
    )
    queries = queries.reshape(I, WIDTH)
    parts = swap(parts, SEQ)
    values = spread([values.reshape(I, WIDTH)] * NY, "y")
    gathered = pltpu.VMEM((NY, I, WIDTH), BF16)
    values = call(
        k_gather,
        [pltpu.HBM((NY, I, WIDTH), BF16)],
        *values,
        far=(0,),
        sems=2,
        scratch=[gathered],
    )
    probs, weights = call(
        k_softmax,
        [pltpu.HBM((ROWS, NY * I), F32), ((NS, ROWS, NY * I), BF16)],
        parts, values,
        far=(1,),
        sems=1,
        scratch=[pltpu.VMEM((ROWS, NY * I), F32)],
    )
    weights = swap(weights, SEQ).reshape(GH * I, NY * I)
    att = call(k_attend, [((TOK, WIDTH), BF16)], weights, values)
    att = swap(att, WIDE)
    back, grads = call(
        k_column,
        [((S * R, 2 * D), BF16), ((TOK, WIDTH), BF16)],
        att, parts, gain_col, out_row, query_col, key_col, value_col, out_col,
        mem=32,
        far=(5, 6, 7),
        sems=6,
        scratch=[weight] * 3 + [pltpu.VMEM((S * R, D), BF16)] * 4,
    )
    grads = swap(grads, WIDE)
    gra, gparts = call(
        k_grad_probs,
        [pltpu.HBM((I, WIDTH), BF16), pltpu.HBM(*block)],
        grads, values, back,
        sems=1 + NS,
        scratch=[pltpu.VMEM((I, WIDTH), BF16), pltpu.VMEM(*block)],
    )
    gparts = swap(gparts, SEQ)
    gv = call(
        k_grad_values,
        [pltpu.HBM((I, WIDTH), BF16)] + [((I, WIDTH), BF16)] * (NY - 1),
        weights, gra,
        sems=1,
        scratch=[gathered],
    )
    gv = spread(gv, "y")
    summand = pltpu.VMEM((I, WIDTH), BF16)
    sum_s = pltpu.VMEM((I, WIDTH), F32)
    some = call(
        k_sum_values,
        [pltpu.HBM((I, WIDTH), F32)],
        gv[0], gv[1], gv[3],
        far=(0,),
        sems=2,
        scratch=[summand, sum_s],
    )
    dl = call(
        k_softmax_grad,
        [pltpu.HBM((NS, ROWS, NY * I), BF16)],
        gparts, probs, some,
        far=(1, 2),
        sems=1 + NS,
        scratch=[pltpu.VMEM((ROWS, NY * I), F32), pltpu.VMEM((ROWS, NY * I), BF16)],
    )
    dl = swap(dl, SEQ).reshape(GH * I, NY * I)
    dl_s = pltpu.VMEM((GH * I, NY * I), BF16)
    gk = call(
        k_grad_keys,
        [pltpu.HBM((D, D), BF16)],
        dl, queries, gv[2],
        far=(0, 1, 2),
        sems=2 * GH + 1,
        scratch=[dl_s, summand, weight],
    )
    gqv = call(
        k_grad_queries,
        [pltpu.HBM(*piece)] * NG,
        dl, keys, some, gv[2],
        far=(0, 2, 3),
        sems=GH + 2 + NG,
        scratch=[dl_s, sum_s, summand, pltpu.VMEM(*part), pltpu.VMEM(*part)] + [pltpu.VMEM(*piece)] * NG,
    )
    gqv = spread(gqv, GRP)
    gk = swap(gk, ALLRES).reshape(NY * NG, R, WIDTH)
    block_out = call(k_block_out, [((S, R, D), BF16)], gparts)
    input_grad = call(
        k_finish,
        [((S, R, D), BF16)],
        *gqv, gk, x, gparts, gain_row, query_row, key_row, value_row,
        far=(0, 4, 8, 9, 10),
        sems=8,
        scratch=[
            pltpu.VMEM((NG, R, 2 * WIDTH), BF16),
            pltpu.VMEM(*piece),
            pltpu.VMEM((NY * NG, R, WIDTH), BF16),
            weight,
            weight,
            weight,
        ],
    )
    return block_out, input_grad


def solution(mesh):
    fine = Mesh(mesh.devices.reshape(2, 4, 2, 4, 2), ("xh", "z", "xl", "y", "c"))
    spec = P(("xh", "z"), ("xl", "y", "c"), None)
    return jax.shard_map(
        local,
        mesh=fine,
        in_specs=(spec, spec) + (P(),) * 10,
        out_specs=(spec, spec),
        check_vma=False,
    )
```

```python
import math

import jax
import jax.numpy as jnp
from jax import lax
from jax.experimental import pallas as pl
from jax.experimental.pallas import tpu as pltpu
from jax.sharding import Mesh
from jax.sharding import PartitionSpec as P

F32 = jnp.float32
BF16 = jnp.bfloat16
D = 768
HEADS = 12
HEAD_DIM = 64
SEQ = ("xh", "z")
GRP = ("xl", "c")
WIDE = ("xh", "z", "xl", "c")
ALLRES = ("y", "xl", "c")
NS, NG, NY = 8, 4, 4
GH = HEADS // NG
S = 4
R = 48
I = R * NG
CR = 6
CP = 8
TOK = NS * S * CP
ROWS = GH * I // NS
SENT = S * CR
BLOCK = ROWS + 2 * SENT
WIDTH = GH * S * HEAD_DIM
ROW_SCALE = 1.0 / math.sqrt(HEAD_DIM * 32)
COL_SCALE = 1.0 / math.sqrt(HEAD_DIM)


def dot(a, b):
    return lax.dot_general(a, b, (((1,), (0,)), ((), ())), preferred_element_type=F32)


def dot_nt(a, b):
    return lax.dot_general(a, b, (((1,), (1,)), ((), ())), preferred_element_type=F32)


def dot_tn(a, b):
    return lax.dot_general(a, b, (((0,), (0,)), ((), ())), preferred_element_type=F32)


def call(kernel, outs, *args, mem=16, scratch=(), far=(), sems=0, cost=None):
    scratch = list(scratch)
    if sems:
        scratch.append(pltpu.SemaphoreType.DMA((sems,)))
    args = [
        pltpu.with_memory_space_constraint(a, pltpu.HBM) if i in far else a
        for i, a in enumerate(args)
    ]
    shapes = [jax.ShapeDtypeStruct(*o) if isinstance(o, tuple) else o for o in outs]
    spaces = [pltpu.VMEM if isinstance(o, tuple) else o.memory_space for o in outs]
    res = pl.pallas_call(
        kernel,
        out_shape=shapes,
        in_specs=[
            pl.BlockSpec(memory_space=pltpu.HBM if i in far else pltpu.VMEM)
            for i in range(len(args))
        ],
        out_specs=[pl.BlockSpec(memory_space=m) for m in spaces],
        scratch_shapes=scratch,
        cost_estimate=cost,
        compiler_params=pltpu.CompilerParams(vmem_limit_bytes=mem * 2**20),
    )(*args)
    return res[0] if len(outs) == 1 else res


def fetch(sources, targets, sems, wait_only=False, cuts=1):
    reads, at = [], 0
    for src, dst in zip(sources, targets):
        copies = []
        parts = cuts if src.shape[0] == D and len(src.shape) == 2 else 1
        for n in range(parts):
            rows = slice(n * D // parts, (n + 1) * D // parts)
            a, b = (src.at[rows], dst.at[rows]) if parts > 1 else (src, dst)
            copies.append(pltpu.make_async_copy(a, b, sems.at[at]))
            at += 1
        for c in copies:
            c.start()

        def read(copies=copies, dst=dst):
            for c in copies:
                c.wait()
            copies.clear()
            return None if wait_only else dst[...]

        reads.append(read)
    return reads


class Pushes:
    def __init__(self, sems, first=0):
        self.sems, self.first, self.begun = sems, first, []

    def start(self, src, dst):
        c = pltpu.make_async_copy(src, dst, self.sems.at[self.first + len(self.begun)])
        c.start()
        self.begun.append(c)

    def finish(self):
        for c in self.begun:
            c.wait()


def my_group():
    return lax.axis_index("xl") * 2 + lax.axis_index("c")


def halves(a, b, half_a, half_b):
    low = lax.broadcasted_iota(jnp.int32, a.shape, 1) < 64
    a = a if half_a == 0 else pltpu.roll(a, 64, 1)
    b = b if half_b == 1 else pltpu.roll(b, 64, 1)
    return jnp.where(low, a, b)


def blk(v, n):
    return v[:, n * 128 : (n + 1) * 128]


def to_column():
    row = lax.broadcasted_iota(jnp.int32, (S * R, S * R), 0)
    col = lax.broadcasted_iota(jnp.int32, (S * R, S * R), 1)
    want = ((row // CR) % S) * R + (row // (CR * S)) * CR + row % CR
    return jnp.where(col == want, 1.0, 0.0).astype(BF16)


def to_padded():
    row = lax.broadcasted_iota(jnp.int32, (TOK, S * R), 0)
    col = lax.broadcasted_iota(jnp.int32, (TOK, S * R), 1)
    r = row % CP
    return jnp.where((r < CR) & (col == (row // CP) * CR + r), 1.0, 0.0).astype(BF16)


def to_wide():
    row = lax.broadcasted_iota(jnp.int32, (TOK, I), 0)
    col = lax.broadcasted_iota(jnp.int32, (TOK, I), 1)
    r = row % CP
    want = ((row // CP) % NG) * R + (row // (CP * NG)) * CR + r
    return jnp.where((r < CR) & (col == want), 1.0, 0.0).astype(BF16)


def moments(v):
    mean = jnp.mean(v, axis=-1, keepdims=True)
    centred = v - mean
    r = lax.rsqrt(jnp.mean(centred * centred, axis=-1, keepdims=True) + 1e-05)
    return centred * r, r


def norm_grad(grad, gain, hat, r):
    g = grad * gain
    return r * (
        g - jnp.mean(g, axis=-1, keepdims=True) - hat * jnp.mean(g * hat, axis=-1, keepdims=True)
    )


def pieces(y, put, after=None):
    for g in range(NG):
        for h in range(GH):
            n = g * GH + h
            src = blk(y, n // 2)
            for sp in range(2):
                a = src[2 * sp * R : (2 * sp + 1) * R]
                b = src[(2 * sp + 1) * R : (2 * sp + 2) * R]
                put(g, h * 256 + sp * 128, halves(a, b, n % 2, n % 2).astype(BF16))
        if after is not None:
            after(g)


def normed_input(x, gain):
    hat, _ = moments(x.astype(F32).reshape(S * R, D))
    return (hat * gain.reshape(1, D)).astype(BF16)


def k_keys(x, gain, w, keys, x_s, g_s, w_s, keys_s, sems):
    x, gain, w = fetch((x, gain, w), (x_s, g_s, w_s), sems, cuts=4)
    push = Pushes(sems, 6)
    normed = normed_input(x(), gain())

    def put(g, at, piece):
        keys_s[g, :, at : at + 128] = piece

    def after(g):
        for yy in range(NY):
            push.start(keys_s.at[g], keys.at[yy * NG + g])

    pieces(dot(normed, w()), put, after)
    push.finish()


def k_queries_values(x, gain, wq, wv, qv0, qv1, qv2, qv3, x_s, g_s, wq_s, wv_s, qv, sems):
    x, gain, wq, wv = fetch((x, gain, wq, wv), (x_s, g_s, wq_s, wv_s), sems)
    normed = normed_input(x(), gain())
    for first, w in ((0, wq), (WIDTH, wv)):

        def put(g, at, piece, first=first):
            qv[g, :, first + at : first + at + 128] = piece

        pieces(dot(normed, w()), put)
    me = my_group()
    for k, out in enumerate((qv0, qv1, qv2, qv3)):
        out[...] = qv[me ^ k]


def rows_out(out, out_s, products, first, second, push):
    done = []
    for a in range(NS):
        while len(done) * I < (a + 1) * ROWS:
            done.append(products(len(done)))
        head = a * ROWS // I
        rows = jnp.concatenate(done[head:], axis=0)
        lo = a * ROWS - head * I
        t = slice(a * SENT, (a + 1) * SENT)
        rows = jnp.concatenate((rows[lo : lo + ROWS], first[t], second[t]), axis=0)
        out_s[a] = rows.astype(BF16)
        push.start(out_s.at[a], out.at[a])


def rows_in(parts):
    got = [parts[a].astype(F32) for a in range(NS)]
    first = jnp.concatenate([t[ROWS : ROWS + SENT] for t in got], axis=0)
    second = jnp.concatenate([t[ROWS + SENT :] for t in got], axis=0)
    return first, second


def k_logits(
    qv0, qv1, qv2, qv3, keys, x, cot, out, queries, values, out_s, q_s, v_s, sems
):
    push = Pushes(sems)
    me = my_group()
    for k, qv in enumerate((qv0, qv1, qv2, qv3)):
        q_s[me ^ k] = qv[:, 0:WIDTH]
        v_s[me ^ k] = qv[:, WIDTH : 2 * WIDTH]
    push.start(q_s, queries)
    push.start(v_s, values)
    perm = to_column()
    first = dot(perm, x[...].astype(F32).reshape(S * R, D).astype(BF16))
    second = dot(perm, cot[...].astype(F32).reshape(S * R, D).astype(BF16))

    def products(h):
        c = slice(h * 256, (h + 1) * 256)
        return dot_nt(q_s[:, :, c].reshape(I, 256), keys[:, c])

    rows_out(out, out_s, products, first, second, push)
    push.finish()


def summed(parts):
    total = parts[0].astype(F32)
    for a in range(1, NS):
        total = total + parts[a].astype(F32)
    return total[:ROWS]


def k_softmax(parts, values, probs, weights, p_s, sems):
    push = Pushes(sems)
    logits = summed(parts) * ROW_SCALE
    e = jnp.exp(logits - jnp.max(logits, axis=-1, keepdims=True))
    p = e * (1.0 / jnp.sum(e, axis=-1, keepdims=True))
    p_s[...] = p
    push.start(p_s, probs)
    w = p.astype(BF16)
    for a in range(NS):
        weights[a] = w
    push.finish()


def k_gather(v0, v1, v2, v3, out, values, sems):
    me = lax.axis_index("y")
    (own,) = fetch((v0,), (values.at[me],), sems, wait_only=True)
    push = Pushes(sems, 1)
    for k, v in enumerate((v1, v2, v3)):
        values[me ^ (k + 1)] = v[...]
    own()
    push.start(values, out)
    push.finish()


def k_attend(weights, values, out):
    perm = to_wide()
    for h in range(GH):
        c = slice(h * 256, (h + 1) * 256)
        v = values[:, :, c].reshape(NY * I, 256)
        att = dot(weights[h * I : (h + 1) * I], v).astype(BF16)
        out[:, c] = dot(perm, att).astype(BF16)


def k_column(
    att_in, sent, gain, out_row, wq, wk, wv, out_col, back, grad_out,
    wk_s, wv_s, oc_s, att_s, gq_s, gk_s, gv_s, sems,
):
    wk, wv, out_col = fetch((wk, wv, out_col), (wk_s, wv_s, oc_s), sems, cuts=2)
    raw = att_in[...].astype(F32).reshape(NS, NG, CP, WIDTH)
    groups = [raw[:, g].reshape(NS * CP, WIDTH) for g in range(NG)]
    per_seq = []
    for s in range(S):
        cols = []
        for fb in range(6):
            pair = []
            for n in (2 * fb, 2 * fb + 1):
                pair.append(blk(groups[n // GH], (n % GH) * 2 + s // 2))
            cols.append(halves(pair[0], pair[1], s % 2, s % 2))
        per_seq.append(jnp.concatenate(cols, axis=1).reshape(NS, 1, CP, D))
    att_row = jnp.concatenate(per_seq, axis=1).reshape(TOK, D).astype(BF16)
    pad = to_padded()
    att_row = dot_tn(pad, att_row).astype(BF16)
    xc, cot = rows_in(sent)
    cot = cot.astype(BF16)
    middle = (xc + dot(att_row, out_row[...])).astype(BF16)
    mid = middle.astype(F32)
    hat, r = moments(mid)
    normed = (hat * gain[...].reshape(1, D)).astype(BF16)
    q = dot(normed, wq[...]).astype(BF16) * jnp.asarray(COL_SCALE, BF16)
    k = dot(normed, wk()).astype(BF16)
    v = dot(normed, wv()).astype(BF16)
    ga = dot_nt(cot, out_col()).astype(BF16)
    row = lax.broadcasted_iota(jnp.int32, (2 * S * R, 1), 0)
    col = lax.broadcasted_iota(jnp.int32, (1, S * R), 1)
    same = (row % CR) == (col % CR)
    low = lax.broadcasted_iota(jnp.int32, (1, 128), 1) < 64
    masks = [jnp.where(low == first, 1.0, 0.0).astype(BF16) for first in (True, False)]

    def stack(t):
        return jnp.concatenate([t * masks[0], t * masks[1]], axis=0)

    def unstack(t):
        return jnp.where(low, t[: S * R], t[S * R :])

    for fb in range(6):
        at = slice(fb * 128, (fb + 1) * 128)
        kb, vb = blk(k, fb), blk(v, fb)
        qs, gs = stack(blk(q, fb)), stack(blk(ga, fb))
        logits = jnp.where(same, dot_nt(qs, kb), -1e30)
        e = jnp.exp(logits - jnp.max(logits, axis=-1, keepdims=True))
        p = e * (1.0 / jnp.sum(e, axis=-1, keepdims=True))
        w = p.astype(BF16)
        grads = dot_nt(gs, vb)
        dl = (p * (grads - jnp.sum(p * grads, axis=-1, keepdims=True))).astype(BF16)
        att_s[:, at] = unstack(dot(w, vb)).astype(BF16)
        gq_s[:, at] = (unstack(dot(dl, kb)) * COL_SCALE).astype(BF16)
        gk_s[:, at] = dot_tn(dl, qs).astype(BF16)
        gv_s[:, at] = dot_tn(w, gs).astype(BF16)
    back[:, 0:D] = (mid + dot(att_s[...], out_col())).astype(BF16)
    gn = (
        dot_nt(gq_s[...], wq[...]) + dot_nt(gk_s[...], wk()) + dot_nt(gv_s[...], wv())
    )
    gmid = (cot.astype(F32) + norm_grad(gn, gain[...].reshape(1, D), hat, r)).astype(BF16)
    back[:, D : 2 * D] = gmid
    gra = dot_nt(gmid, out_row[...]).astype(BF16)
    gra = dot(pad, gra).reshape(NS, S, CP, D)
    seqs = [gra[:, s].reshape(NS * CP, D) for s in range(S)]
    per_group = []
    for g in range(NG):
        cols = []
        for h in range(GH):
            n = g * GH + h
            for sp in range(2):
                cols.append(
                    halves(blk(seqs[2 * sp], n // 2), blk(seqs[2 * sp + 1], n // 2), n % 2, n % 2)
                )
        per_group.append(jnp.concatenate(cols, axis=1).reshape(NS, 1, CP, WIDTH))
    grad_out[...] = jnp.concatenate(per_group, axis=1).reshape(TOK, WIDTH).astype(BF16)


def k_grad_probs(grads, values, back, gra, out, gra_s, out_s, sems):
    push = Pushes(sems)
    perm = to_wide()
    for h in range(GH):
        c = slice(h * 256, (h + 1) * 256)
        gra_s[:, c] = dot_tn(perm, grads[:, c]).astype(BF16)
    push.start(gra_s, gra)
    first, second = back[:, 0:D].astype(F32), back[:, D : 2 * D].astype(F32)

    def products(h):
        c = slice(h * 256, (h + 1) * 256)
        return dot_nt(gra_s[:, c], values[:, :, c].reshape(NY * I, 256))

    rows_out(out, out_s, products, first, second, push)
    push.finish()


def k_grad_values(weights, gra, gv0, gv1, gv2, gv3, gv, sems):
    for h in range(GH):
        c = slice(h * 256, (h + 1) * 256)
        t = dot_tn(weights[h * I : (h + 1) * I], gra[:, c]).astype(BF16)
        gv[:, :, c] = t.reshape(NY, I, 256)
    me = lax.axis_index("y")
    push = Pushes(sems)
    push.start(gv.at[me], gv0)
    for k, out in enumerate((gv1, gv2, gv3)):
        out[...] = gv[me ^ (k + 1)]
    push.finish()


def k_sum_values(gv0, gv1, gv3, gv, g_s, gv_s, sems):
    (gv0,) = fetch((gv0,), (g_s,), sems)
    push = Pushes(sems, 1)
    total = gv1[...].astype(F32) + gv3[...].astype(F32)
    gv_s[...] = total + gv0().astype(F32)
    push.start(gv_s, gv)
    push.finish()


def k_softmax_grad(parts, probs, gv, out, p_s, out_s, sems):
    (probs,) = fetch((probs,), (p_s,), sems)
    push = Pushes(sems, 1)
    grads = summed(parts)
    p = probs()
    dl = p * (grads - jnp.sum(p * grads, axis=-1, keepdims=True)) * ROW_SCALE
    out_s[...] = dl.astype(BF16)
    for a in range(NS):
        push.start(out_s, out.at[a])
    push.finish()


def k_grad_keys(dl, queries, before, gk, dl_s, q_s, gk_s, sems):
    heads = [slice(h * I, (h + 1) * I) for h in range(GH)]
    queries, *dl = fetch(
        [queries] + [dl.at[c] for c in heads], [q_s] + [dl_s.at[c] for c in heads], sems
    )
    push = Pushes(sems, GH + 1)
    queries = queries()
    for h in range(GH):
        c = slice(h * 256, (h + 1) * 256)
        gk_s[:, c] = dot_tn(dl[h](), queries[:, c]).astype(BF16)
        for r in (slice(0, D // 2), slice(D // 2, D)):
            push.start(gk_s.at[r, c], gk.at[r, c])
    push.finish()


def k_grad_queries(
    dl, keys, gv, gv2, gqv0, gqv1, gqv2, gqv3,
    dl_s, sum_s, two_s, gv_s, gq_s, o0, o1, o2, o3, sems,
):
    heads = [slice(h * I, (h + 1) * I) for h in range(GH)]
    *dl, gv, gv2 = fetch(
        [dl.at[c] for c in heads] + [gv, gv2],
        [dl_s.at[c] for c in heads] + [sum_s, two_s],
        sems,
    )
    push = Pushes(sems, GH + 2)
    for h in range(GH):
        c = slice(h * 256, (h + 1) * 256)
        gq_s[:, :, c] = dot(dl[h](), keys[:, c]).astype(BF16).reshape(NG, R, 256)
    gv_s[...] = (gv() + gv2().astype(F32)).astype(BF16).reshape(NG, R, WIDTH)
    me = my_group()
    for k, (held, out) in enumerate(zip((o0, o1, o2, o3), (gqv0, gqv1, gqv2, gqv3))):
        held[:, 0:WIDTH] = gq_s[me ^ k]
        held[:, WIDTH : 2 * WIDTH] = gv_s[me ^ k]
        push.start(held, out)
    push.finish()


def k_block_out(sent, out):
    first, _ = rows_in(sent)
    out[...] = dot_tn(to_column(), first.astype(BF16)).reshape(S, R, D).astype(BF16)


def token_rows(groups):
    rows = []
    for s in range(S):
        cols = []
        for fb in range(6):
            pair = []
            for n in (2 * fb, 2 * fb + 1):
                pair.append(blk(groups[n // GH], (n % GH) * 2 + s // 2))
            cols.append(halves(pair[0], pair[1], s % 2, s % 2))
        rows.append(jnp.concatenate(cols, axis=1))
    return jnp.concatenate(rows, axis=0).astype(BF16)


def k_finish_keys(gk, wk, out, gk_s, wk_s, out_s, sems):
    gk, wk = fetch((gk, wk), (gk_s, wk_s), sems, cuts=3)
    push = Pushes(sems, 6)
    gk()
    groups = []
    for g in range(NG):
        t = gk_s[g * R : (g + 1) * R].astype(F32)
        for yy in range(1, NY):
            lo = (yy * NG + g) * R
            t = t + gk_s[lo : lo + R].astype(F32)
        groups.append(t)
    out_s[...] = dot_nt(token_rows(groups), wk())
    push.start(out_s, out)
    push.finish()


def k_finish(
    gqv0, gqv1, gqv2, gqv3, part, x, sent, gain, wq, wv, input_grad,
    gqv, own_s, part_s, sems,
):
    gqv0, part = fetch((gqv0, part), (own_s, part_s), sems)
    me = my_group()
    for k, got in enumerate((gqv1, gqv2, gqv3)):
        gqv[me ^ (k + 1)] = got[...]
    perm = to_column()
    _, second = rows_in(sent)
    gmid = dot_tn(perm, second.astype(BF16))
    hat, r = moments(x[...].astype(F32).reshape(S * R, D))
    gqv[me] = gqv0()
    total = None
    for first, w in ((0, wq), (WIDTH, wv)):
        groups = [gqv[g, :, first : first + WIDTH].astype(F32) for g in range(NG)]
        t = dot_nt(token_rows(groups), w[...])
        total = t if total is None else total + t
    total = total + part()
    grad = gmid + norm_grad(total, gain[...].reshape(1, D), hat, r)
    input_grad[...] = grad.reshape(S, R, D).astype(BF16)


def swap(x, axes):
    return lax.all_to_all(x, axes, split_axis=0, concat_axis=0, tiled=True)


def spread(parts, axes):
    n = len(parts)
    pairs = [[(i, i ^ k) for i in range(n)] for k in range(n)]
    return [parts[0]] + [lax.ppermute(parts[k], axes, pairs[k]) for k in range(1, n)]


def local(
    x,
    cot,
    gain_row,
    query_row,
    key_row,
    value_row,
    out_row,
    gain_col,
    query_col,
    key_col,
    value_col,
    out_col,
):
    piece = ((R, 2 * WIDTH), BF16)
    block = ((NS, BLOCK, NY * I), BF16)
    part = ((NG, R, WIDTH), BF16)
    weight = pltpu.VMEM((D, D), BF16)
    row = pltpu.VMEM((S, R, D), BF16)
    gain = pltpu.VMEM((D,), F32)
    keys = call(
        k_keys,
        [pltpu.HBM((NY * NG, R, WIDTH), BF16)],
        x, gain_row, key_row,
        far=(0, 1, 2),
        sems=6 + NY * NG,
        scratch=[row, gain, weight, pltpu.VMEM(*part)],
    )
    qv = call(
        k_queries_values,
        [piece] * NG,
        x, gain_row, query_row, value_row,
        far=(0, 1, 2, 3),
        sems=4,
        scratch=[row, gain, weight, weight, pltpu.VMEM((NG, R, 2 * WIDTH), BF16)],
    )
    qv = spread(qv, GRP)
    keys = swap(keys, ALLRES).reshape(NY * I, WIDTH)
    parts, queries, values = call(
        k_logits,
        [pltpu.HBM(*block), pltpu.HBM(*part), pltpu.HBM(*part)],
        *qv, keys, x, cot,
        sems=2 + NS,
        scratch=[pltpu.VMEM(*block), pltpu.VMEM(*part), pltpu.VMEM(*part)],
    )
    queries = queries.reshape(I, WIDTH)
    parts = swap(parts, SEQ)
    values = spread([values.reshape(I, WIDTH)] * NY, "y")
    gathered = pltpu.VMEM((NY, I, WIDTH), BF16)
    values = call(
        k_gather,
        [pltpu.HBM((NY, I, WIDTH), BF16)],
        *values,
        far=(0,),
        sems=2,
        scratch=[gathered],
    )
    probs, weights = call(
        k_softmax,
        [pltpu.HBM((ROWS, NY * I), F32), ((NS, ROWS, NY * I), BF16)],
        parts, values,
        far=(1,),
        sems=1,
        scratch=[pltpu.VMEM((ROWS, NY * I), F32)],
    )
    weights = swap(weights, SEQ).reshape(GH * I, NY * I)
    att = call(k_attend, [((TOK, WIDTH), BF16)], weights, values)
    att = swap(att, WIDE)
    back, grads = call(
        k_column,
        [((S * R, 2 * D), BF16), ((TOK, WIDTH), BF16)],
        att, parts, gain_col, out_row, query_col, key_col, value_col, out_col,
        mem=32,
        far=(5, 6, 7),
        sems=6,
        scratch=[weight] * 3 + [pltpu.VMEM((S * R, D), BF16)] * 4,
    )
    grads = swap(grads, WIDE)
    gra, gparts = call(
        k_grad_probs,
        [pltpu.HBM((I, WIDTH), BF16), pltpu.HBM(*block)],
        grads, values, back,
        sems=1 + NS,
        scratch=[pltpu.VMEM((I, WIDTH), BF16), pltpu.VMEM(*block)],
    )
    gparts = swap(gparts, SEQ)
    gv = call(
        k_grad_values,
        [pltpu.HBM((I, WIDTH), BF16)] + [((I, WIDTH), BF16)] * (NY - 1),
        weights, gra,
        sems=1,
        scratch=[gathered],
    )
    gv = spread(gv, "y")
    summand = pltpu.VMEM((I, WIDTH), BF16)
    sum_s = pltpu.VMEM((I, WIDTH), F32)
    some = call(
        k_sum_values,
        [pltpu.HBM((I, WIDTH), F32)],
        gv[0], gv[1], gv[3],
        far=(0,),
        sems=2,
        scratch=[summand, sum_s],
    )
    dl = call(
        k_softmax_grad,
        [pltpu.HBM((NS, ROWS, NY * I), BF16)],
        gparts, probs, some,
        far=(1, 2),
        sems=1 + NS,
        scratch=[pltpu.VMEM((ROWS, NY * I), F32), pltpu.VMEM((ROWS, NY * I), BF16)],
    )
    dl = swap(dl, SEQ).reshape(GH * I, NY * I)
    dl_s = pltpu.VMEM((GH * I, NY * I), BF16)
    gk = call(
        k_grad_keys,
        [pltpu.HBM((D, D), BF16)],
        dl, queries, gv[2],
        far=(0, 1, 2),
        sems=3 * GH + 1,
        scratch=[dl_s, summand, weight],
    )
    gqv = call(
        k_grad_queries,
        [pltpu.HBM(*piece)] * NG,
        dl, keys, some, gv[2],
        far=(0, 2, 3),
        sems=GH + 2 + NG,
        scratch=[dl_s, sum_s, summand, pltpu.VMEM(*part), pltpu.VMEM(*part)] + [pltpu.VMEM(*piece)] * NG,
    )
    gqv = spread(gqv, GRP)
    gk = swap(gk, ALLRES).reshape(NY * I, WIDTH)
    block_out = call(k_block_out, [((S, R, D), BF16)], gparts)
    total = pltpu.VMEM((S * R, D), F32)
    from_keys = call(
        k_finish_keys,
        [pltpu.HBM((S * R, D), F32)],
        gk, key_row,
        cost=pl.CostEstimate(flops=4 * 10**9, bytes_accessed=3 * 10**6, transcendentals=0),
        far=(0, 1),
        sems=7,
        scratch=[weight, weight, total],
    )
    input_grad = call(
        k_finish,
        [((S, R, D), BF16)],
        *gqv, from_keys, x, gparts, gain_row, query_row, value_row,
        far=(0, 4),
        sems=2,
        scratch=[
            pltpu.VMEM((NG, R, 2 * WIDTH), BF16),
            pltpu.VMEM(*piece),
            total,
        ],
    )
    return block_out, input_grad


def solution(mesh):
    fine = Mesh(mesh.devices.reshape(2, 4, 2, 4, 2), ("xh", "z", "xl", "y", "c"))
    spec = P(("xh", "z"), ("xl", "y", "c"), None)
    return jax.shard_map(
        local,
        mesh=fine,
        in_specs=(spec, spec) + (P(),) * 10,
        out_specs=(spec, spec),
        check_vma=False,
    )
```

```python
import math

import jax
import jax.numpy as jnp
from jax import lax
from jax.experimental import pallas as pl
from jax.experimental.pallas import tpu as pltpu
from jax.sharding import Mesh
from jax.sharding import PartitionSpec as P

F32 = jnp.float32
BF16 = jnp.bfloat16
D = 768
HEADS = 12
HEAD_DIM = 64
SEQ = ("xh", "z")
GRP = ("xl", "c")
WIDE = ("xh", "z", "xl", "c")
ALLRES = ("y", "xl", "c")
NS, NG, NY = 8, 4, 4
GH = HEADS // NG
S = 4
R = 48
I = R * NG
CR = 6
CP = 8
TOK = NS * S * CP
ROWS = GH * I // NS
SENT = S * CR
BLOCK = ROWS + 2 * SENT
WIDTH = GH * S * HEAD_DIM
ROW_SCALE = 1.0 / math.sqrt(HEAD_DIM * 32)
COL_SCALE = 1.0 / math.sqrt(HEAD_DIM)


def dot(a, b):
    return lax.dot_general(a, b, (((1,), (0,)), ((), ())), preferred_element_type=F32)


def dot_nt(a, b):
    return lax.dot_general(a, b, (((1,), (1,)), ((), ())), preferred_element_type=F32)


def dot_tn(a, b):
    return lax.dot_general(a, b, (((0,), (0,)), ((), ())), preferred_element_type=F32)


def call(kernel, outs, *args, mem=16, scratch=(), far=(), sems=0, cost=None):
    scratch = list(scratch)
    if sems:
        scratch.append(pltpu.SemaphoreType.DMA((sems,)))
    args = [
        pltpu.with_memory_space_constraint(a, pltpu.HBM) if i in far else a
        for i, a in enumerate(args)
    ]
    shapes = [jax.ShapeDtypeStruct(*o) if isinstance(o, tuple) else o for o in outs]
    spaces = [pltpu.VMEM if isinstance(o, tuple) else o.memory_space for o in outs]
    res = pl.pallas_call(
        kernel,
        out_shape=shapes,
        in_specs=[
            pl.BlockSpec(memory_space=pltpu.HBM if i in far else pltpu.VMEM)
            for i in range(len(args))
        ],
        out_specs=[pl.BlockSpec(memory_space=m) for m in spaces],
        scratch_shapes=scratch,
        cost_estimate=cost,
        compiler_params=pltpu.CompilerParams(vmem_limit_bytes=mem * 2**20),
    )(*args)
    return res[0] if len(outs) == 1 else res


def fetch(sources, targets, sems, wait_only=False, cuts=1):
    reads, at = [], 0
    for src, dst in zip(sources, targets):
        copies = []
        parts = cuts if src.shape[0] == D and len(src.shape) == 2 else 1
        for n in range(parts):
            rows = slice(n * D // parts, (n + 1) * D // parts)
            a, b = (src.at[rows], dst.at[rows]) if parts > 1 else (src, dst)
            copies.append(pltpu.make_async_copy(a, b, sems.at[at]))
            at += 1
        for c in copies:
            c.start()

        def read(copies=copies, dst=dst):
            for c in copies:
                c.wait()
            copies.clear()
            return None if wait_only else dst[...]

        reads.append(read)
    return reads


class Pushes:
    def __init__(self, sems, first=0):
        self.sems, self.first, self.begun = sems, first, []

    def start(self, src, dst):
        c = pltpu.make_async_copy(src, dst, self.sems.at[self.first + len(self.begun)])
        c.start()
        self.begun.append(c)

    def finish(self):
        for c in self.begun:
            c.wait()


def my_group():
    return lax.axis_index("xl") * 2 + lax.axis_index("c")


def halves(a, b, half_a, half_b):
    low = lax.broadcasted_iota(jnp.int32, a.shape, 1) < 64
    a = a if half_a == 0 else pltpu.roll(a, 64, 1)
    b = b if half_b == 1 else pltpu.roll(b, 64, 1)
    return jnp.where(low, a, b)


def blk(v, n):
    return v[:, n * 128 : (n + 1) * 128]


def to_column():
    row = lax.broadcasted_iota(jnp.int32, (S * R, S * R), 0)
    col = lax.broadcasted_iota(jnp.int32, (S * R, S * R), 1)
    want = ((row // CR) % S) * R + (row // (CR * S)) * CR + row % CR
    return jnp.where(col == want, 1.0, 0.0).astype(BF16)


def to_padded():
    row = lax.broadcasted_iota(jnp.int32, (TOK, S * R), 0)
    col = lax.broadcasted_iota(jnp.int32, (TOK, S * R), 1)
    r = row % CP
    return jnp.where((r < CR) & (col == (row // CP) * CR + r), 1.0, 0.0).astype(BF16)


def to_wide():
    row = lax.broadcasted_iota(jnp.int32, (TOK, I), 0)
    col = lax.broadcasted_iota(jnp.int32, (TOK, I), 1)
    r = row % CP
    want = ((row // CP) % NG) * R + (row // (CP * NG)) * CR + r
    return jnp.where((r < CR) & (col == want), 1.0, 0.0).astype(BF16)


def moments(v):
    mean = jnp.mean(v, axis=-1, keepdims=True)
    centred = v - mean
    r = lax.rsqrt(jnp.mean(centred * centred, axis=-1, keepdims=True) + 1e-05)
    return centred * r, r


def norm_grad(grad, gain, hat, r):
    g = grad * gain
    return r * (
        g - jnp.mean(g, axis=-1, keepdims=True) - hat * jnp.mean(g * hat, axis=-1, keepdims=True)
    )


def pieces(y, put, after=None):
    for g in range(NG):
        for h in range(GH):
            n = g * GH + h
            src = blk(y, n // 2)
            for sp in range(2):
                a = src[2 * sp * R : (2 * sp + 1) * R]
                b = src[(2 * sp + 1) * R : (2 * sp + 2) * R]
                put(g, h * 256 + sp * 128, halves(a, b, n % 2, n % 2).astype(BF16))
        if after is not None:
            after(g)


def normed_input(x, gain):
    hat, _ = moments(x.astype(F32).reshape(S * R, D))
    return (hat * gain.reshape(1, D)).astype(BF16)


def k_keys(x, gain, w, keys, x_s, g_s, w_s, keys_s, sems):
    x, gain, w = fetch((x, gain, w), (x_s, g_s, w_s), sems, cuts=4)
    push = Pushes(sems, 6)
    normed = normed_input(x(), gain())

    def put(g, at, piece):
        keys_s[g, :, at : at + 128] = piece

    def after(g):
        for yy in range(NY):
            push.start(keys_s.at[g], keys.at[yy * NG + g])

    pieces(dot(normed, w()), put, after)
    push.finish()


def k_queries_values(x, gain, wq, wv, qv0, qv1, qv2, qv3, x_s, g_s, wq_s, wv_s, qv, sems):
    x, gain, wq, wv = fetch((x, gain, wq, wv), (x_s, g_s, wq_s, wv_s), sems)
    normed = normed_input(x(), gain())
    for first, w in ((0, wq), (WIDTH, wv)):

        def put(g, at, piece, first=first):
            qv[g, :, first + at : first + at + 128] = piece

        pieces(dot(normed, w()), put)
    me = my_group()
    for k, out in enumerate((qv0, qv1, qv2, qv3)):
        out[...] = qv[me ^ k]


def rows_out(out, out_s, products, first, second, push):
    done = []
    for a in range(NS):
        while len(done) * I < (a + 1) * ROWS:
            done.append(products(len(done)))
        head = a * ROWS // I
        rows = jnp.concatenate(done[head:], axis=0)
        lo = a * ROWS - head * I
        t = slice(a * SENT, (a + 1) * SENT)
        rows = jnp.concatenate((rows[lo : lo + ROWS], first[t], second[t]), axis=0)
        out_s[a] = rows.astype(BF16)
        push.start(out_s.at[a], out.at[a])


def rows_in(parts):
    got = [parts[a].astype(F32) for a in range(NS)]
    first = jnp.concatenate([t[ROWS : ROWS + SENT] for t in got], axis=0)
    second = jnp.concatenate([t[ROWS + SENT :] for t in got], axis=0)
    return first, second


def k_logits(
    qv0, qv1, qv2, qv3, keys, x, cot, out, queries, values, out_s, q_s, v_s, sems
):
    push = Pushes(sems)
    me = my_group()
    for k, qv in enumerate((qv0, qv1, qv2, qv3)):
        q_s[me ^ k] = qv[:, 0:WIDTH]
        v_s[me ^ k] = qv[:, WIDTH : 2 * WIDTH]
    push.start(q_s, queries)
    push.start(v_s, values)
    perm = to_column()
    first = dot(perm, x[...].astype(F32).reshape(S * R, D).astype(BF16))
    second = dot(perm, cot[...].astype(F32).reshape(S * R, D).astype(BF16))

    def products(h):
        c = slice(h * 256, (h + 1) * 256)
        return dot_nt(q_s[:, :, c].reshape(I, 256), keys[:, c])

    rows_out(out, out_s, products, first, second, push)
    push.finish()


def summed(parts):
    total = parts[0].astype(F32)
    for a in range(1, NS):
        total = total + parts[a].astype(F32)
    return total[:ROWS]


def k_softmax(parts, values, probs, weights, p_s, sems):
    push = Pushes(sems)
    logits = summed(parts) * ROW_SCALE
    e = jnp.exp(logits - jnp.max(logits, axis=-1, keepdims=True))
    p = e * (1.0 / jnp.sum(e, axis=-1, keepdims=True))
    p_s[...] = p
    push.start(p_s, probs)
    w = p.astype(BF16)
    for a in range(NS):
        weights[a] = w
    push.finish()


def k_gather(v0, v1, v2, v3, out, values, sems):
    me = lax.axis_index("y")
    (own,) = fetch((v0,), (values.at[me],), sems, wait_only=True)
    push = Pushes(sems, 1)
    for k, v in enumerate((v1, v2, v3)):
        values[me ^ (k + 1)] = v[...]
    own()
    push.start(values, out)
    push.finish()


def k_attend(weights, values, out):
    perm = to_wide()
    for h in range(GH):
        c = slice(h * 256, (h + 1) * 256)
        v = values[:, :, c].reshape(NY * I, 256)
        att = dot(weights[h * I : (h + 1) * I], v).astype(BF16)
        out[:, c] = dot(perm, att).astype(BF16)


def k_column(
    att_in, sent, gain, out_row, wq, wk, wv, out_col, back, grad_out,
    wk_s, wv_s, oc_s, att_s, gq_s, gk_s, gv_s, sems,
):
    wk, wv, out_col = fetch((wk, wv, out_col), (wk_s, wv_s, oc_s), sems, cuts=2)
    raw = att_in[...].astype(F32).reshape(NS, NG, CP, WIDTH)
    groups = [raw[:, g].reshape(NS * CP, WIDTH) for g in range(NG)]
    per_seq = []
    for s in range(S):
        cols = []
        for fb in range(6):
            pair = []
            for n in (2 * fb, 2 * fb + 1):
                pair.append(blk(groups[n // GH], (n % GH) * 2 + s // 2))
            cols.append(halves(pair[0], pair[1], s % 2, s % 2))
        per_seq.append(jnp.concatenate(cols, axis=1).reshape(NS, 1, CP, D))
    att_row = jnp.concatenate(per_seq, axis=1).reshape(TOK, D).astype(BF16)
    pad = to_padded()
    att_row = dot_tn(pad, att_row).astype(BF16)
    xc, cot = rows_in(sent)
    cot = cot.astype(BF16)
    middle = (xc + dot(att_row, out_row[...])).astype(BF16)
    mid = middle.astype(F32)
    hat, r = moments(mid)
    normed = (hat * gain[...].reshape(1, D)).astype(BF16)
    q = dot(normed, wq[...]).astype(BF16) * jnp.asarray(COL_SCALE, BF16)
    k = dot(normed, wk()).astype(BF16)
    v = dot(normed, wv()).astype(BF16)
    ga = dot_nt(cot, out_col()).astype(BF16)
    row = lax.broadcasted_iota(jnp.int32, (2 * S * R, 1), 0)
    col = lax.broadcasted_iota(jnp.int32, (1, S * R), 1)
    same = (row % CR) == (col % CR)
    low = lax.broadcasted_iota(jnp.int32, (1, 128), 1) < 64
    masks = [jnp.where(low == first, 1.0, 0.0).astype(BF16) for first in (True, False)]

    def stack(t):
        return jnp.concatenate([t * masks[0], t * masks[1]], axis=0)

    def unstack(t):
        return jnp.where(low, t[: S * R], t[S * R :])

    for fb in range(6):
        at = slice(fb * 128, (fb + 1) * 128)
        kb, vb = blk(k, fb), blk(v, fb)
        qs, gs = stack(blk(q, fb)), stack(blk(ga, fb))
        logits = jnp.where(same, dot_nt(qs, kb), -1e30)
        e = jnp.exp(logits - jnp.max(logits, axis=-1, keepdims=True))
        p = e * (1.0 / jnp.sum(e, axis=-1, keepdims=True))
        w = p.astype(BF16)
        grads = dot_nt(gs, vb)
        dl = (p * (grads - jnp.sum(p * grads, axis=-1, keepdims=True))).astype(BF16)
        att_s[:, at] = unstack(dot(w, vb)).astype(BF16)
        gq_s[:, at] = (unstack(dot(dl, kb)) * COL_SCALE).astype(BF16)
        gk_s[:, at] = dot_tn(dl, qs).astype(BF16)
        gv_s[:, at] = dot_tn(w, gs).astype(BF16)
    back[:, 0:D] = (mid + dot(att_s[...], out_col())).astype(BF16)
    gn = (
        dot_nt(gq_s[...], wq[...]) + dot_nt(gk_s[...], wk()) + dot_nt(gv_s[...], wv())
    )
    gmid = (cot.astype(F32) + norm_grad(gn, gain[...].reshape(1, D), hat, r)).astype(BF16)
    back[:, D : 2 * D] = gmid
    gra = dot_nt(gmid, out_row[...]).astype(BF16)
    gra = dot(pad, gra).reshape(NS, S, CP, D)
    seqs = [gra[:, s].reshape(NS * CP, D) for s in range(S)]
    per_group = []
    for g in range(NG):
        cols = []
        for h in range(GH):
            n = g * GH + h
            for sp in range(2):
                cols.append(
                    halves(blk(seqs[2 * sp], n // 2), blk(seqs[2 * sp + 1], n // 2), n % 2, n % 2)
                )
        per_group.append(jnp.concatenate(cols, axis=1).reshape(NS, 1, CP, WIDTH))
    grad_out[...] = jnp.concatenate(per_group, axis=1).reshape(TOK, WIDTH).astype(BF16)


def k_grad_probs(grads, values, back, gra, out, gra_s, out_s, sems):
    push = Pushes(sems)
    perm = to_wide()
    for h in range(GH):
        c = slice(h * 256, (h + 1) * 256)
        gra_s[:, c] = dot_tn(perm, grads[:, c]).astype(BF16)
    push.start(gra_s, gra)
    first, second = back[:, 0:D].astype(F32), back[:, D : 2 * D].astype(F32)

    def products(h):
        c = slice(h * 256, (h + 1) * 256)
        return dot_nt(gra_s[:, c], values[:, :, c].reshape(NY * I, 256))

    rows_out(out, out_s, products, first, second, push)
    push.finish()


def k_grad_values(weights, gra, gv0, gv1, gv2, gv3, gv, sems):
    for h in range(GH):
        c = slice(h * 256, (h + 1) * 256)
        t = dot_tn(weights[h * I : (h + 1) * I], gra[:, c]).astype(BF16)
        gv[:, :, c] = t.reshape(NY, I, 256)
    me = lax.axis_index("y")
    push = Pushes(sems)
    push.start(gv.at[me], gv0)
    for k, out in enumerate((gv1, gv2, gv3)):
        out[...] = gv[me ^ (k + 1)]
    push.finish()


def k_sum_values(gv0, gv1, gv3, gv, g_s, gv_s, sems):
    (gv0,) = fetch((gv0,), (g_s,), sems)
    push = Pushes(sems, 1)
    total = gv1[...].astype(F32) + gv3[...].astype(F32)
    gv_s[...] = total + gv0().astype(F32)
    push.start(gv_s, gv)
    push.finish()


def k_softmax_grad(parts, probs, gv, out, p_s, out_s, sems):
    (probs,) = fetch((probs,), (p_s,), sems)
    push = Pushes(sems, 1)
    grads = summed(parts)
    p = probs()
    dl = p * (grads - jnp.sum(p * grads, axis=-1, keepdims=True)) * ROW_SCALE
    out_s[...] = dl.astype(BF16)
    for a in range(NS):
        push.start(out_s, out.at[a])
    push.finish()


def k_grad_keys(dl, queries, before, gk, q_s, gk_s, sems):
    (queries,) = fetch((queries,), (q_s,), sems)
    push = Pushes(sems, 1)
    queries = queries()
    for h in range(GH):
        c = slice(h * 256, (h + 1) * 256)
        gk_s[:, c] = dot_tn(dl[h * I : (h + 1) * I], queries[:, c]).astype(BF16)
        for r in (slice(0, D // 2), slice(D // 2, D)):
            push.start(gk_s.at[r, c], gk.at[r, c])
    push.finish()


def k_grad_queries(
    dl, keys, gv, gv2, gqv0, gqv1, gqv2, gqv3,
    sum_s, two_s, gv_s, gq_s, o0, o1, o2, o3, sems,
):
    gv, gv2 = fetch((gv, gv2), (sum_s, two_s), sems)
    push = Pushes(sems, 2)
    for h in range(GH):
        c = slice(h * 256, (h + 1) * 256)
        gq_s[:, :, c] = dot(dl[h * I : (h + 1) * I], keys[:, c]).astype(BF16).reshape(NG, R, 256)
    gv_s[...] = (gv() + gv2().astype(F32)).astype(BF16).reshape(NG, R, WIDTH)
    me = my_group()
    for k, (held, out) in enumerate(zip((o0, o1, o2, o3), (gqv0, gqv1, gqv2, gqv3))):
        held[:, 0:WIDTH] = gq_s[me ^ k]
        held[:, WIDTH : 2 * WIDTH] = gv_s[me ^ k]
        push.start(held, out)
    push.finish()


def k_block_out(sent, out):
    first, _ = rows_in(sent)
    out[...] = dot_tn(to_column(), first.astype(BF16)).reshape(S, R, D).astype(BF16)


def token_rows(groups):
    rows = []
    for s in range(S):
        cols = []
        for fb in range(6):
            pair = []
            for n in (2 * fb, 2 * fb + 1):
                pair.append(blk(groups[n // GH], (n % GH) * 2 + s // 2))
            cols.append(halves(pair[0], pair[1], s % 2, s % 2))
        rows.append(jnp.concatenate(cols, axis=1))
    return jnp.concatenate(rows, axis=0).astype(BF16)


def k_finish_keys(gk, wk, out, gk_s, wk_s, out_s, sems):
    gk, wk = fetch((gk, wk), (gk_s, wk_s), sems, cuts=3)
    push = Pushes(sems, 6)
    gk()
    groups = []
    for g in range(NG):
        t = gk_s[g * R : (g + 1) * R].astype(F32)
        for yy in range(1, NY):
            lo = (yy * NG + g) * R
            t = t + gk_s[lo : lo + R].astype(F32)
        groups.append(t)
    out_s[...] = dot_nt(token_rows(groups), wk())
    push.start(out_s, out)
    push.finish()


def k_finish(
    gqv0, gqv1, gqv2, gqv3, part, x, sent, gain, wq, wv, input_grad,
    gqv, own_s, part_s, sems,
):
    gqv0, part = fetch((gqv0, part), (own_s, part_s), sems)
    me = my_group()
    for k, got in enumerate((gqv1, gqv2, gqv3)):
        gqv[me ^ (k + 1)] = got[...]
    perm = to_column()
    _, second = rows_in(sent)
    gmid = dot_tn(perm, second.astype(BF16))
    hat, r = moments(x[...].astype(F32).reshape(S * R, D))
    gqv[me] = gqv0()
    total = None
    for first, w in ((0, wq), (WIDTH, wv)):
        groups = [gqv[g, :, first : first + WIDTH].astype(F32) for g in range(NG)]
        t = dot_nt(token_rows(groups), w[...])
        total = t if total is None else total + t
    total = total + part()
    grad = gmid + norm_grad(total, gain[...].reshape(1, D), hat, r)
    input_grad[...] = grad.reshape(S, R, D).astype(BF16)


def swap(x, axes):
    return lax.all_to_all(x, axes, split_axis=0, concat_axis=0, tiled=True)


def spread(parts, axes):
    n = len(parts)
    pairs = [[(i, i ^ k) for i in range(n)] for k in range(n)]
    return [parts[0]] + [lax.ppermute(parts[k], axes, pairs[k]) for k in range(1, n)]


def local(
    x,
    cot,
    gain_row,
    query_row,
    key_row,
    value_row,
    out_row,
    gain_col,
    query_col,
    key_col,
    value_col,
    out_col,
):
    piece = ((R, 2 * WIDTH), BF16)
    block = ((NS, BLOCK, NY * I), BF16)
    part = ((NG, R, WIDTH), BF16)
    weight = pltpu.VMEM((D, D), BF16)
    row = pltpu.VMEM((S, R, D), BF16)
    gain = pltpu.VMEM((D,), F32)
    keys = call(
        k_keys,
        [pltpu.HBM((NY * NG, R, WIDTH), BF16)],
        x, gain_row, key_row,
        far=(0, 1, 2),
        sems=6 + NY * NG,
        scratch=[row, gain, weight, pltpu.VMEM(*part)],
    )
    qv = call(
        k_queries_values,
        [piece] * NG,
        x, gain_row, query_row, value_row,
        far=(0, 1, 2, 3),
        sems=4,
        scratch=[row, gain, weight, weight, pltpu.VMEM((NG, R, 2 * WIDTH), BF16)],
    )
    qv = spread(qv, GRP)
    keys = swap(keys, ALLRES).reshape(NY * I, WIDTH)
    parts, queries, values = call(
        k_logits,
        [pltpu.HBM(*block), pltpu.HBM(*part), pltpu.HBM(*part)],
        *qv, keys, x, cot,
        sems=2 + NS,
        scratch=[pltpu.VMEM(*block), pltpu.VMEM(*part), pltpu.VMEM(*part)],
    )
    queries = queries.reshape(I, WIDTH)
    parts = swap(parts, SEQ)
    values = spread([values.reshape(I, WIDTH)] * NY, "y")
    gathered = pltpu.VMEM((NY, I, WIDTH), BF16)
    values = call(
        k_gather,
        [pltpu.HBM((NY, I, WIDTH), BF16)],
        *values,
        far=(0,),
        sems=2,
        scratch=[gathered],
    )
    probs, weights = call(
        k_softmax,
        [pltpu.HBM((ROWS, NY * I), F32), ((NS, ROWS, NY * I), BF16)],
        parts, values,
        far=(1,),
        sems=1,
        scratch=[pltpu.VMEM((ROWS, NY * I), F32)],
    )
    weights = swap(weights, SEQ).reshape(GH * I, NY * I)
    att = call(k_attend, [((TOK, WIDTH), BF16)], weights, values)
    att = swap(att, WIDE)
    back, grads = call(
        k_column,
        [((S * R, 2 * D), BF16), ((TOK, WIDTH), BF16)],
        att, parts, gain_col, out_row, query_col, key_col, value_col, out_col,
        mem=32,
        far=(5, 6, 7),
        sems=6,
        scratch=[weight] * 3 + [pltpu.VMEM((S * R, D), BF16)] * 4,
    )
    grads = swap(grads, WIDE)
    gra, gparts = call(
        k_grad_probs,
        [pltpu.HBM((I, WIDTH), BF16), pltpu.HBM(*block)],
        grads, values, back,
        sems=1 + NS,
        scratch=[pltpu.VMEM((I, WIDTH), BF16), pltpu.VMEM(*block)],
    )
    gparts = swap(gparts, SEQ)
    gv = call(
        k_grad_values,
        [pltpu.HBM((I, WIDTH), BF16)] + [((I, WIDTH), BF16)] * (NY - 1),
        weights, gra,
        sems=1,
        scratch=[gathered],
    )
    gv = spread(gv, "y")
    summand = pltpu.VMEM((I, WIDTH), BF16)
    sum_s = pltpu.VMEM((I, WIDTH), F32)
    some = call(
        k_sum_values,
        [pltpu.HBM((I, WIDTH), F32)],
        gv[0], gv[1], gv[3],
        far=(0,),
        sems=2,
        scratch=[summand, sum_s],
    )
    dl = call(
        k_softmax_grad,
        [pltpu.HBM((NS, ROWS, NY * I), BF16)],
        gparts, probs, some,
        far=(1, 2),
        sems=1 + NS,
        scratch=[pltpu.VMEM((ROWS, NY * I), F32), pltpu.VMEM((ROWS, NY * I), BF16)],
    )
    dl = swap(dl, SEQ).reshape(GH * I, NY * I)
    gk = call(
        k_grad_keys,
        [pltpu.HBM((D, D), BF16)],
        dl, queries, gv[2],
        far=(1, 2),
        sems=2 * GH + 1,
        scratch=[summand, weight],
    )
    gqv = call(
        k_grad_queries,
        [pltpu.HBM(*piece)] * NG,
        dl, keys, some, gv[2],
        far=(2, 3),
        sems=2 + NG,
        scratch=[sum_s, summand, pltpu.VMEM(*part), pltpu.VMEM(*part)] + [pltpu.VMEM(*piece)] * NG,
    )
    gqv = spread(gqv, GRP)
    gk = swap(gk, ALLRES).reshape(NY * I, WIDTH)
    block_out = call(k_block_out, [((S, R, D), BF16)], gparts)
    total = pltpu.VMEM((S * R, D), F32)
    from_keys = call(
        k_finish_keys,
        [pltpu.HBM((S * R, D), F32)],
        gk, key_row,
        cost=pl.CostEstimate(flops=4 * 10**9, bytes_accessed=3 * 10**6, transcendentals=0),
        far=(0, 1),
        sems=7,
        scratch=[weight, weight, total],
    )
    input_grad = call(
        k_finish,
        [((S, R, D), BF16)],
        *gqv, from_keys, x, gparts, gain_row, query_row, value_row,
        far=(0, 4),
        sems=2,
        scratch=[
            pltpu.VMEM((NG, R, 2 * WIDTH), BF16),
            pltpu.VMEM(*piece),
            total,
        ],
    )
    return block_out, input_grad


def solution(mesh):
    fine = Mesh(mesh.devices.reshape(2, 4, 2, 4, 2), ("xh", "z", "xl", "y", "c"))
    spec = P(("xh", "z"), ("xl", "y", "c"), None)
    return jax.shard_map(
        local,
        mesh=fine,
        in_specs=(spec, spec) + (P(),) * 10,
        out_specs=(spec, spec),
        check_vma=False,
    )
```

```python
import math

import jax
import jax.numpy as jnp
from jax import lax
from jax.experimental import pallas as pl
from jax.experimental.pallas import tpu as pltpu
from jax.sharding import Mesh
from jax.sharding import PartitionSpec as P

F32 = jnp.float32
BF16 = jnp.bfloat16
D = 768
HEADS = 12
HEAD_DIM = 64
SEQ = ("xh", "z")
GRP = ("xl", "c")
WIDE = ("xh", "z", "xl", "c")
ALLRES = ("y", "xl", "c")
NS, NG, NY = 8, 4, 4
GH = HEADS // NG
S = 4
R = 48
I = R * NG
CR = 6
CP = 8
TOK = NS * S * CP
ROWS = GH * I // NS
SENT = S * CR
BLOCK = ROWS + 2 * SENT
READ = 80
WIDTH = GH * S * HEAD_DIM
ROW_SCALE = 1.0 / math.sqrt(HEAD_DIM * 32)
COL_SCALE = 1.0 / math.sqrt(HEAD_DIM)


def dot(a, b):
    return lax.dot_general(a, b, (((1,), (0,)), ((), ())), preferred_element_type=F32)


def dot_nt(a, b):
    return lax.dot_general(a, b, (((1,), (1,)), ((), ())), preferred_element_type=F32)


def dot_tn(a, b):
    return lax.dot_general(a, b, (((0,), (0,)), ((), ())), preferred_element_type=F32)


def call(kernel, outs, *args, mem=16, scratch=(), far=(), sems=0, cost=None):
    scratch = list(scratch)
    if sems:
        scratch.append(pltpu.SemaphoreType.DMA((sems,)))
    args = [
        pltpu.with_memory_space_constraint(a, pltpu.HBM) if i in far else a
        for i, a in enumerate(args)
    ]
    shapes = [jax.ShapeDtypeStruct(*o) if isinstance(o, tuple) else o for o in outs]
    spaces = [pltpu.VMEM if isinstance(o, tuple) else o.memory_space for o in outs]
    res = pl.pallas_call(
        kernel,
        out_shape=shapes,
        in_specs=[
            pl.BlockSpec(memory_space=pltpu.HBM if i in far else pltpu.VMEM)
            for i in range(len(args))
        ],
        out_specs=[pl.BlockSpec(memory_space=m) for m in spaces],
        scratch_shapes=scratch,
        cost_estimate=cost,
        compiler_params=pltpu.CompilerParams(vmem_limit_bytes=mem * 2**20),
    )(*args)
    return res[0] if len(outs) == 1 else res


def fetch(sources, targets, sems, wait_only=False, cuts=1):
    reads, at = [], 0
    for src, dst in zip(sources, targets):
        copies = []
        parts = cuts if src.shape[0] == D and len(src.shape) == 2 else 1
        for n in range(parts):
            rows = slice(n * D // parts, (n + 1) * D // parts)
            a, b = (src.at[rows], dst.at[rows]) if parts > 1 else (src, dst)
            copies.append(pltpu.make_async_copy(a, b, sems.at[at]))
            at += 1
        for c in copies:
            c.start()

        def read(copies=copies, dst=dst):
            for c in copies:
                c.wait()
            copies.clear()
            return None if wait_only else dst[...]

        reads.append(read)
    return reads


class Pushes:
    def __init__(self, sems, first=0):
        self.sems, self.first, self.begun = sems, first, []

    def start(self, src, dst):
        c = pltpu.make_async_copy(src, dst, self.sems.at[self.first + len(self.begun)])
        c.start()
        self.begun.append(c)

    def finish(self):
        for c in self.begun:
            c.wait()


def my_group():
    return lax.axis_index("xl") * 2 + lax.axis_index("c")


def halves(a, b, half_a, half_b):
    low = lax.broadcasted_iota(jnp.int32, a.shape, 1) < 64
    a = a if half_a == 0 else pltpu.roll(a, 64, 1)
    b = b if half_b == 1 else pltpu.roll(b, 64, 1)
    return jnp.where(low, a, b)


def blk(v, n):
    return v[:, n * 128 : (n + 1) * 128]


def to_column():
    row = lax.broadcasted_iota(jnp.int32, (S * R, S * R), 0)
    col = lax.broadcasted_iota(jnp.int32, (S * R, S * R), 1)
    want = ((row // CR) % S) * R + (row // (CR * S)) * CR + row % CR
    return jnp.where(col == want, 1.0, 0.0).astype(BF16)


def to_padded():
    row = lax.broadcasted_iota(jnp.int32, (TOK, S * R), 0)
    col = lax.broadcasted_iota(jnp.int32, (TOK, S * R), 1)
    r = row % CP
    return jnp.where((r < CR) & (col == (row // CP) * CR + r), 1.0, 0.0).astype(BF16)


def to_wide():
    row = lax.broadcasted_iota(jnp.int32, (TOK, I), 0)
    col = lax.broadcasted_iota(jnp.int32, (TOK, I), 1)
    r = row % CP
    want = ((row // CP) % NG) * R + (row // (CP * NG)) * CR + r
    return jnp.where((r < CR) & (col == want), 1.0, 0.0).astype(BF16)


def moments(v):
    mean = jnp.mean(v, axis=-1, keepdims=True)
    centred = v - mean
    r = lax.rsqrt(jnp.mean(centred * centred, axis=-1, keepdims=True) + 1e-05)
    return centred * r, r


def norm_grad(grad, gain, hat, r):
    g = grad * gain
    return r * (
        g - jnp.mean(g, axis=-1, keepdims=True) - hat * jnp.mean(g * hat, axis=-1, keepdims=True)
    )


def pieces(y, put, after=None):
    for g in range(NG):
        for h in range(GH):
            n = g * GH + h
            src = blk(y, n // 2)
            for sp in range(2):
                a = src[2 * sp * R : (2 * sp + 1) * R]
                b = src[(2 * sp + 1) * R : (2 * sp + 2) * R]
                put(g, h * 256 + sp * 128, halves(a, b, n % 2, n % 2).astype(BF16))
        if after is not None:
            after(g)


def normed_input(x, gain):
    hat, _ = moments(x.astype(F32).reshape(S * R, D))
    return (hat * gain.reshape(1, D)).astype(BF16)


def k_keys(x, gain, w, keys, x_s, g_s, w_s, keys_s, sems):
    x, gain, w = fetch((x, gain, w), (x_s, g_s, w_s), sems, cuts=4)
    push = Pushes(sems, 6)
    normed = normed_input(x(), gain())

    def put(g, at, piece):
        keys_s[g, :, at : at + 128] = piece

    def after(g):
        for yy in range(NY):
            push.start(keys_s.at[g], keys.at[yy * NG + g])

    pieces(dot(normed, w()), put, after)
    push.finish()


def k_queries_values(x, gain, wq, wv, qv0, qv1, qv2, qv3, x_s, g_s, wq_s, wv_s, qv, sems):
    x, gain, wq, wv = fetch((x, gain, wq, wv), (x_s, g_s, wq_s, wv_s), sems)
    normed = normed_input(x(), gain())
    for first, w in ((0, wq), (WIDTH, wv)):

        def put(g, at, piece, first=first):
            qv[g, :, first + at : first + at + 128] = piece

        pieces(dot(normed, w()), put)
    me = my_group()
    for k, out in enumerate((qv0, qv1, qv2, qv3)):
        out[...] = qv[me ^ k]


def rows_out(out, out_s, products, first, second, push):
    done = []
    for a in range(NS):
        while len(done) * I < (a + 1) * ROWS:
            done.append(products(len(done)))
        head = a * ROWS // I
        rows = jnp.concatenate(done[head:], axis=0)
        lo = a * ROWS - head * I
        t = slice(a * SENT, (a + 1) * SENT)
        rows = jnp.concatenate((rows[lo : lo + ROWS], first[t], second[t]), axis=0)
        out_s[a] = rows.astype(BF16)
        push.start(out_s.at[a], out.at[a])


def rows_in(parts):
    got = [parts[a].astype(F32) for a in range(NS)]
    first = jnp.concatenate([t[ROWS : ROWS + SENT] for t in got], axis=0)
    second = jnp.concatenate([t[ROWS + SENT :] for t in got], axis=0)
    return first, second


def k_logits(
    qv0, qv1, qv2, qv3, keys, x, cot, out, queries, values, out_s, q_s, v_s, sems
):
    push = Pushes(sems)
    me = my_group()
    for k, qv in enumerate((qv0, qv1, qv2, qv3)):
        q_s[me ^ k] = qv[:, 0:WIDTH]
        v_s[me ^ k] = qv[:, WIDTH : 2 * WIDTH]
    push.start(q_s, queries)
    push.start(v_s, values)
    perm = to_column()
    first = dot(perm, x[...].astype(F32).reshape(S * R, D).astype(BF16))
    second = dot(perm, cot[...].astype(F32).reshape(S * R, D).astype(BF16))

    def products(h):
        c = slice(h * 256, (h + 1) * 256)
        return dot_nt(q_s[:, :, c].reshape(I, 256), keys[:, c])

    rows_out(out, out_s, products, first, second, push)
    push.finish()


def summed(parts):
    total = parts[0, 0:READ].astype(F32)
    for a in range(1, NS):
        total = total + parts[a, 0:READ].astype(F32)
    return total[:ROWS]


def k_softmax(parts, values, probs, weights, p_s, sems):
    push = Pushes(sems)
    logits = summed(parts) * ROW_SCALE
    e = jnp.exp(logits - jnp.max(logits, axis=-1, keepdims=True))
    p = e * (1.0 / jnp.sum(e, axis=-1, keepdims=True))
    p_s[...] = p
    push.start(p_s, probs)
    w = p.astype(BF16)
    for a in range(NS):
        weights[a] = w
    push.finish()


def k_gather(v0, v1, v2, v3, out, values, sems):
    me = lax.axis_index("y")
    (own,) = fetch((v0,), (values.at[me],), sems, wait_only=True)
    push = Pushes(sems, 1)
    for k, v in enumerate((v1, v2, v3)):
        values[me ^ (k + 1)] = v[...]
    own()
    push.start(values, out)
    push.finish()


def k_attend(weights, values, out):
    perm = to_wide()
    for h in range(GH):
        c = slice(h * 256, (h + 1) * 256)
        v = values[:, :, c].reshape(NY * I, 256)
        att = dot(weights[h * I : (h + 1) * I], v).astype(BF16)
        out[:, c] = dot(perm, att).astype(BF16)


def k_column(
    att_in, sent, gain, out_row, wq, wk, wv, out_col, back, grad_out,
    wk_s, wv_s, oc_s, att_s, gq_s, gk_s, gv_s, sems,
):
    wk, wv, out_col = fetch((wk, wv, out_col), (wk_s, wv_s, oc_s), sems, cuts=2)
    raw = att_in[...].astype(F32).reshape(NS, NG, CP, WIDTH)
    groups = [raw[:, g].reshape(NS * CP, WIDTH) for g in range(NG)]
    per_seq = []
    for s in range(S):
        cols = []
        for fb in range(6):
            pair = []
            for n in (2 * fb, 2 * fb + 1):
                pair.append(blk(groups[n // GH], (n % GH) * 2 + s // 2))
            cols.append(halves(pair[0], pair[1], s % 2, s % 2))
        per_seq.append(jnp.concatenate(cols, axis=1).reshape(NS, 1, CP, D))
    att_row = jnp.concatenate(per_seq, axis=1).reshape(TOK, D).astype(BF16)
    pad = to_padded()
    att_row = dot_tn(pad, att_row).astype(BF16)
    xc, cot = rows_in(sent)
    cot = cot.astype(BF16)
    middle = (xc + dot(att_row, out_row[...])).astype(BF16)
    mid = middle.astype(F32)
    hat, r = moments(mid)
    normed = (hat * gain[...].reshape(1, D)).astype(BF16)
    q = dot(normed, wq[...]).astype(BF16) * jnp.asarray(COL_SCALE, BF16)
    k = dot(normed, wk()).astype(BF16)
    v = dot(normed, wv()).astype(BF16)
    ga = dot_nt(cot, out_col()).astype(BF16)
    row = lax.broadcasted_iota(jnp.int32, (2 * S * R, 1), 0)
    col = lax.broadcasted_iota(jnp.int32, (1, S * R), 1)
    same = (row % CR) == (col % CR)
    low = lax.broadcasted_iota(jnp.int32, (1, 128), 1) < 64
    masks = [jnp.where(low == first, 1.0, 0.0).astype(BF16) for first in (True, False)]

    def stack(t):
        return jnp.concatenate([t * masks[0], t * masks[1]], axis=0)

    def unstack(t):
        return jnp.where(low, t[: S * R], t[S * R :])

    for fb in range(6):
        at = slice(fb * 128, (fb + 1) * 128)
        kb, vb = blk(k, fb), blk(v, fb)
        qs, gs = stack(blk(q, fb)), stack(blk(ga, fb))
        logits = jnp.where(same, dot_nt(qs, kb), -1e30)
        e = jnp.exp(logits - jnp.max(logits, axis=-1, keepdims=True))
        p = e * (1.0 / jnp.sum(e, axis=-1, keepdims=True))
        w = p.astype(BF16)
        grads = dot_nt(gs, vb)
        dl = (p * (grads - jnp.sum(p * grads, axis=-1, keepdims=True))).astype(BF16)
        att_s[:, at] = unstack(dot(w, vb)).astype(BF16)
        gq_s[:, at] = (unstack(dot(dl, kb)) * COL_SCALE).astype(BF16)
        gk_s[:, at] = dot_tn(dl, qs).astype(BF16)
        gv_s[:, at] = dot_tn(w, gs).astype(BF16)
    back[:, 0:D] = (mid + dot(att_s[...], out_col())).astype(BF16)
    gn = (
        dot_nt(gq_s[...], wq[...]) + dot_nt(gk_s[...], wk()) + dot_nt(gv_s[...], wv())
    )
    gmid = (cot.astype(F32) + norm_grad(gn, gain[...].reshape(1, D), hat, r)).astype(BF16)
    back[:, D : 2 * D] = gmid
    gra = dot_nt(gmid, out_row[...]).astype(BF16)
    gra = dot(pad, gra).reshape(NS, S, CP, D)
    seqs = [gra[:, s].reshape(NS * CP, D) for s in range(S)]
    per_group = []
    for g in range(NG):
        cols = []
        for h in range(GH):
            n = g * GH + h
            for sp in range(2):
                cols.append(
                    halves(blk(seqs[2 * sp], n // 2), blk(seqs[2 * sp + 1], n // 2), n % 2, n % 2)
                )
        per_group.append(jnp.concatenate(cols, axis=1).reshape(NS, 1, CP, WIDTH))
    grad_out[...] = jnp.concatenate(per_group, axis=1).reshape(TOK, WIDTH).astype(BF16)


def k_grad_probs(grads, values, back, gra, out, gra_s, out_s, sems):
    push = Pushes(sems)
    perm = to_wide()
    for h in range(GH):
        c = slice(h * 256, (h + 1) * 256)
        gra_s[:, c] = dot_tn(perm, grads[:, c]).astype(BF16)
    push.start(gra_s, gra)
    first, second = back[:, 0:D].astype(F32), back[:, D : 2 * D].astype(F32)

    def products(h):
        c = slice(h * 256, (h + 1) * 256)
        return dot_nt(gra_s[:, c], values[:, :, c].reshape(NY * I, 256))

    rows_out(out, out_s, products, first, second, push)
    push.finish()


def k_grad_values(weights, gra, gv0, gv1, gv2, gv3, gv, sems):
    for h in range(GH):
        c = slice(h * 256, (h + 1) * 256)
        t = dot_tn(weights[h * I : (h + 1) * I], gra[:, c]).astype(BF16)
        gv[:, :, c] = t.reshape(NY, I, 256)
    me = lax.axis_index("y")
    push = Pushes(sems)
    push.start(gv.at[me], gv0)
    for k, out in enumerate((gv1, gv2, gv3)):
        out[...] = gv[me ^ (k + 1)]
    push.finish()


def k_sum_values(gv0, gv1, gv3, gv, g_s, gv_s, sems):
    (gv0,) = fetch((gv0,), (g_s,), sems)
    push = Pushes(sems, 1)
    total = gv1[...].astype(F32) + gv3[...].astype(F32)
    gv_s[...] = total + gv0().astype(F32)
    push.start(gv_s, gv)
    push.finish()


def k_softmax_grad(parts, probs, gv, out, p_s, out_s, sems):
    (probs,) = fetch((probs,), (p_s,), sems)
    push = Pushes(sems, 1)
    grads = summed(parts)
    p = probs()
    dl = p * (grads - jnp.sum(p * grads, axis=-1, keepdims=True)) * ROW_SCALE
    out_s[...] = dl.astype(BF16)
    for a in range(NS):
        push.start(out_s, out.at[a])
    push.finish()


def k_grad_keys(dl, queries, before, gk, q_s, gk_s, sems):
    (queries,) = fetch((queries,), (q_s,), sems)
    push = Pushes(sems, 1)
    queries = queries()
    for h in range(GH):
        c = slice(h * 256, (h + 1) * 256)
        gk_s[:, c] = dot_tn(dl[h * I : (h + 1) * I], queries[:, c]).astype(BF16)
        for r in (slice(0, D // 2), slice(D // 2, D)):
            push.start(gk_s.at[r, c], gk.at[r, c])
    push.finish()


def k_grad_queries(
    dl, keys, gv, gv2, gqv0, gqv1, gqv2, gqv3,
    sum_s, two_s, gv_s, gq_s, o0, o1, o2, o3, sems,
):
    gv, gv2 = fetch((gv, gv2), (sum_s, two_s), sems)
    push = Pushes(sems, 2)
    for h in range(GH):
        c = slice(h * 256, (h + 1) * 256)
        gq_s[:, :, c] = dot(dl[h * I : (h + 1) * I], keys[:, c]).astype(BF16).reshape(NG, R, 256)
    gv_s[...] = (gv() + gv2().astype(F32)).astype(BF16).reshape(NG, R, WIDTH)
    me = my_group()
    for k, (held, out) in enumerate(zip((o0, o1, o2, o3), (gqv0, gqv1, gqv2, gqv3))):
        held[:, 0:WIDTH] = gq_s[me ^ k]
        held[:, WIDTH : 2 * WIDTH] = gv_s[me ^ k]
        push.start(held, out)
    push.finish()


def k_block_out(sent, out):
    first, _ = rows_in(sent)
    out[...] = dot_tn(to_column(), first.astype(BF16)).reshape(S, R, D).astype(BF16)


def token_rows(groups):
    rows = []
    for s in range(S):
        cols = []
        for fb in range(6):
            pair = []
            for n in (2 * fb, 2 * fb + 1):
                pair.append(blk(groups[n // GH], (n % GH) * 2 + s // 2))
            cols.append(halves(pair[0], pair[1], s % 2, s % 2))
        rows.append(jnp.concatenate(cols, axis=1))
    return jnp.concatenate(rows, axis=0).astype(BF16)


def k_finish_keys(gk, wk, out, gk_s, wk_s, out_s, sems):
    gk, wk = fetch((gk, wk), (gk_s, wk_s), sems, cuts=3)
    push = Pushes(sems, 6)
    gk()
    groups = []
    for g in range(NG):
        t = gk_s[g * R : (g + 1) * R].astype(F32)
        for yy in range(1, NY):
            lo = (yy * NG + g) * R
            t = t + gk_s[lo : lo + R].astype(F32)
        groups.append(t)
    out_s[...] = dot_nt(token_rows(groups), wk())
    push.start(out_s, out)
    push.finish()


def k_finish(
    gqv0, gqv1, gqv2, gqv3, part, x, sent, gain, wq, wv, input_grad,
    gqv, own_s, part_s, sems,
):
    gqv0, part = fetch((gqv0, part), (own_s, part_s), sems)
    me = my_group()
    for k, got in enumerate((gqv1, gqv2, gqv3)):
        gqv[me ^ (k + 1)] = got[...]
    perm = to_column()
    _, second = rows_in(sent)
    gmid = dot_tn(perm, second.astype(BF16))
    hat, r = moments(x[...].astype(F32).reshape(S * R, D))
    gqv[me] = gqv0()
    total = None
    for first, w in ((0, wq), (WIDTH, wv)):
        groups = [gqv[g, :, first : first + WIDTH].astype(F32) for g in range(NG)]
        t = dot_nt(token_rows(groups), w[...])
        total = t if total is None else total + t
    total = total + part()
    grad = gmid + norm_grad(total, gain[...].reshape(1, D), hat, r)
    input_grad[...] = grad.reshape(S, R, D).astype(BF16)


def swap(x, axes):
    return lax.all_to_all(x, axes, split_axis=0, concat_axis=0, tiled=True)


def spread(parts, axes):
    n = len(parts)
    pairs = [[(i, i ^ k) for i in range(n)] for k in range(n)]
    return [parts[0]] + [lax.ppermute(parts[k], axes, pairs[k]) for k in range(1, n)]


def local(
    x,
    cot,
    gain_row,
    query_row,
    key_row,
    value_row,
    out_row,
    gain_col,
    query_col,
    key_col,
    value_col,
    out_col,
):
    piece = ((R, 2 * WIDTH), BF16)
    block = ((NS, BLOCK, NY * I), BF16)
    part = ((NG, R, WIDTH), BF16)
    weight = pltpu.VMEM((D, D), BF16)
    row = pltpu.VMEM((S, R, D), BF16)
    gain = pltpu.VMEM((D,), F32)
    keys = call(
        k_keys,
        [pltpu.HBM((NY * NG, R, WIDTH), BF16)],
        x, gain_row, key_row,
        far=(0, 1, 2),
        sems=6 + NY * NG,
        scratch=[row, gain, weight, pltpu.VMEM(*part)],
    )
    qv = call(
        k_queries_values,
        [piece] * NG,
        x, gain_row, query_row, value_row,
        far=(0, 1, 2, 3),
        sems=4,
        scratch=[row, gain, weight, weight, pltpu.VMEM((NG, R, 2 * WIDTH), BF16)],
    )
    qv = spread(qv, GRP)
    keys = swap(keys, ALLRES).reshape(NY * I, WIDTH)
    parts, queries, values = call(
        k_logits,
        [pltpu.HBM(*block), pltpu.HBM(*part), pltpu.HBM(*part)],
        *qv, keys, x, cot,
        sems=2 + NS,
        scratch=[pltpu.VMEM(*block), pltpu.VMEM(*part), pltpu.VMEM(*part)],
    )
    queries = queries.reshape(I, WIDTH)
    parts = swap(parts, SEQ)
    values = spread([values.reshape(I, WIDTH)] * NY, "y")
    gathered = pltpu.VMEM((NY, I, WIDTH), BF16)
    values = call(
        k_gather,
        [pltpu.HBM((NY, I, WIDTH), BF16)],
        *values,
        far=(0,),
        sems=2,
        scratch=[gathered],
    )
    probs, weights = call(
        k_softmax,
        [pltpu.HBM((ROWS, NY * I), F32), ((NS, ROWS, NY * I), BF16)],
        parts, values,
        far=(1,),
        sems=1,
        scratch=[pltpu.VMEM((ROWS, NY * I), F32)],
    )
    weights = swap(weights, SEQ).reshape(GH * I, NY * I)
    att = call(k_attend, [((TOK, WIDTH), BF16)], weights, values)
    att = swap(att, WIDE)
    back, grads = call(
        k_column,
        [((S * R, 2 * D), BF16), ((TOK, WIDTH), BF16)],
        att, parts, gain_col, out_row, query_col, key_col, value_col, out_col,
        mem=32,
        far=(5, 6, 7),
        sems=6,
        scratch=[weight] * 3 + [pltpu.VMEM((S * R, D), BF16)] * 4,
    )
    grads = swap(grads, WIDE)
    gra, gparts = call(
        k_grad_probs,
        [pltpu.HBM((I, WIDTH), BF16), pltpu.HBM(*block)],
        grads, values, back,
        sems=1 + NS,
        scratch=[pltpu.VMEM((I, WIDTH), BF16), pltpu.VMEM(*block)],
    )
    gparts = swap(gparts, SEQ)
    gv = call(
        k_grad_values,
        [pltpu.HBM((I, WIDTH), BF16)] + [((I, WIDTH), BF16)] * (NY - 1),
        weights, gra,
        sems=1,
        scratch=[gathered],
    )
    gv = spread(gv, "y")
    summand = pltpu.VMEM((I, WIDTH), BF16)
    sum_s = pltpu.VMEM((I, WIDTH), F32)
    some = call(
        k_sum_values,
        [pltpu.HBM((I, WIDTH), F32)],
        gv[0], gv[1], gv[3],
        far=(0,),
        sems=2,
        scratch=[summand, sum_s],
    )
    dl = call(
        k_softmax_grad,
        [pltpu.HBM((NS, ROWS, NY * I), BF16)],
        gparts, probs, some,
        far=(1, 2),
        sems=1 + NS,
        scratch=[pltpu.VMEM((ROWS, NY * I), F32), pltpu.VMEM((ROWS, NY * I), BF16)],
    )
    dl = swap(dl, SEQ).reshape(GH * I, NY * I)
    gk = call(
        k_grad_keys,
        [pltpu.HBM((D, D), BF16)],
        dl, queries, gv[2],
        far=(1, 2),
        sems=2 * GH + 1,
        scratch=[summand, weight],
    )
    gqv = call(
        k_grad_queries,
        [pltpu.HBM(*piece)] * NG,
        dl, keys, some, gv[2],
        far=(2, 3),
        sems=2 + NG,
        scratch=[sum_s, summand, pltpu.VMEM(*part), pltpu.VMEM(*part)] + [pltpu.VMEM(*piece)] * NG,
    )
    gqv = spread(gqv, GRP)
    gk = swap(gk, ALLRES).reshape(NY * I, WIDTH)
    block_out = call(k_block_out, [((S, R, D), BF16)], gparts)
    total = pltpu.VMEM((S * R, D), F32)
    from_keys = call(
        k_finish_keys,
        [pltpu.HBM((S * R, D), F32)],
        gk, key_row,
        cost=pl.CostEstimate(flops=4 * 10**9, bytes_accessed=3 * 10**6, transcendentals=0),
        far=(0, 1),
        sems=7,
        scratch=[weight, weight, total],
    )
    input_grad = call(
        k_finish,
        [((S, R, D), BF16)],
        *gqv, from_keys, x, gparts, gain_row, query_row, value_row,
        far=(0, 4),
        sems=2,
        scratch=[
            pltpu.VMEM((NG, R, 2 * WIDTH), BF16),
            pltpu.VMEM(*piece),
            total,
        ],
    )
    return block_out, input_grad


def solution(mesh):
    fine = Mesh(mesh.devices.reshape(2, 4, 2, 4, 2), ("xh", "z", "xl", "y", "c"))
    spec = P(("xh", "z"), ("xl", "y", "c"), None)
    return jax.shard_map(
        local,
        mesh=fine,
        in_specs=(spec, spec) + (P(),) * 10,
        out_specs=(spec, spec),
        check_vma=False,
    )
```

```python
import math

import jax
import jax.numpy as jnp
from jax import lax
from jax.experimental import pallas as pl
from jax.experimental.pallas import tpu as pltpu
from jax.sharding import Mesh
from jax.sharding import PartitionSpec as P

F32 = jnp.float32
BF16 = jnp.bfloat16
D = 768
HEADS = 12
HEAD_DIM = 64
SEQ = ("xh", "z")
GRP = ("xl", "c")
WIDE = ("xh", "z", "xl", "c")
ALLRES = ("y", "xl", "c")
NS, NG, NY = 8, 4, 4
GH = HEADS // NG
S = 4
R = 48
I = R * NG
CR = 6
CP = 8
TOK = NS * S * CP
ROWS = GH * I // NS
SENT = S * CR
BLOCK = ROWS + 2 * SENT
READ = 80
WIDTH = GH * S * HEAD_DIM
ROW_SCALE = 1.0 / math.sqrt(HEAD_DIM * 32)
COL_SCALE = 1.0 / math.sqrt(HEAD_DIM)


def dot(a, b):
    return lax.dot_general(a, b, (((1,), (0,)), ((), ())), preferred_element_type=F32)


def dot_nt(a, b):
    return lax.dot_general(a, b, (((1,), (1,)), ((), ())), preferred_element_type=F32)


def dot_tn(a, b):
    return lax.dot_general(a, b, (((0,), (0,)), ((), ())), preferred_element_type=F32)


def call(kernel, outs, *args, mem=16, scratch=(), far=(), sems=0, cost=None):
    scratch = list(scratch)
    if sems:
        scratch.append(pltpu.SemaphoreType.DMA((sems,)))
    args = [
        pltpu.with_memory_space_constraint(a, pltpu.HBM) if i in far else a
        for i, a in enumerate(args)
    ]
    shapes = [jax.ShapeDtypeStruct(*o) if isinstance(o, tuple) else o for o in outs]
    spaces = [pltpu.VMEM if isinstance(o, tuple) else o.memory_space for o in outs]
    res = pl.pallas_call(
        kernel,
        out_shape=shapes,
        in_specs=[
            pl.BlockSpec(memory_space=pltpu.HBM if i in far else pltpu.VMEM)
            for i in range(len(args))
        ],
        out_specs=[pl.BlockSpec(memory_space=m) for m in spaces],
        scratch_shapes=scratch,
        cost_estimate=cost,
        compiler_params=pltpu.CompilerParams(vmem_limit_bytes=mem * 2**20),
    )(*args)
    return res[0] if len(outs) == 1 else res


def fetch(sources, targets, sems, wait_only=False, cuts=1):
    reads, at = [], 0
    for src, dst in zip(sources, targets):
        copies = []
        parts = cuts if src.shape[0] == D and len(src.shape) == 2 else 1
        for n in range(parts):
            rows = slice(n * D // parts, (n + 1) * D // parts)
            a, b = (src.at[rows], dst.at[rows]) if parts > 1 else (src, dst)
            copies.append(pltpu.make_async_copy(a, b, sems.at[at]))
            at += 1
        for c in copies:
            c.start()

        def read(copies=copies, dst=dst):
            for c in copies:
                c.wait()
            copies.clear()
            return None if wait_only else dst[...]

        reads.append(read)
    return reads


class Pushes:
    def __init__(self, sems, first=0):
        self.sems, self.first, self.begun = sems, first, []

    def start(self, src, dst):
        c = pltpu.make_async_copy(src, dst, self.sems.at[self.first + len(self.begun)])
        c.start()
        self.begun.append(c)

    def finish(self):
        for c in self.begun:
            c.wait()


def my_group():
    return lax.axis_index("xl") * 2 + lax.axis_index("c")


def halves(a, b, half_a, half_b):
    low = lax.broadcasted_iota(jnp.int32, a.shape, 1) < 64
    a = a if half_a == 0 else pltpu.roll(a, 64, 1)
    b = b if half_b == 1 else pltpu.roll(b, 64, 1)
    return jnp.where(low, a, b)


def blk(v, n):
    return v[:, n * 128 : (n + 1) * 128]


def to_column():
    row = lax.broadcasted_iota(jnp.int32, (S * R, S * R), 0)
    col = lax.broadcasted_iota(jnp.int32, (S * R, S * R), 1)
    want = ((row // CR) % S) * R + (row // (CR * S)) * CR + row % CR
    return jnp.where(col == want, 1.0, 0.0).astype(BF16)


def to_padded():
    row = lax.broadcasted_iota(jnp.int32, (TOK, S * R), 0)
    col = lax.broadcasted_iota(jnp.int32, (TOK, S * R), 1)
    r = row % CP
    return jnp.where((r < CR) & (col == (row // CP) * CR + r), 1.0, 0.0).astype(BF16)


def to_wide():
    row = lax.broadcasted_iota(jnp.int32, (TOK, I), 0)
    col = lax.broadcasted_iota(jnp.int32, (TOK, I), 1)
    r = row % CP
    want = ((row // CP) % NG) * R + (row // (CP * NG)) * CR + r
    return jnp.where((r < CR) & (col == want), 1.0, 0.0).astype(BF16)


def moments(v):
    mean = jnp.mean(v, axis=-1, keepdims=True)
    centred = v - mean
    r = lax.rsqrt(jnp.mean(centred * centred, axis=-1, keepdims=True) + 1e-05)
    return centred * r, r


def norm_grad(grad, gain, hat, r):
    g = grad * gain
    return r * (
        g - jnp.mean(g, axis=-1, keepdims=True) - hat * jnp.mean(g * hat, axis=-1, keepdims=True)
    )


def pieces(y, put, after=None):
    for g in range(NG):
        for h in range(GH):
            n = g * GH + h
            src = blk(y, n // 2)
            for sp in range(2):
                a = src[2 * sp * R : (2 * sp + 1) * R]
                b = src[(2 * sp + 1) * R : (2 * sp + 2) * R]
                put(g, h * 256 + sp * 128, halves(a, b, n % 2, n % 2).astype(BF16))
        if after is not None:
            after(g)


def normed_input(x, gain):
    hat, _ = moments(x.astype(F32).reshape(S * R, D))
    return (hat * gain.reshape(1, D)).astype(BF16)


def k_keys(x, gain, w, keys, x_s, g_s, w_s, keys_s, sems):
    x, gain, w = fetch((x, gain, w), (x_s, g_s, w_s), sems, cuts=4)
    push = Pushes(sems, 6)
    normed = normed_input(x(), gain())

    def put(g, at, piece):
        keys_s[g, :, at : at + 128] = piece

    def after(g):
        for yy in range(NY):
            push.start(keys_s.at[g], keys.at[yy * NG + g])

    pieces(dot(normed, w()), put, after)
    push.finish()


def k_queries_values(x, gain, wq, wv, qv0, qv1, qv2, qv3, x_s, g_s, wq_s, wv_s, qv, sems):
    x, gain, wq, wv = fetch((x, gain, wq, wv), (x_s, g_s, wq_s, wv_s), sems)
    normed = normed_input(x(), gain())
    for first, w in ((0, wq), (WIDTH, wv)):

        def put(g, at, piece, first=first):
            qv[g, :, first + at : first + at + 128] = piece

        pieces(dot(normed, w()), put)
    me = my_group()
    for k, out in enumerate((qv0, qv1, qv2, qv3)):
        out[...] = qv[me ^ k]


def rows_out(out, out_s, products, first, second, push):
    done = []
    for a in range(NS):
        while len(done) * I < (a + 1) * ROWS:
            done.append(products(len(done)))
        head = a * ROWS // I
        rows = jnp.concatenate(done[head:], axis=0)
        lo = a * ROWS - head * I
        t = slice(a * SENT, (a + 1) * SENT)
        rows = jnp.concatenate((rows[lo : lo + ROWS], first[t], second[t]), axis=0)
        out_s[a] = rows.astype(BF16)
        push.start(out_s.at[a], out.at[a])


def rows_in(parts):
    got = [parts[a].astype(F32) for a in range(NS)]
    first = jnp.concatenate([t[ROWS : ROWS + SENT] for t in got], axis=0)
    second = jnp.concatenate([t[ROWS + SENT :] for t in got], axis=0)
    return first, second


def k_logits(
    qv0, qv1, qv2, qv3, keys, x, cot, out, queries, values, out_s, q_s, v_s, sems
):
    push = Pushes(sems)
    me = my_group()
    for k, qv in enumerate((qv0, qv1, qv2, qv3)):
        q_s[me ^ k] = qv[:, 0:WIDTH]
        v_s[me ^ k] = qv[:, WIDTH : 2 * WIDTH]
    push.start(q_s, queries)
    push.start(v_s, values)
    perm = to_column()
    first = dot(perm, x[...].astype(F32).reshape(S * R, D).astype(BF16))
    second = dot(perm, cot[...].astype(F32).reshape(S * R, D).astype(BF16))

    def products(h):
        c = slice(h * 256, (h + 1) * 256)
        return dot_nt(q_s[:, :, c].reshape(I, 256), keys[:, c])

    rows_out(out, out_s, products, first, second, push)
    push.finish()


def summed(parts):
    total = parts[0, 0:READ].astype(F32)
    for a in range(1, NS):
        total = total + parts[a, 0:READ].astype(F32)
    return total[:ROWS]


def k_softmax(parts, values, probs, weights, p_s, sems):
    push = Pushes(sems)
    logits = summed(parts) * ROW_SCALE
    e = jnp.exp(logits - jnp.max(logits, axis=-1, keepdims=True))
    p = e * (1.0 / jnp.sum(e, axis=-1, keepdims=True))
    p_s[...] = p
    push.start(p_s, probs)
    w = p.astype(BF16)
    for a in range(NS):
        weights[a] = w
    push.finish()


def k_gather(v0, v1, v2, v3, out, values, sems):
    me = lax.axis_index("y")
    (own,) = fetch((v0,), (values.at[me],), sems, wait_only=True)
    push = Pushes(sems, 1)
    for k, v in enumerate((v1, v2, v3)):
        values[me ^ (k + 1)] = v[...]
    own()
    push.start(values, out)
    push.finish()


def k_attend(weights, values, out):
    perm = to_wide()
    for h in range(GH):
        c = slice(h * 256, (h + 1) * 256)
        v = values[:, :, c].reshape(NY * I, 256)
        att = dot(weights[h * I : (h + 1) * I], v).astype(BF16)
        out[:, c] = dot(perm, att).astype(BF16)


def k_column(
    att_in, sent, gain, out_row, wq, wk, wv, out_col, back, grad_out,
    wv_s, oc_s, att_s, gq_s, gk_s, gv_s, sems,
):
    wv, out_col = fetch((wv, out_col), (wv_s, oc_s), sems, cuts=2)
    raw = att_in[...].astype(F32).reshape(NS, NG, CP, WIDTH)
    groups = [raw[:, g].reshape(NS * CP, WIDTH) for g in range(NG)]
    per_seq = []
    for s in range(S):
        cols = []
        for fb in range(6):
            pair = []
            for n in (2 * fb, 2 * fb + 1):
                pair.append(blk(groups[n // GH], (n % GH) * 2 + s // 2))
            cols.append(halves(pair[0], pair[1], s % 2, s % 2))
        per_seq.append(jnp.concatenate(cols, axis=1).reshape(NS, 1, CP, D))
    att_row = jnp.concatenate(per_seq, axis=1).reshape(TOK, D).astype(BF16)
    pad = to_padded()
    att_row = dot_tn(pad, att_row).astype(BF16)
    xc, cot = rows_in(sent)
    cot = cot.astype(BF16)
    middle = (xc + dot(att_row, out_row[...])).astype(BF16)
    mid = middle.astype(F32)
    hat, r = moments(mid)
    normed = (hat * gain[...].reshape(1, D)).astype(BF16)
    q = dot(normed, wq[...]).astype(BF16) * jnp.asarray(COL_SCALE, BF16)
    k = dot(normed, wk[...]).astype(BF16)
    v = dot(normed, wv()).astype(BF16)
    ga = dot_nt(cot, out_col()).astype(BF16)
    row = lax.broadcasted_iota(jnp.int32, (2 * S * R, 1), 0)
    col = lax.broadcasted_iota(jnp.int32, (1, S * R), 1)
    same = (row % CR) == (col % CR)
    low = lax.broadcasted_iota(jnp.int32, (1, 128), 1) < 64
    masks = [jnp.where(low == first, 1.0, 0.0).astype(BF16) for first in (True, False)]

    def stack(t):
        return jnp.concatenate([t * masks[0], t * masks[1]], axis=0)

    def unstack(t):
        return jnp.where(low, t[: S * R], t[S * R :])

    for fb in range(6):
        at = slice(fb * 128, (fb + 1) * 128)
        kb, vb = blk(k, fb), blk(v, fb)
        qs, gs = stack(blk(q, fb)), stack(blk(ga, fb))
        logits = jnp.where(same, dot_nt(qs, kb), -1e30)
        e = jnp.exp(logits - jnp.max(logits, axis=-1, keepdims=True))
        p = e * (1.0 / jnp.sum(e, axis=-1, keepdims=True))
        w = p.astype(BF16)
        grads = dot_nt(gs, vb)
        dl = (p * (grads - jnp.sum(p * grads, axis=-1, keepdims=True))).astype(BF16)
        att_s[:, at] = unstack(dot(w, vb)).astype(BF16)
        gq_s[:, at] = (unstack(dot(dl, kb)) * COL_SCALE).astype(BF16)
        gk_s[:, at] = dot_tn(dl, qs).astype(BF16)
        gv_s[:, at] = dot_tn(w, gs).astype(BF16)
    back[:, 0:D] = (mid + dot(att_s[...], out_col())).astype(BF16)
    gn = (
        dot_nt(gq_s[...], wq[...]) + dot_nt(gk_s[...], wk[...]) + dot_nt(gv_s[...], wv())
    )
    gmid = (cot.astype(F32) + norm_grad(gn, gain[...].reshape(1, D), hat, r)).astype(BF16)
    back[:, D : 2 * D] = gmid
    gra = dot_nt(gmid, out_row[...]).astype(BF16)
    gra = dot(pad, gra).reshape(NS, S, CP, D)
    seqs = [gra[:, s].reshape(NS * CP, D) for s in range(S)]
    per_group = []
    for g in range(NG):
        cols = []
        for h in range(GH):
            n = g * GH + h
            for sp in range(2):
                cols.append(
                    halves(blk(seqs[2 * sp], n // 2), blk(seqs[2 * sp + 1], n // 2), n % 2, n % 2)
                )
        per_group.append(jnp.concatenate(cols, axis=1).reshape(NS, 1, CP, WIDTH))
    grad_out[...] = jnp.concatenate(per_group, axis=1).reshape(TOK, WIDTH).astype(BF16)


def k_grad_probs(grads, values, back, gra, out, gra_s, out_s, sems):
    push = Pushes(sems)
    perm = to_wide()
    for h in range(GH):
        c = slice(h * 256, (h + 1) * 256)
        gra_s[:, c] = dot_tn(perm, grads[:, c]).astype(BF16)
    push.start(gra_s, gra)
    first, second = back[:, 0:D].astype(F32), back[:, D : 2 * D].astype(F32)

    def products(h):
        c = slice(h * 256, (h + 1) * 256)
        return dot_nt(gra_s[:, c], values[:, :, c].reshape(NY * I, 256))

    rows_out(out, out_s, products, first, second, push)
    push.finish()


def k_grad_values(weights, gra, gv0, gv1, gv2, gv3, gv, sems):
    for h in range(GH):
        c = slice(h * 256, (h + 1) * 256)
        t = dot_tn(weights[h * I : (h + 1) * I], gra[:, c]).astype(BF16)
        gv[:, :, c] = t.reshape(NY, I, 256)
    me = lax.axis_index("y")
    push = Pushes(sems)
    push.start(gv.at[me], gv0)
    for k, out in enumerate((gv1, gv2, gv3)):
        out[...] = gv[me ^ (k + 1)]
    push.finish()


def k_sum_values(gv0, gv1, gv3, gv, g_s, gv_s, sems):
    (gv0,) = fetch((gv0,), (g_s,), sems)
    push = Pushes(sems, 1)
    total = gv1[...].astype(F32) + gv3[...].astype(F32)
    gv_s[...] = total + gv0().astype(F32)
    push.start(gv_s, gv)
    push.finish()


def k_softmax_grad(parts, probs, gv, out, p_s, out_s, sems):
    (probs,) = fetch((probs,), (p_s,), sems)
    push = Pushes(sems, 1)
    grads = summed(parts)
    p = probs()
    dl = p * (grads - jnp.sum(p * grads, axis=-1, keepdims=True)) * ROW_SCALE
    out_s[...] = dl.astype(BF16)
    for a in range(NS):
        push.start(out_s, out.at[a])
    push.finish()


def k_grad_keys(dl, queries, before, gk, q_s, gk_s, sems):
    (queries,) = fetch((queries,), (q_s,), sems)
    push = Pushes(sems, 1)
    queries = queries()
    for h in range(GH):
        c = slice(h * 256, (h + 1) * 256)
        gk_s[:, c] = dot_tn(dl[h * I : (h + 1) * I], queries[:, c]).astype(BF16)
        for r in (slice(0, D // 2), slice(D // 2, D)):
            push.start(gk_s.at[r, c], gk.at[r, c])
    push.finish()


def k_grad_queries(
    dl, keys, gv, gv2, gqv0, gqv1, gqv2, gqv3,
    sum_s, two_s, gv_s, gq_s, o0, o1, o2, o3, sems,
):
    gv, gv2 = fetch((gv, gv2), (sum_s, two_s), sems)
    push = Pushes(sems, 2)
    for h in range(GH):
        c = slice(h * 256, (h + 1) * 256)
        gq_s[:, :, c] = dot(dl[h * I : (h + 1) * I], keys[:, c]).astype(BF16).reshape(NG, R, 256)
    gv_s[...] = (gv() + gv2().astype(F32)).astype(BF16).reshape(NG, R, WIDTH)
    me = my_group()
    for k, (held, out) in enumerate(zip((o0, o1, o2, o3), (gqv0, gqv1, gqv2, gqv3))):
        held[:, 0:WIDTH] = gq_s[me ^ k]
        held[:, WIDTH : 2 * WIDTH] = gv_s[me ^ k]
        push.start(held, out)
    push.finish()


def k_block_out(sent, out):
    first, _ = rows_in(sent)
    out[...] = dot_tn(to_column(), first.astype(BF16)).reshape(S, R, D).astype(BF16)


def token_rows(groups):
    rows = []
    for s in range(S):
        cols = []
        for fb in range(6):
            pair = []
            for n in (2 * fb, 2 * fb + 1):
                pair.append(blk(groups[n // GH], (n % GH) * 2 + s // 2))
            cols.append(halves(pair[0], pair[1], s % 2, s % 2))
        rows.append(jnp.concatenate(cols, axis=1))
    return jnp.concatenate(rows, axis=0).astype(BF16)


def k_finish_keys(gk, wk, out, gk_s, wk_s, out_s, sems):
    gk, wk = fetch((gk, wk), (gk_s, wk_s), sems, cuts=3)
    push = Pushes(sems, 6)
    gk()
    groups = []
    for g in range(NG):
        t = gk_s[g * R : (g + 1) * R].astype(F32)
        for yy in range(1, NY):
            lo = (yy * NG + g) * R
            t = t + gk_s[lo : lo + R].astype(F32)
        groups.append(t)
    out_s[...] = dot_nt(token_rows(groups), wk())
    push.start(out_s, out)
    push.finish()


def k_finish(
    gqv0, gqv1, gqv2, gqv3, part, x, sent, gain, wq, wv, input_grad,
    gqv, own_s, part_s, sems,
):
    gqv0, part = fetch((gqv0, part), (own_s, part_s), sems)
    me = my_group()
    for k, got in enumerate((gqv1, gqv2, gqv3)):
        gqv[me ^ (k + 1)] = got[...]
    perm = to_column()
    _, second = rows_in(sent)
    gmid = dot_tn(perm, second.astype(BF16))
    hat, r = moments(x[...].astype(F32).reshape(S * R, D))
    gqv[me] = gqv0()
    total = None
    for first, w in ((0, wq), (WIDTH, wv)):
        groups = [gqv[g, :, first : first + WIDTH].astype(F32) for g in range(NG)]
        t = dot_nt(token_rows(groups), w[...])
        total = t if total is None else total + t
    total = total + part()
    grad = gmid + norm_grad(total, gain[...].reshape(1, D), hat, r)
    input_grad[...] = grad.reshape(S, R, D).astype(BF16)


def swap(x, axes):
    return lax.all_to_all(x, axes, split_axis=0, concat_axis=0, tiled=True)


def spread(parts, axes):
    n = len(parts)
    pairs = [[(i, i ^ k) for i in range(n)] for k in range(n)]
    return [parts[0]] + [lax.ppermute(parts[k], axes, pairs[k]) for k in range(1, n)]


def local(
    x,
    cot,
    gain_row,
    query_row,
    key_row,
    value_row,
    out_row,
    gain_col,
    query_col,
    key_col,
    value_col,
    out_col,
):
    piece = ((R, 2 * WIDTH), BF16)
    block = ((NS, BLOCK, NY * I), BF16)
    part = ((NG, R, WIDTH), BF16)
    weight = pltpu.VMEM((D, D), BF16)
    row = pltpu.VMEM((S, R, D), BF16)
    gain = pltpu.VMEM((D,), F32)
    keys = call(
        k_keys,
        [pltpu.HBM((NY * NG, R, WIDTH), BF16)],
        x, gain_row, key_row,
        far=(0, 1, 2),
        sems=6 + NY * NG,
        scratch=[row, gain, weight, pltpu.VMEM(*part)],
    )
    qv = call(
        k_queries_values,
        [piece] * NG,
        x, gain_row, query_row, value_row,
        far=(0, 1, 2, 3),
        sems=4,
        scratch=[row, gain, weight, weight, pltpu.VMEM((NG, R, 2 * WIDTH), BF16)],
    )
    qv = spread(qv, GRP)
    keys = swap(keys, ALLRES).reshape(NY * I, WIDTH)
    parts, queries, values = call(
        k_logits,
        [pltpu.HBM(*block), pltpu.HBM(*part), pltpu.HBM(*part)],
        *qv, keys, x, cot,
        sems=2 + NS,
        scratch=[pltpu.VMEM(*block), pltpu.VMEM(*part), pltpu.VMEM(*part)],
    )
    queries = queries.reshape(I, WIDTH)
    parts = swap(parts, SEQ)
    values = spread([values.reshape(I, WIDTH)] * NY, "y")
    gathered = pltpu.VMEM((NY, I, WIDTH), BF16)
    values = call(
        k_gather,
        [pltpu.HBM((NY, I, WIDTH), BF16)],
        *values,
        far=(0,),
        sems=2,
        scratch=[gathered],
    )
    probs, weights = call(
        k_softmax,
        [pltpu.HBM((ROWS, NY * I), F32), ((NS, ROWS, NY * I), BF16)],
        parts, values,
        far=(1,),
        sems=1,
        scratch=[pltpu.VMEM((ROWS, NY * I), F32)],
    )
    weights = swap(weights, SEQ).reshape(GH * I, NY * I)
    att = call(k_attend, [((TOK, WIDTH), BF16)], weights, values)
    att = swap(att, WIDE)
    back, grads = call(
        k_column,
        [((S * R, 2 * D), BF16), ((TOK, WIDTH), BF16)],
        att, parts, gain_col, out_row, query_col, key_col, value_col, out_col,
        mem=32,
        far=(6, 7),
        sems=4,
        scratch=[weight] * 2 + [pltpu.VMEM((S * R, D), BF16)] * 4,
    )
    grads = swap(grads, WIDE)
    gra, gparts = call(
        k_grad_probs,
        [pltpu.HBM((I, WIDTH), BF16), pltpu.HBM(*block)],
        grads, values, back,
        sems=1 + NS,
        scratch=[pltpu.VMEM((I, WIDTH), BF16), pltpu.VMEM(*block)],
    )
    gparts = swap(gparts, SEQ)
    gv = call(
        k_grad_values,
        [pltpu.HBM((I, WIDTH), BF16)] + [((I, WIDTH), BF16)] * (NY - 1),
        weights, gra,
        sems=1,
        scratch=[gathered],
    )
    gv = spread(gv, "y")
    summand = pltpu.VMEM((I, WIDTH), BF16)
    sum_s = pltpu.VMEM((I, WIDTH), F32)
    some = call(
        k_sum_values,
        [pltpu.HBM((I, WIDTH), F32)],
        gv[0], gv[1], gv[3],
        far=(0,),
        sems=2,
        scratch=[summand, sum_s],
    )
    dl = call(
        k_softmax_grad,
        [pltpu.HBM((NS, ROWS, NY * I), BF16)],
        gparts, probs, some,
        far=(1, 2),
        sems=1 + NS,
        scratch=[pltpu.VMEM((ROWS, NY * I), F32), pltpu.VMEM((ROWS, NY * I), BF16)],
    )
    dl = swap(dl, SEQ).reshape(GH * I, NY * I)
    gk = call(
        k_grad_keys,
        [pltpu.HBM((D, D), BF16)],
        dl, queries, gv[2],
        far=(1, 2),
        sems=2 * GH + 1,
        scratch=[summand, weight],
    )
    gqv = call(
        k_grad_queries,
        [pltpu.HBM(*piece)] * NG,
        dl, keys, some, gv[2],
        far=(2, 3),
        sems=2 + NG,
        scratch=[sum_s, summand, pltpu.VMEM(*part), pltpu.VMEM(*part)] + [pltpu.VMEM(*piece)] * NG,
    )
    gqv = spread(gqv, GRP)
    gk = swap(gk, ALLRES).reshape(NY * I, WIDTH)
    block_out = call(k_block_out, [((S, R, D), BF16)], gparts)
    total = pltpu.VMEM((S * R, D), F32)
    from_keys = call(
        k_finish_keys,
        [pltpu.HBM((S * R, D), F32)],
        gk, key_row,
        cost=pl.CostEstimate(flops=4 * 10**9, bytes_accessed=3 * 10**6, transcendentals=0),
        far=(0, 1),
        sems=7,
        scratch=[weight, weight, total],
    )
    input_grad = call(
        k_finish,
        [((S, R, D), BF16)],
        *gqv, from_keys, x, gparts, gain_row, query_row, value_row,
        far=(0, 4),
        sems=2,
        scratch=[
            pltpu.VMEM((NG, R, 2 * WIDTH), BF16),
            pltpu.VMEM(*piece),
            total,
        ],
    )
    return block_out, input_grad


def solution(mesh):
    fine = Mesh(mesh.devices.reshape(2, 4, 2, 4, 2), ("xh", "z", "xl", "y", "c"))
    spec = P(("xh", "z"), ("xl", "y", "c"), None)
    return jax.shard_map(
        local,
        mesh=fine,
        in_specs=(spec, spec) + (P(),) * 10,
        out_specs=(spec, spec),
        check_vma=False,
    )
```
